128 devices in a mesh: group: 4 (over z), band: 32 (over y, x, core).
Axes of the slice: x: 4, y: 4, z: 4, core: 2. Of those that a mesh axis runs over, the one named last changes fastest.
Arguments:
- fine_state: bfloat16 [1536, 2048, 128], P(('group', 'band')), may hold values from -6 to 6
- cotangent: bfloat16 [1536, 2048, 128], P(('group', 'band')), may hold values from -6 to 6
- coarse: bfloat16 [8192, 256], P(('group', 'band')), may hold values from -6 to 6
- conv_weight: bfloat16 [3, 3, 128, 128], replicated, may hold values from -0.1875 to 0.1875
- cond_weight: bfloat16 [256, 128], replicated, may hold values from -0.375 to 0.375
- slot_patch: int32 [128, 128, 16], P(('group', 'band')), may hold values from 0 to 1535
- slot_target: int32 [128, 128, 16], P(('group', 'band')), may hold values from 0 to 15
- slot_weight: float32 [128, 128, 16], P(('group', 'band')), may hold values from 0.1 to 1
- block_count: int32 [128, 128], P(('group', 'band')), may hold values from 0 to 16, as said below
- panel_perm: int32 [4, 2048], replicated, may hold values from 0 to 2047, each once within a row
Outputs:
- grad_fine: bfloat16 [1536, 2048, 128], P(('group', 'band'))
- grad_owned: float32 [8192, 256], P(('group', 'band'))
The draws below stay inside these ranges and needn't reach their ends.
Inputs may be any that keep to these rules, and one draw needn't show every extreme that they name: `panel_perm`: each row is a permutation of the panel's 2048 cells. Only the first block_count slots of a block are live; some block is full, and some owner receives full blocks from every sender.
All inputs are finite; a program needn't handle non-finite values.
Results may differ from the reference program's by a relative error of at most 0.015.
Values may be sent and summed in bfloat16 or wider, within the bound.
No kernel may reach another device: no remote copies, remote signals or barrier semaphores. Data moves between devices by JAX's collectives and lax.ppermute only.
A program may use at most 128 MiB of HBM per device.

```python
import jax
import jax.numpy as jnp
from jax import lax

C = 128
CH = 256
W = 2048
PW = 16
CS = 64
CAP = 16
NGRP = 4
NDEV = 128
NY = 1536
TGT = 16
PANEL = 2048
NCOARSE = 8192
FP = 1536
N_BAND = 32


def draw_block_count(key, part):
    key = jax.random.fold_in(key, 11)
    first, second, third = jax.random.split(key, 3)
    sources = jnp.arange(NDEV, dtype=jnp.int32)
    distance = jnp.abs(2 * sources - (NDEV - 1))
    ceiling = CAP // 2 + CAP // 2 * distance // NDEV
    raw_bits = jax.random.randint(first, (NDEV, NDEV), 0, 1 << 20)
    counts = raw_bits % (ceiling[:, None] + 1)
    full_column = jax.random.randint(second, (), 0, NDEV)
    shuffled = jax.random.permutation(third, NDEV)
    owners = jnp.arange(NDEV, dtype=jnp.int32)
    full_block = (owners[None, :] == full_column) | (owners[None, :] == shuffled[:, None])
    return jnp.where(full_block, CAP, counts).astype(jnp.int32)


def plant(entries, rng, low, top_value):
    longest = entries.shape.index(max(entries.shape))
    spots = []
    for shift in (0, 1):
        where = [jax.random.randint(jax.random.fold_in(rng, axis), (), 0, length) for axis, length in enumerate(entries.shape)]
        where[longest] = (where[longest] + shift) % entries.shape[longest]
        spots.append(tuple(where))
    return entries.at[spots[0]].set(low).at[spots[1]].set(top_value)


def block_scale(key, dims, cuts, low, largest):
    gain = 1.0
    for dim, shards_of in cuts:
        steps = jax.random.uniform(jax.random.fold_in(jax.random.fold_in(key, 6), dim), (shards_of,), jnp.float32, low / len(cuts), largest / len(cuts))
        gain = gain * jnp.repeat(jnp.exp(steps), dims[dim] // shards_of).reshape((-1,) + (1,) * (len(dims) - 1 - dim))
    return gain


def scatter_about(rng, extent, width, reach, cuts=(), kind=jnp.bfloat16):
    values = width * jax.random.normal(rng, extent, jnp.float32)
    if cuts:
        values = values * block_scale(rng, extent, cuts, -0.22, 0.18)
    return jnp.clip(values, -reach, reach).astype(kind)


def setup_inputs(seed: int = 0) -> dict:
    seeds = jax.random.split(jax.random.key(seed), 11)
    return {
        "fine_state": scatter_about(seeds[0], (NY, W, C), 1.0, 6.0, ((0, 128),)),
        "cotangent": scatter_about(seeds[1], (NY, W, C), 1.0, 6.0, ((0, 128),)),
        "coarse": scatter_about(seeds[2], (NCOARSE, CH), 1.0, 6.0, ((0, 128),)),
        "conv_weight": scatter_about(seeds[3], (3, 3, C, C), (9 * C) ** -0.5, 0.1875),
        "cond_weight": scatter_about(seeds[4], (CH, C), CH ** -0.5, 0.375),
        "slot_patch": plant(jax.random.randint(seeds[5], (NDEV, NDEV, CAP), 0, FP), jax.random.fold_in(seeds[5], 1), 0, FP - 1).astype(jnp.int32),
        "slot_target": plant(jax.random.randint(seeds[6], (NDEV, NDEV, CAP), 0, TGT), jax.random.fold_in(seeds[6], 1), 0, TGT - 1).astype(jnp.int32),
        "slot_weight": jnp.clip(0.1 + 0.9 * jax.random.uniform(seeds[7], (NDEV, NDEV, CAP), jnp.float32) ** block_scale(seeds[7], (NDEV, NDEV, CAP), ((0, 128),), -0.2, 0.2), 0.1, 1.0),
        "block_count": draw_block_count(jax.random.fold_in(seeds[10], 71), 0),
        "panel_perm": jax.vmap(lambda own: jax.random.permutation(own, PANEL))(jax.random.split(seeds[9], NGRP)).reshape((NGRP, PANEL)).astype(jnp.int32),
    }


def conv_same(field, kernel):
    return lax.conv_general_dilated(field[None], kernel, (1, 1), ((1, 1), (1, 1)), dimension_numbers=("NHWC", "HWIO", "NHWC"), preferred_element_type=jnp.float32)[0]


def reference(fine_state, cotangent, coarse, conv_weight, cond_weight, slot_patch, slot_target, slot_weight, block_count, panel_perm):
    sources = jnp.arange(NDEV, dtype=jnp.int32)
    src_group = sources // N_BAND
    live_mask = jnp.arange(CAP, dtype=jnp.int32)[None, None, :] < block_count[:, :, None]
    weight = jnp.where(live_mask, slot_weight, jnp.float32(0.0)).reshape(-1)
    slot_index = (sources[None, :, None] * TGT + slot_target).reshape(NDEV, NDEV * CAP)
    panel_index = jnp.take_along_axis(panel_perm[src_group], slot_index, axis=1)
    coarse_row = (src_group[:, None] * PANEL + panel_index).reshape(-1)
    patch_global = (sources[:, None] * FP + slot_patch.reshape(NDEV, NDEV * CAP)).reshape(-1)
    picked = coarse[coarse_row].astype(jnp.float32) * weight[:, None]
    condition = jax.ops.segment_sum(picked, patch_global, num_segments=NDEV * FP).astype(jnp.bfloat16)
    cond_proj = jnp.dot(condition, cond_weight, preferred_element_type=jnp.float32)
    cond_proj = jnp.broadcast_to(cond_proj.reshape(NY, W // PW, 1, C), (NY, W // PW, PW, C)).reshape(NY, W, C)
    hidden = (fine_state.astype(jnp.float32) + cond_proj).astype(jnp.bfloat16)
    preact = conv_same(hidden, conv_weight)
    sigmoid = jax.nn.sigmoid(preact)
    grad_pre = (cotangent.astype(jnp.float32) * sigmoid * (1.0 + preact * (1.0 - sigmoid))).astype(jnp.bfloat16)
    flipped = jnp.transpose(conv_weight[::-1, ::-1], (0, 1, 3, 2))
    grad_in = conv_same(grad_pre, flipped)
    grad_fine = (cotangent.astype(jnp.float32) + grad_in).astype(jnp.bfloat16)
    grad_patch = grad_in.reshape(NY, W // PW, PW, C).sum(axis=2).reshape(NDEV * FP, C).astype(jnp.bfloat16)
    grad_cond = jnp.dot(grad_patch, cond_weight.T, preferred_element_type=jnp.float32)
    contribution = grad_cond[patch_global] * weight[:, None]
    owner = jnp.broadcast_to(sources[None, :, None], (NDEV, NDEV, CAP))
    owned_row = (owner * CS + src_group[:, None, None] * TGT + slot_target).reshape(-1)
    grad_owned = jax.ops.segment_sum(contribution, owned_row, num_segments=NCOARSE)
    return grad_fine, grad_owned
```

```python
import functools

import jax
import jax.numpy as jnp
from jax import lax
from jax.experimental import pallas as pl
from jax.experimental.pallas import tpu as pltpu
from jax.sharding import PartitionSpec as P

PW = 16
ROWS = 12
LON = 2048
PC = LON // PW
CH = 128
PAIRS = ROWS // 2
SLOTS = 2048
BF = jnp.bfloat16
F32 = jnp.float32
MB = 1 << 20
BOTH = ("group", "band")


def dot(a, b):
    return jnp.dot(a, b, preferred_element_type=F32)


def pack_rows(kernel):
    zero = jnp.zeros(kernel.shape[2:], kernel.dtype)
    packed = []
    for kx in range(3):
        rows = [
            jnp.concatenate(
                [kernel[r, kx] if r < 3 else zero, kernel[r - 1, kx] if r >= 1 else zero], axis=1
            )
            for r in range(4)
        ]
        packed.append(jnp.concatenate(rows, axis=0))
    return jnp.stack(packed)


def conv_pair(rows, w_ref, write):
    lhs = jnp.concatenate(rows, axis=1)
    left = dot(lhs, w_ref[0])
    right = dot(lhs, w_ref[2])
    place = lax.broadcasted_iota(jnp.int32, (LON, 1), 0)
    total = dot(lhs, w_ref[1])
    total += jnp.where(place == 0, 0.0, pltpu.roll(left, 1, 0))
    total += jnp.where(place == LON - 1, 0.0, pltpu.roll(right, LON - 1, 0))
    write(0, total[:, :CH])
    write(1, total[:, CH:])


def conv_rows(up, mid, down, halo_up, halo_down):
    i = pl.program_id(0)
    first = jnp.where(i == 0, halo_up[0], up[0])
    last = jnp.where(i == PAIRS - 1, halo_down[0], down[0])
    return [first, mid[0], mid[1], last]


def conv_state_kernel(up, mid, down, halo_up, halo_down, w_ref, out):
    def write(r, value):
        out[r] = value

    conv_pair(conv_rows(up, mid, down, halo_up, halo_down), w_ref, write)


def conv_grad_kernel(up, mid, down, halo_up, halo_down, w_ref, cot, out):
    def write(r, value):
        out[r] = (cot[r].astype(F32) + value).astype(BF)

    conv_pair(conv_rows(up, mid, down, halo_up, halo_down), w_ref, write)


ROW_UP = pl.BlockSpec((1, LON, CH), lambda i: (jnp.maximum(2 * i - 1, 0), 0, 0))
ROW_PAIR = pl.BlockSpec((2, LON, CH), lambda i: (i, 0, 0))
ROW_DOWN = pl.BlockSpec((1, LON, CH), lambda i: (jnp.minimum(2 * i + 2, ROWS - 1), 0, 0))
ROW_HALO = pl.BlockSpec((1, LON, CH), lambda i: (0, 0, 0))
PACKED = pl.BlockSpec((3, 4 * CH, 2 * CH), lambda i: (0, 0, 0))


def conv_cost(out_bytes):
    return pl.CostEstimate(
        flops=2 * ROWS * LON * 9 * CH * CH, bytes_accessed=ROWS * LON * CH * (4 + out_bytes), transcendentals=0
    )


def conv_state(field, halo_up, halo_down, packed):
    return pl.pallas_call(
        conv_state_kernel,
        grid=(PAIRS,),
        in_specs=[ROW_UP, ROW_PAIR, ROW_DOWN, ROW_HALO, ROW_HALO, PACKED],
        out_specs=ROW_PAIR,
        out_shape=jax.ShapeDtypeStruct((ROWS, LON, CH), F32),
        compiler_params=pltpu.CompilerParams(vmem_limit_bytes=50 * MB),
        cost_estimate=conv_cost(4),
        name="conv_state",
    )(field, field, field, halo_up, halo_down, packed)


def conv_grad(field, halo_up, halo_down, packed, cotangent):
    return pl.pallas_call(
        conv_grad_kernel,
        grid=(PAIRS,),
        in_specs=[ROW_UP, ROW_PAIR, ROW_DOWN, ROW_HALO, ROW_HALO, PACKED, ROW_PAIR],
        out_specs=ROW_PAIR,
        out_shape=jax.ShapeDtypeStruct((ROWS, LON, CH), BF),
        compiler_params=pltpu.CompilerParams(vmem_limit_bytes=50 * MB),
        cost_estimate=conv_cost(4),
        name="conv_grad",
    )(field, field, field, halo_up, halo_down, packed, cotangent)


SC_CHUNK = 512


def onehot(height, index_row):
    place = lax.broadcasted_iota(jnp.int32, (height, index_row.shape[1]), 0)
    return jnp.where(place == index_row, 1.0, 0.0).astype(BF)


def contract0(a, b):
    return lax.dot_general(a, b, (((0,), (0,)), ((), ())), preferred_element_type=F32)


def contract1(a, b):
    return lax.dot_general(a, b, (((1,), (1,)), ((), ())), preferred_element_type=F32)


def spread_kernel(panel, source, patch, weight, out):
    patches = ROWS * PC
    total = jnp.zeros((patches, CH), F32)
    for lo in range(0, SLOTS, SC_CHUNK):
        cut = slice(lo, lo + SC_CHUNK)
        picked = contract0(panel[...], onehot(SLOTS, source[:, cut]))
        picked = (picked * weight[:, cut]).astype(BF)
        total += contract1(onehot(patches, patch[:, cut]), picked)
    out[...] = total.astype(BF)


def spread(panel, source, patch, weight):
    return pl.pallas_call(
        spread_kernel,
        out_shape=jax.ShapeDtypeStruct((ROWS * PC, CH), BF),
        compiler_params=pltpu.CompilerParams(vmem_limit_bytes=50 * MB),
        cost_estimate=pl.CostEstimate(flops=4 * 2048 * 2048 * 128, bytes_accessed=MB, transcendentals=0),
        name="spread",
    )(panel, source, patch, weight)


EX_CELLS = 1024
RD_CELLS = 256


def expand_matrix():
    cells = jnp.arange(EX_CELLS)[:, None]
    patch = jnp.arange(EX_CELLS // PW)[None, :]
    inside = cells // PW == patch
    return jnp.concatenate(
        [inside, inside & (cells % PW == 0), inside & (cells % PW == PW - 1)], axis=1
    ).astype(BF)


def shift_patch(value, step):
    place = lax.broadcasted_iota(jnp.int32, (PC, 1), 0)
    if step > 0:
        return jnp.where(place == 0, 0.0, pltpu.roll(value, 1, 0))
    return jnp.where(place == PC - 1, 0.0, pltpu.roll(value, PC - 1, 0))


def silu_kernel(pre, cot, c_up, c_mid, c_down, h_up, h_down, w_ref, ex_ref, rd_ref, out, sums):
    i = pl.program_id(0)
    first = jnp.where(i == 0, h_up[...], c_up[0])
    last = jnp.where(i == PAIRS - 1, h_down[...], c_down[0])
    lhs = jnp.concatenate([first, c_mid[0], c_mid[1], last], axis=1)
    west, here, east = [dot(lhs, w_ref[k]) for k in range(3)]
    inner = (west + here + east).astype(BF)
    at_first = (shift_patch(west, 1) - west).astype(BF)
    at_last = (shift_patch(east, -1) - east).astype(BF)
    per = EX_CELLS // PW
    part_sum, part_first, part_last = [], [], []
    for lo in range(0, LON, EX_CELLS):
        cut = slice(lo // PW, lo // PW + per)
        terms = jnp.concatenate([inner[cut], at_first[cut], at_last[cut]], axis=0)
        spread_terms = dot(ex_ref[...], terms)
        grads = []
        for r in range(2):
            x = pre[r, lo : lo + EX_CELLS] + spread_terms[:, r * CH : (r + 1) * CH]
            s = 0.5 * jnp.tanh(0.5 * x) + 0.5
            g = (cot[r, lo : lo + EX_CELLS].astype(F32) * s * (1.0 + x * (1.0 - s))).astype(BF)
            out[r, lo : lo + EX_CELLS] = g
            grads.append(g)
        grads = jnp.concatenate(grads, axis=1)
        for at in range(0, EX_CELLS, RD_CELLS):
            reduced = dot(rd_ref[...], grads[at : at + RD_CELLS])
            part_sum.append(reduced[:PW])
            part_first.append(reduced[PW : 2 * PW])
            part_last.append(reduced[2 * PW :])
    whole, firsts, lasts = [jnp.concatenate(p, axis=0) for p in (part_sum, part_first, part_last)]
    from_west = (whole - lasts + shift_patch(lasts, 1)).astype(BF)
    from_east = (whole - firsts + shift_patch(firsts, -1)).astype(BF)
    whole = whole.astype(BF)
    for r in range(2):
        cut = slice(r * CH, (r + 1) * CH)
        sums[r] = jnp.concatenate([from_west[:, cut], whole[:, cut], from_east[:, cut]], axis=1)


def silu_grad(pre, cotangent, cond, cond_up, cond_down, packed):
    expand = expand_matrix()
    reduce_m = expand_matrix_small()
    cond = cond.reshape(ROWS, PC, CH)
    return pl.pallas_call(
        silu_kernel,
        grid=(PAIRS,),
        in_specs=[
            ROW_PAIR,
            ROW_PAIR,
            pl.BlockSpec((1, PC, CH), lambda i: (jnp.maximum(2 * i - 1, 0), 0, 0)),
            pl.BlockSpec((2, PC, CH), lambda i: (i, 0, 0)),
            pl.BlockSpec((1, PC, CH), lambda i: (jnp.minimum(2 * i + 2, ROWS - 1), 0, 0)),
            pl.BlockSpec((PC, CH), lambda i: (0, 0)),
            pl.BlockSpec((PC, CH), lambda i: (0, 0)),
            PACKED,
            pl.BlockSpec(expand.shape, lambda i: (0, 0)),
            pl.BlockSpec(reduce_m.shape, lambda i: (0, 0)),
        ],
        out_specs=[ROW_PAIR, pl.BlockSpec((2, PC, 3 * CH), lambda i: (i, 0, 0))],
        out_shape=[
            jax.ShapeDtypeStruct((ROWS, LON, CH), BF),
            jax.ShapeDtypeStruct((ROWS, PC, 3 * CH), BF),
        ],
        compiler_params=pltpu.CompilerParams(vmem_limit_bytes=50 * MB),
        cost_estimate=pl.CostEstimate(flops=10**9, bytes_accessed=8 * ROWS * LON * CH, transcendentals=0),
        name="silu_grad",
    )(pre, cotangent, cond, cond, cond, cond_up, cond_down, packed, expand, reduce_m)


def expand_matrix_small():
    cells = jnp.arange(RD_CELLS)[None, :]
    patch = jnp.arange(RD_CELLS // PW)[:, None]
    inside = cells // PW == patch
    return jnp.concatenate(
        [inside, inside & (cells % PW == 0), inside & (cells % PW == PW - 1)], axis=0
    ).astype(BF)


def collect_kernel(sums, s_up, s_down, w_ref, patch, target, weight, out):
    patches = ROWS * PC
    ext = jnp.concatenate([s_up[...], sums[...], s_down[...]], axis=0)
    grad_patch = dot(ext[:patches], w_ref[0])
    grad_patch += dot(ext[PC : PC + patches], w_ref[1])
    grad_patch += dot(ext[2 * PC :], w_ref[2])
    grad_patch = grad_patch.astype(BF)
    block = 256
    row = lax.broadcasted_iota(jnp.int32, (block, block), 0)
    own = lax.broadcasted_iota(jnp.int32, (block, block), 1) // 16 * 16
    for lo in range(0, SLOTS, SC_CHUNK):
        cut = slice(lo, lo + SC_CHUNK)
        picked = contract0(grad_patch, onehot(patches, patch[:, cut]))
        picked = (picked * weight[:, cut]).astype(BF)
        for at in range(0, SC_CHUNK, block):
            place = own + target[:, lo + at : lo + at + block]
            hit = jnp.where(row == place, 1.0, 0.0).astype(BF)
            out[lo + at : lo + at + block, :] = contract1(hit, picked[:, at : at + block]).astype(BF)


def collect(sums, s_up, s_down, w, patch, target, weight):
    return pl.pallas_call(
        collect_kernel,
        out_shape=jax.ShapeDtypeStruct((SLOTS, CH), BF),
        compiler_params=pltpu.CompilerParams(vmem_limit_bytes=50 * MB),
        cost_estimate=pl.CostEstimate(flops=2 * 2048 * 2048 * 128, bytes_accessed=2 * MB, transcendentals=0),
        name="collect",
    )(sums.reshape(ROWS * PC, 3 * CH), s_up, s_down, w, patch, target, weight)


def from_neighbours(head, tail):
    count = lax.axis_size(BOTH)
    up = lax.ppermute(tail, BOTH, [(i, i + 1) for i in range(count - 1)])
    down = lax.ppermute(head, BOTH, [(i + 1, i) for i in range(count - 1)])
    return up, down


def body(
    fine_state,
    cotangent,
    coarse,
    conv_weight,
    cond_weight,
    slot_patch,
    slot_target,
    slot_weight,
    block_count,
    panel_perm,
):
    group = lax.axis_index("group")
    packed = pack_rows(conv_weight)
    flipped = jnp.transpose(conv_weight[::-1, ::-1], (0, 1, 3, 2))
    packed_back = pack_rows(flipped)
    w_back = flipped.reshape(3, 3 * CH, CH)

    panel = lax.all_gather(dot(coarse, cond_weight).astype(BF), "band", axis=0, tiled=True)
    fine_up, fine_down = from_neighbours(fine_state[:1], fine_state[-1:])

    target = slot_target[0]
    perm_row = lax.dynamic_index_in_dim(panel_perm, group, 0, keepdims=False).reshape(-1, 1, 16)
    steps = jnp.arange(16, dtype=jnp.int32)
    source = jnp.sum(jnp.where(target[:, :, None] == steps, perm_row, 0), axis=2).reshape(1, SLOTS)
    live = steps[None, :] < block_count[0][:, None]
    weight = jnp.where(live, slot_weight[0], 0.0).reshape(1, SLOTS)
    patch = slot_patch.reshape(1, SLOTS)
    target_row = slot_target.reshape(1, SLOTS)

    pre = conv_state(fine_state, fine_up, fine_down, packed)
    cond = spread(panel, source, patch, weight)
    cond_up, cond_down = from_neighbours(cond[:PC], cond[-PC:])
    grad_pre, sums = silu_grad(pre, cotangent, cond, cond_up, cond_down, packed)
    sums_up, sums_down = from_neighbours(sums[0], sums[-1])
    grad_up, grad_down = from_neighbours(grad_pre[:1], grad_pre[-1:])
    owned = collect(sums, sums_up, sums_down, w_back, patch, target_row, weight)
    received = lax.all_to_all(owned.reshape(-1, 16, CH), BOTH, 0, 0, tiled=True)
    grad_fine = conv_grad(grad_pre, grad_up, grad_down, packed_back, cotangent)
    groups = lax.axis_size("group")
    received = received.reshape(groups, -1, 16, CH).astype(F32).sum(axis=1).reshape(groups * 16, CH)
    grad_owned = lax.dot_general(
        received.astype(BF), cond_weight, (((1,), (1,)), ((), ())), preferred_element_type=F32
    )
    return grad_fine, grad_owned


def solution(mesh):
    rows3 = P(BOTH, None, None)
    rows2 = P(BOTH, None)
    return jax.shard_map(
        body,
        mesh=mesh,
        in_specs=(rows3, rows3, rows2, P(), P(), rows3, rows3, rows3, rows2, P()),
        out_specs=(rows3, rows2),
        check_vma=False,
    )
```

```python
import functools

import jax
import jax.numpy as jnp
import numpy as np
from jax import lax
from jax.experimental import pallas as pl
from jax.experimental.pallas import tpu as pltpu
from jax.sharding import PartitionSpec as P

PW = 16
ROWS = 12
LON = 2048
PC = LON // PW
CH = 128
PAIRS = ROWS // 2
EXT = ROWS + 2
SLOTS = 2048
BF = jnp.bfloat16
F32 = jnp.float32
MB = 1 << 20
BOTH = ("group", "band")


def dot(a, b):
    return jnp.dot(a, b, preferred_element_type=F32)


def pack_rows(kernel):
    zero = jnp.zeros(kernel.shape[2:], kernel.dtype)
    packed = []
    for kx in range(3):
        rows = [
            jnp.concatenate(
                [kernel[r, kx] if r < 3 else zero, kernel[r - 1, kx] if r >= 1 else zero], axis=1
            )
            for r in range(4)
        ]
        packed.append(jnp.concatenate(rows, axis=0))
    return jnp.stack(packed)


WHOLE = pl.BlockSpec(memory_space=pltpu.VMEM)


def params(mib):
    return pltpu.CompilerParams(vmem_limit_bytes=mib * MB)


def conv_pair(rows, w_ref, write):
    lhs = jnp.concatenate(rows, axis=1)
    left = dot(lhs, w_ref[0])
    right = dot(lhs, w_ref[2])
    place = lax.broadcasted_iota(jnp.int32, (LON, 1), 0)
    total = dot(lhs, w_ref[1])
    total += jnp.where(place == 0, 0.0, pltpu.roll(left, 1, 0))
    total += jnp.where(place == LON - 1, 0.0, pltpu.roll(right, LON - 1, 0))
    write(0, total[:, :CH])
    write(1, total[:, CH:])


def conv_state_inner_kernel(start, *refs):
    field, w_ref, out = refs[0], refs[1], refs[-1]
    q = start + pl.program_id(0)

    def write(r, value):
        out[2 * q + r] = value

    conv_pair([field[2 * q - 2 + r] for r in range(4)], w_ref, write)


def conv_state_rim_kernel(field, w_ref, up, down, before, out):
    q = pl.program_id(0) * PAIRS
    above = jnp.maximum(2 * q - 2, 0)
    below = jnp.minimum(2 * q, ROWS - 2)
    rows = [jnp.where(q == 0, up[r], field[above + r]) for r in range(2)]
    rows += [jnp.where(q == PAIRS, down[r], field[below + r]) for r in range(2)]

    def write(r, value):
        out[2 * q + r] = value

    conv_pair(rows, w_ref, write)


def conv_cost(pairs):
    return pl.CostEstimate(
        flops=4 * pairs * LON * 12 * CH * CH, bytes_accessed=pairs * LON * CH * 12, transcendentals=0
    )


PRE = pltpu.VMEM((EXT, LON, CH), F32)


def conv_state_inner(field, packed, start, count, before=None):
    args = (field, packed) if before is None else (field, packed, before)
    return pl.pallas_call(
        functools.partial(conv_state_inner_kernel, start),
        grid=(count,),
        in_specs=[WHOLE] * len(args),
        out_specs=WHOLE,
        out_shape=PRE,
        input_output_aliases={} if before is None else {2: 0},
        compiler_params=params(12),
        cost_estimate=conv_cost(count),
        name="conv_state",
    )(*args)


def conv_state_rim(field, packed, up, down, before):
    return pl.pallas_call(
        conv_state_rim_kernel,
        grid=(2,),
        in_specs=[WHOLE] * 5,
        out_specs=WHOLE,
        out_shape=PRE,
        input_output_aliases={4: 0},
        compiler_params=params(12),
        cost_estimate=conv_cost(2),
        name="conv_state_rim",
    )(field, packed, up, down, before)


def conv_grad_kernel(start, *refs):
    field, w_ref, cot, out = refs[0], refs[1], refs[2], refs[-1]
    p = start + pl.program_id(0)

    def write(r, value):
        out[r] = (cot[2 * p + r].astype(F32) + value).astype(BF)

    conv_pair([field[2 * p + r] for r in range(4)], w_ref, write)


def conv_grad(field, packed, cotangent, start, count, before=None):
    args = [field, packed, cotangent] + ([] if before is None else [before])
    specs = [WHOLE] * 3 + ([] if before is None else [pl.BlockSpec(memory_space=pl.ANY)])
    return pl.pallas_call(
        functools.partial(conv_grad_kernel, start),
        grid=(count,),
        in_specs=specs,
        out_specs=pl.BlockSpec((2, LON, CH), lambda i: (start + i, 0, 0)),
        out_shape=jax.ShapeDtypeStruct((ROWS, LON, CH), BF),
        input_output_aliases={} if before is None else {3: 0},
        compiler_params=params(16),
        cost_estimate=conv_cost(count),
        name="conv_grad",
    )(*args)


SC_CHUNK = 512


def onehot(height, index_row):
    place = lax.broadcasted_iota(jnp.int32, (height, index_row.shape[1]), 0)
    return jnp.where(place == index_row, 1.0, 0.0).astype(BF)


def contract0(a, b):
    return lax.dot_general(a, b, (((0,), (0,)), ((), ())), preferred_element_type=F32)


def contract1(a, b):
    return lax.dot_general(a, b, (((1,), (1,)), ((), ())), preferred_element_type=F32)


def spread_kernel(near, far, source, patch, weight, out):
    patches = ROWS * PC
    panel = jnp.concatenate([near[...], far[...]], axis=0)
    total = jnp.zeros((patches, CH), F32)
    for lo in range(0, SLOTS, SC_CHUNK):
        cut = slice(lo, lo + SC_CHUNK)
        picked = contract0(panel, onehot(SLOTS, source[:, cut]))
        picked = (picked * weight[:, cut]).astype(BF)
        total += contract1(onehot(patches, patch[:, cut]), picked)
    out[...] = total.astype(BF)


def spread(near, far, source, patch, weight):
    return pl.pallas_call(
        spread_kernel,
        in_specs=[WHOLE] * 5,
        out_specs=WHOLE,
        out_shape=jax.ShapeDtypeStruct((ROWS * PC, CH), BF),
        compiler_params=params(16),
        cost_estimate=pl.CostEstimate(flops=4 * 2048 * 2048 * 128, bytes_accessed=MB, transcendentals=0),
        name="spread",
    )(near, far, source, patch, weight)


EX_CELLS = 1024
RD_CELLS = 256


def patch_marks(count):
    cells = np.arange(count)[:, None]
    inside = cells // PW == np.arange(count // PW)[None, :]
    marks = [inside, inside & (cells % PW == 0), inside & (cells % PW == PW - 1)]
    return np.concatenate(marks, axis=1).astype(np.float32)


def shift_patch(value, step):
    place = lax.broadcasted_iota(jnp.int32, (PC, 1), 0)
    if step > 0:
        return jnp.where(place == 0, 0.0, pltpu.roll(value, 1, 0))
    return jnp.where(place == PC - 1, 0.0, pltpu.roll(value, PC - 1, 0))


def silu_kernel(pre, cot, up, down, cond, c_up, c_down, w_ref, ex_ref, rd_ref, out, sums):
    q = pl.program_id(0)
    above = jnp.where(q == 0, c_up[...], cond[jnp.maximum(q - 1, 0)])
    below = jnp.where(q == PAIRS, c_down[...], cond[jnp.minimum(q, PAIRS - 1)])
    lhs = jnp.concatenate([above[:PC], above[PC:], below[:PC], below[PC:]], axis=1)
    west, here, east = [dot(lhs, w_ref[k]) for k in range(3)]
    inner = (west + here + east).astype(BF)
    at_first = (shift_patch(west, 1) - west).astype(BF)
    at_last = (shift_patch(east, -1) - east).astype(BF)
    per = EX_CELLS // PW
    part_sum, part_first, part_last = [], [], []
    for lo in range(0, LON, EX_CELLS):
        cells = slice(lo, lo + EX_CELLS)
        cut = slice(lo // PW, lo // PW + per)
        terms = jnp.concatenate([inner[cut], at_first[cut], at_last[cut]], axis=0)
        spread_terms = dot(ex_ref[...], terms)
        weights = [
            jnp.where(q == 0, up[2, cells], cot[jnp.maximum(2 * q - 1, 0), cells]),
            jnp.where(q == PAIRS, down[2, cells], cot[jnp.minimum(2 * q, ROWS - 1), cells]),
        ]
        grads = []
        for r in range(2):
            half = 0.5 * (pre[2 * q + r, cells] + spread_terms[:, r * CH : (r + 1) * CH])
            t = jnp.tanh(half)
            slope = (0.5 + 0.5 * t) * (1.0 + half * (1.0 - t))
            g = (weights[r].astype(F32) * slope).astype(BF)
            out[2 * q + r, cells] = g
            grads.append(g)
        grads = jnp.concatenate(grads, axis=1)
        for at in range(0, EX_CELLS, RD_CELLS):
            reduced = dot(rd_ref[...], grads[at : at + RD_CELLS])
            part_sum.append(reduced[:PW])
            part_first.append(reduced[PW : 2 * PW])
            part_last.append(reduced[2 * PW :])
    whole, firsts, lasts = [jnp.concatenate(p, axis=0) for p in (part_sum, part_first, part_last)]
    from_west = (whole - lasts + shift_patch(lasts, 1)).astype(BF)
    from_east = (whole - firsts + shift_patch(firsts, -1)).astype(BF)
    whole = whole.astype(BF)
    for r in range(2):
        cut = slice(r * CH, (r + 1) * CH)
        sums[2 * q + r] = jnp.concatenate([from_west[:, cut], whole[:, cut], from_east[:, cut]], axis=1)


def silu_grad(pre, cotangent, up, down, cond, c_up, c_down, packed):
    expand = jnp.asarray(patch_marks(EX_CELLS), BF)
    reduce_m = jnp.asarray(patch_marks(RD_CELLS).T, BF)
    cond = cond.reshape(PAIRS, 2 * PC, CH)
    return pl.pallas_call(
        silu_kernel,
        grid=(PAIRS + 1,),
        in_specs=[WHOLE] * 10,
        out_specs=[WHOLE, WHOLE],
        out_shape=[pltpu.VMEM((EXT, LON, CH), BF), pltpu.VMEM((EXT, PC, 3 * CH), BF)],
        compiler_params=params(12),
        cost_estimate=pl.CostEstimate(flops=10**9, bytes_accessed=8 * ROWS * LON * CH, transcendentals=0),
        name="silu_grad",
    )(pre, cotangent, up, down, cond, c_up, c_down, packed, expand, reduce_m)


def collect_kernel(here, sums, w_ref, patch, target, weight, keep, send, total):
    patches = ROWS * PC
    grad_patch = dot(sums[:patches], w_ref[0])
    grad_patch += dot(sums[PC : PC + patches], w_ref[1])
    grad_patch += dot(sums[2 * PC :], w_ref[2])
    grad_patch = grad_patch.astype(BF)
    block = 256
    row = lax.broadcasted_iota(jnp.int32, (block, block), 0)
    own = lax.broadcasted_iota(jnp.int32, (block, block), 1) // 16 * 16
    group, band = here[0], here[1]
    for lo in range(0, SLOTS, SC_CHUNK):
        cut = slice(lo, lo + SC_CHUNK)
        picked = contract0(grad_patch, onehot(patches, patch[:, cut]))
        picked = (picked * weight[:, cut]).astype(BF)
        for at in range(0, SC_CHUNK, block):
            place = own + target[:, lo + at : lo + at + block]
            hit = jnp.where(row == place, 1.0, 0.0).astype(BF)
            rows = contract1(hit, picked[:, at : at + block])
            for j in range(0, block, 16):
                owner = (lo + at + j) // 16
                to = ((owner % 32) ^ band) * 64 + ((owner // 32) ^ group) * 16
                total[pl.ds(pl.multiple_of(to, 16), 16), :] = rows[j : j + 16]
    keep[...] = total[: SLOTS // 2]
    send[...] = total[SLOTS // 2 :].astype(BF)


def collect(here, sums, w, patch, target, weight):
    return pl.pallas_call(
        collect_kernel,
        in_specs=[pl.BlockSpec(memory_space=pltpu.SMEM)] + [WHOLE] * 5,
        out_specs=[WHOLE, WHOLE],
        out_shape=[
            jax.ShapeDtypeStruct((SLOTS // 2, CH), F32),
            jax.ShapeDtypeStruct((SLOTS // 2, CH), BF),
        ],
        scratch_shapes=[pltpu.VMEM((SLOTS, CH), F32)],
        compiler_params=params(16),
        cost_estimate=pl.CostEstimate(flops=2 * 2048 * 2048 * 128, bytes_accessed=2 * MB, transcendentals=0),
        name="collect",
    )(here, sums.reshape(EXT * PC, 3 * CH), w, patch, target, weight)


def halve_kernel(kept, got, keep, send):
    half = keep.shape[0]
    total = kept[...] + got[...].astype(F32)
    keep[...] = total[:half]
    send[...] = total[half:].astype(BF)


def halve(kept, got):
    half = kept.shape[0] // 2
    return pl.pallas_call(
        halve_kernel,
        in_specs=[WHOLE] * 2,
        out_specs=[WHOLE, WHOLE],
        out_shape=[jax.ShapeDtypeStruct((half, CH), F32), jax.ShapeDtypeStruct((half, CH), BF)],
        compiler_params=params(4),
        name="halve",
    )(kept, got)


def settle_kernel(kept, got, even, odd):
    total = (kept[...] + got[...].astype(F32)).astype(BF)
    even[:16] = total[:16]
    even[16:] = total[32:48]
    odd[:16] = total[16:32]
    odd[16:] = total[48:]


def settle(kept, got):
    half = jax.ShapeDtypeStruct((32, CH), BF)
    return pl.pallas_call(
        settle_kernel,
        in_specs=[WHOLE] * 2,
        out_specs=[WHOLE, WHOLE],
        out_shape=[half, half],
        compiler_params=params(4),
        name="settle",
    )(kept, got)


def finish_kernel(here, even, got, last, w_ref, out):
    rows = jnp.concatenate([even[:16], got[:16], last[...]], axis=0)
    value = contract1(rows, w_ref[...])
    for k in range(4):
        to = pl.multiple_of((here[0] ^ k) * 16, 16)
        out[pl.ds(to, 16), :] = value[16 * k : 16 * k + 16]


def finish(here, even, got, last, cond_weight):
    return pl.pallas_call(
        finish_kernel,
        in_specs=[pl.BlockSpec(memory_space=pltpu.SMEM)] + [WHOLE] * 4,
        out_specs=WHOLE,
        out_shape=jax.ShapeDtypeStruct((64, cond_weight.shape[0]), F32),
        compiler_params=params(4),
        name="finish",
    )(here, even, got, last, cond_weight)


def from_neighbours(head, tail):
    count = lax.axis_size(BOTH)
    up = lax.ppermute(tail, BOTH, [(i, i + 1) for i in range(count - 1)])
    down = lax.ppermute(head, BOTH, [(i + 1, i) for i in range(count - 1)])
    return up, down


def swap(value, axis, bit):
    return lax.ppermute(value, axis, [(i, i ^ bit) for i in range(lax.axis_size(axis))])


def after(value, *earlier):
    return lax.optimization_barrier((value,) + earlier)[0]


def body(
    fine_state,
    cotangent,
    coarse,
    conv_weight,
    cond_weight,
    slot_patch,
    slot_target,
    slot_weight,
    block_count,
    panel_perm,
):
    group = lax.axis_index("group")
    band = lax.axis_index("band")
    here = jnp.stack([group, band]).astype(jnp.int32)
    packed = pack_rows(conv_weight)
    flipped = jnp.transpose(conv_weight[::-1, ::-1], (0, 1, 3, 2))
    packed_back = pack_rows(flipped)
    w_back = flipped.reshape(3, 3 * CH, CH)

    target = slot_target[0]
    perm_row = lax.dynamic_index_in_dim(panel_perm, group, 0, keepdims=False).reshape(-1, 1, 16)
    steps = jnp.arange(16, dtype=jnp.int32)
    source = jnp.sum(jnp.where(target[:, :, None] == steps, perm_row, 0), axis=2)
    source = (source ^ (band.astype(jnp.int32) * coarse.shape[0])).reshape(1, SLOTS)
    live = steps[None, :] < block_count[0][:, None]
    weight = jnp.where(live, slot_weight[0], 0.0).reshape(1, SLOTS)
    patch = slot_patch.reshape(1, SLOTS)
    target_row = slot_target.reshape(1, SLOTS)

    panel = dot(coarse, cond_weight).astype(BF)
    up, down = from_neighbours(
        jnp.concatenate([fine_state[:2], cotangent[:1]], axis=0),
        jnp.concatenate([fine_state[-2:], cotangent[-1:]], axis=0),
    )
    for bit in (1, 2, 4):
        panel = jnp.concatenate([panel, swap(panel, "band", bit)], axis=0)
    field = after(fine_state, panel)
    pre = conv_state_inner(field, packed, 1, 2)
    panel = jnp.concatenate([panel, swap(panel, "band", 8)], axis=0)
    panel, pre = lax.optimization_barrier((panel, pre))
    far = swap(panel, "band", 16)
    pre = conv_state_inner(field, packed, 3, 2, pre)
    far, pre = lax.optimization_barrier((far, pre))
    cond = spread(panel, far, source, patch, weight)
    pre = after(pre, cond)
    cond_up, cond_down = from_neighbours(cond[: 2 * PC], cond[-2 * PC :])
    pre = conv_state_inner(field, packed, 5, 1, pre)
    pre = conv_state_rim(field, packed, up, down, pre)
    grad_pre, sums = silu_grad(pre, cotangent, up, down, cond, cond_up, cond_down, packed)

    keep, send = collect(here, sums, w_back, patch, target_row, weight)
    grad_pre = after(grad_pre, keep)
    grad_fine = None
    for step, bit in enumerate((16, 8, 4, 2)):
        got = swap(send, "band", bit)
        if step < 3:
            grad_fine = conv_grad(grad_pre, packed_back, cotangent, 2 * step, 2, grad_fine)
            got, grad_fine = lax.optimization_barrier((got, grad_fine))
        keep, send = halve(keep, got)
    even, odd = settle(keep, swap(send, "band", 1))
    got = swap(odd, "group", 1)
    last = swap(jnp.concatenate([even[16:], got[16:]], axis=0), "group", 2)
    grad_owned = finish(here, even, got, last, cond_weight)
    return grad_fine, grad_owned


def solution(mesh):
    rows3 = P(BOTH, None, None)
    rows2 = P(BOTH, None)
    return jax.shard_map(
        body,
        mesh=mesh,
        in_specs=(rows3, rows3, rows2, P(), P(), rows3, rows3, rows3, rows2, P()),
        out_specs=(rows3, rows2),
        check_vma=False,
    )
```

```python
import functools

import jax
import jax.numpy as jnp
import numpy as np
from jax import lax
from jax.experimental import pallas as pl
from jax.experimental.pallas import tpu as pltpu
from jax.sharding import PartitionSpec as P

PW = 16
ROWS = 12
LON = 2048
PC = LON // PW
CH = 128
PAIRS = ROWS // 2
EXT = ROWS + 2
SLOTS = 2048
OWNERS = 128
BF = jnp.bfloat16
F32 = jnp.float32
MB = 1 << 20
BOTH = ("group", "band")


def dot(a, b):
    return jnp.dot(a, b, preferred_element_type=F32)


WHOLE = pl.BlockSpec(memory_space=pltpu.VMEM)


def params(mib):
    return pltpu.CompilerParams(vmem_limit_bytes=mib * MB)


ANYWHERE = pl.BlockSpec(memory_space=pl.ANY)
SCALARS = pl.BlockSpec(memory_space=pltpu.SMEM)
MESH_BITS = (4, 2, 16, 8, 1)


def block_of(other):
    place = 0
    for to, bit in enumerate(MESH_BITS):
        place += jnp.where((other & bit) != 0, 1 << to, 0)
    return place


def project_kernel(coarse, w_ref, out):
    out[...] = dot(coarse[...], w_ref[...]).astype(BF)


def project(coarse, cond_weight):
    return pl.pallas_call(
        project_kernel,
        in_specs=[WHOLE] * 2,
        out_specs=WHOLE,
        out_shape=jax.ShapeDtypeStruct((coarse.shape[0], CH), BF),
        compiler_params=params(4),
        name="project",
    )(coarse, cond_weight)


def rims_kernel(field, cot, head, tail, sems):
    copies = [
        pltpu.make_async_copy(field.at[pl.ds(0, 2)], head.at[pl.ds(0, 2)], sems.at[0]),
        pltpu.make_async_copy(cot.at[pl.ds(0, 1)], head.at[pl.ds(2, 1)], sems.at[1]),
        pltpu.make_async_copy(field.at[pl.ds(ROWS - 2, 2)], tail.at[pl.ds(0, 2)], sems.at[2]),
        pltpu.make_async_copy(cot.at[pl.ds(ROWS - 1, 1)], tail.at[pl.ds(2, 1)], sems.at[3]),
    ]
    for copy in copies:
        copy.start()
    for copy in copies:
        copy.wait()


def rims(field, cot):
    rim = jax.ShapeDtypeStruct((3, LON, CH), BF)
    return pl.pallas_call(
        rims_kernel,
        in_specs=[pl.BlockSpec(memory_space=pltpu.HBM)] * 2,
        out_specs=[ANYWHERE] * 2,
        out_shape=[rim, rim],
        scratch_shapes=[pltpu.SemaphoreType.DMA((4,))],
        compiler_params=params(4),
        name="rims",
    )(field, cot)


def pack_kernel(w_ref, packed, back, w_back):
    zero = jnp.zeros((CH, CH), BF)
    left, right = slice(0, CH), slice(CH, 2 * CH)
    for kx in range(3):
        flipped = []
        for ky in range(3):
            turned = w_ref[2 - ky, 2 - kx].astype(F32).T.astype(BF)
            w_back[ky, kx * CH : (kx + 1) * CH, :] = turned
            flipped.append(turned)
        for r in range(4):
            rows = slice(r * CH, (r + 1) * CH)
            packed[kx, rows, left] = w_ref[r, kx] if r < 3 else zero
            packed[kx, rows, right] = w_ref[r - 1, kx] if r >= 1 else zero
            back[kx, rows, left] = flipped[r] if r < 3 else zero
            back[kx, rows, right] = flipped[r - 1] if r >= 1 else zero


def pack(conv_weight):
    both = jax.ShapeDtypeStruct((3, 4 * CH, 2 * CH), BF)
    return pl.pallas_call(
        pack_kernel,
        in_specs=[WHOLE],
        out_specs=[WHOLE] * 3,
        out_shape=[both, both, jax.ShapeDtypeStruct((3, 3 * CH, CH), BF)],
        compiler_params=params(4),
        name="pack",
    )(conv_weight)


def conv_pair(rows, w_ref, write):
    lhs = jnp.concatenate(rows, axis=1)
    left = dot(lhs, w_ref[0])
    right = dot(lhs, w_ref[2])
    place = lax.broadcasted_iota(jnp.int32, (LON, 1), 0)
    total = dot(lhs, w_ref[1])
    total += jnp.where(place == 0, 0.0, pltpu.roll(left, 1, 0))
    total += jnp.where(place == LON - 1, 0.0, pltpu.roll(right, LON - 1, 0))
    write(0, total[:, :CH])
    write(1, total[:, CH:])


def conv_state_inner_kernel(start, *refs):
    field, w_ref, out = refs[0], refs[1], refs[-1]
    q = start + pl.program_id(0)

    def write(r, value):
        out[2 * q + r] = value

    conv_pair([field[2 * q - 2 + r] for r in range(4)], w_ref, write)


def conv_state_rim_kernel(field, w_ref, up, down, before, out):
    def write_to(at):
        def write(r, value):
            out[at + r] = value

        return write

    @pl.when(pl.program_id(0) == 0)
    def _():
        conv_pair([up[0], up[1], field[0], field[1]], w_ref, write_to(0))

    @pl.when(pl.program_id(0) == 1)
    def _():
        conv_pair([field[ROWS - 2], field[ROWS - 1], down[0], down[1]], w_ref, write_to(ROWS))


def conv_cost(pairs):
    return pl.CostEstimate(
        flops=4 * pairs * LON * 12 * CH * CH, bytes_accessed=pairs * LON * CH * 12, transcendentals=0
    )


PRE = pltpu.VMEM((EXT, LON, CH), F32)


def conv_state_inner(field, packed, start, count, before=None):
    args = (field, packed) if before is None else (field, packed, before)
    return pl.pallas_call(
        functools.partial(conv_state_inner_kernel, start),
        grid=(count,),
        in_specs=[WHOLE] * len(args),
        out_specs=WHOLE,
        out_shape=PRE,
        input_output_aliases={} if before is None else {2: 0},
        compiler_params=params(12),
        cost_estimate=conv_cost(count),
        name="conv_state",
    )(*args)


def conv_state_rim(field, packed, up, down, before):
    return pl.pallas_call(
        conv_state_rim_kernel,
        grid=(2,),
        in_specs=[WHOLE] * 5,
        out_specs=WHOLE,
        out_shape=PRE,
        input_output_aliases={4: 0},
        compiler_params=params(12),
        cost_estimate=conv_cost(2),
        name="conv_state_rim",
    )(field, packed, up, down, before)


def conv_grad_kernel(start, *refs):
    field, w_ref, cot, out = refs[0], refs[1], refs[2], refs[-1]
    p = start + pl.program_id(0)

    def write(r, value):
        out[r] = (cot[2 * p + r].astype(F32) + value).astype(BF)

    conv_pair([field[2 * p + r] for r in range(4)], w_ref, write)


def conv_grad(field, packed, cotangent, start, count, before=None):
    args = [field, packed, cotangent] + ([] if before is None else [before])
    specs = [WHOLE] * 3 + ([] if before is None else [pl.BlockSpec(memory_space=pl.ANY)])
    return pl.pallas_call(
        functools.partial(conv_grad_kernel, start),
        grid=(count,),
        in_specs=specs,
        out_specs=pl.BlockSpec((2, LON, CH), lambda i: (start + i, 0, 0)),
        out_shape=jax.ShapeDtypeStruct((ROWS, LON, CH), BF),
        input_output_aliases={} if before is None else {3: 0},
        compiler_params=params(16),
        cost_estimate=conv_cost(count),
        name="conv_grad",
    )(*args)


SC_CHUNK = 512


def onehot(height, index_row):
    place = lax.broadcasted_iota(jnp.int32, (height, index_row.shape[1]), 0)
    return jnp.where(place == index_row, 1.0, 0.0).astype(BF)


def contract0(a, b):
    return lax.dot_general(a, b, (((0,), (0,)), ((), ())), preferred_element_type=F32)


def contract1(a, b):
    return lax.dot_general(a, b, (((1,), (1,)), ((), ())), preferred_element_type=F32)


def slot_row(ref, first):
    return jnp.concatenate([ref[first + k : first + k + 1, :] for k in range(SC_CHUNK // OWNERS)], axis=1)


def live_weight(weight, count):
    slot = lax.broadcasted_iota(jnp.int32, weight.shape, 0)
    return jnp.where(slot < count[...], weight[...], 0.0)


def spread_kernel(here, near, far, perm, patch, target, weight, count, out, source, live):
    live[...] = live_weight(weight, count)
    row = jnp.zeros(target.shape, jnp.int32)
    for t in range(16):
        row += jnp.where(target[...] == t, perm[t : t + 1, :], 0)
    source[...] = block_of((row >> 6) ^ here[1]) * 64 + (row & 63)
    patches = ROWS * PC
    panel = jnp.concatenate([near[...], far[...]], axis=0)
    total = jnp.zeros((patches, CH), F32)
    for first in range(0, 16, SC_CHUNK // OWNERS):
        picked = contract0(panel, onehot(SLOTS, slot_row(source, first)))
        picked = (picked * slot_row(live, first)).astype(BF)
        total += contract1(onehot(patches, slot_row(patch, first)), picked)
    out[...] = total.astype(BF)


def spread(here, near, far, perm, patch, target, weight, count):
    return pl.pallas_call(
        spread_kernel,
        in_specs=[SCALARS] + [WHOLE] * 7,
        out_specs=WHOLE,
        out_shape=jax.ShapeDtypeStruct((ROWS * PC, CH), BF),
        scratch_shapes=[pltpu.VMEM((16, OWNERS), jnp.int32), pltpu.VMEM((16, OWNERS), F32)],
        compiler_params=params(16),
        cost_estimate=pl.CostEstimate(flops=4 * 2048 * 2048 * 128, bytes_accessed=MB, transcendentals=0),
        name="spread",
    )(here, near, far, perm, patch, target, weight, count)


EX_CELLS = 1024
RD_CELLS = 256


def patch_marks(count):
    cells = np.arange(count)[:, None]
    inside = cells // PW == np.arange(count // PW)[None, :]
    marks = [inside, inside & (cells % PW == 0), inside & (cells % PW == PW - 1)]
    return np.concatenate(marks, axis=1).astype(np.float32)


def shift_patch(value, step):
    place = lax.broadcasted_iota(jnp.int32, (PC, 1), 0)
    if step > 0:
        return jnp.where(place == 0, 0.0, pltpu.roll(value, 1, 0))
    return jnp.where(place == PC - 1, 0.0, pltpu.roll(value, PC - 1, 0))


def silu_kernel(pre, cot, up, down, cond, c_up, c_down, w_ref, ex_ref, rd_ref, out, sums):
    q = pl.program_id(0)
    above = jnp.where(q == 0, c_up[...], cond[jnp.maximum(q - 1, 0)])
    below = jnp.where(q == PAIRS, c_down[...], cond[jnp.minimum(q, PAIRS - 1)])
    lhs = jnp.concatenate([above[:PC], above[PC:], below[:PC], below[PC:]], axis=1)
    west, here, east = [dot(lhs, w_ref[k]) for k in range(3)]
    inner = (west + here + east).astype(BF)
    at_first = (shift_patch(west, 1) - west).astype(BF)
    at_last = (shift_patch(east, -1) - east).astype(BF)
    per = EX_CELLS // PW
    part_sum, part_first, part_last = [], [], []
    for lo in range(0, LON, EX_CELLS):
        cells = slice(lo, lo + EX_CELLS)
        cut = slice(lo // PW, lo // PW + per)
        terms = jnp.concatenate([inner[cut], at_first[cut], at_last[cut]], axis=0)
        spread_terms = dot(ex_ref[...], terms)
        weights = [
            jnp.where(q == 0, up[2, cells], cot[jnp.maximum(2 * q - 1, 0), cells]),
            jnp.where(q == PAIRS, down[2, cells], cot[jnp.minimum(2 * q, ROWS - 1), cells]),
        ]
        grads = []
        for r in range(2):
            half = 0.5 * (pre[2 * q + r, cells] + spread_terms[:, r * CH : (r + 1) * CH])
            t = jnp.tanh(half)
            slope = (0.5 + 0.5 * t) * (1.0 + half * (1.0 - t))
            g = (weights[r].astype(F32) * slope).astype(BF)
            out[2 * q + r, cells] = g
            grads.append(g)
        grads = jnp.concatenate(grads, axis=1)
        for at in range(0, EX_CELLS, RD_CELLS):
            reduced = dot(rd_ref[...], grads[at : at + RD_CELLS])
            part_sum.append(reduced[:PW])
            part_first.append(reduced[PW : 2 * PW])
            part_last.append(reduced[2 * PW :])
    whole, firsts, lasts = [jnp.concatenate(p, axis=0) for p in (part_sum, part_first, part_last)]
    from_west = (whole - lasts + shift_patch(lasts, 1)).astype(BF)
    from_east = (whole - firsts + shift_patch(firsts, -1)).astype(BF)
    whole = whole.astype(BF)
    for r in range(2):
        cut = slice(r * CH, (r + 1) * CH)
        sums[2 * q + r] = jnp.concatenate([from_west[:, cut], whole[:, cut], from_east[:, cut]], axis=1)


def silu_grad(pre, cotangent, up, down, cond, c_up, c_down, packed):
    expand = jnp.asarray(patch_marks(EX_CELLS), BF)
    reduce_m = jnp.asarray(patch_marks(RD_CELLS).T, BF)
    cond = cond.reshape(PAIRS, 2 * PC, CH)
    return pl.pallas_call(
        silu_kernel,
        grid=(PAIRS + 1,),
        in_specs=[WHOLE] * 10,
        out_specs=[WHOLE, WHOLE],
        out_shape=[pltpu.VMEM((EXT, LON, CH), BF), pltpu.VMEM((EXT, PC, 3 * CH), BF)],
        compiler_params=params(12),
        cost_estimate=pl.CostEstimate(flops=10**9, bytes_accessed=8 * ROWS * LON * CH, transcendentals=0),
        name="silu_grad",
    )(pre, cotangent, up, down, cond, c_up, c_down, packed, expand, reduce_m)


def collect_kernel(here, sums, w_ref, patch, target, weight, count, keep, send, total, slots, shares, picked):
    patches = ROWS * PC
    grad_patch = dot(sums[:patches], w_ref[0])
    grad_patch += dot(sums[PC : PC + patches], w_ref[1])
    grad_patch += dot(sums[2 * PC :], w_ref[2])
    grad_patch = grad_patch.astype(BF)
    owner = lax.broadcasted_iota(jnp.int32, (OWNERS, OWNERS), 0)
    place = block_of((owner & 31) ^ here[1]) * 4 + ((owner >> 5) ^ here[0])
    order = jnp.where(place == lax.broadcasted_iota(jnp.int32, (OWNERS, OWNERS), 1), 1.0, 0.0)
    values = jnp.concatenate(
        [patch[...].astype(F32), target[...].astype(F32), live_weight(weight, count)], axis=0
    )
    values = jnp.dot(values, order, preferred_element_type=F32, precision=lax.Precision.HIGHEST)
    slots[...] = (values[:32] + 0.5).astype(jnp.int32)
    step = lax.broadcasted_iota(jnp.int32, (16, OWNERS), 0)
    for k in range(16):
        hit = step == slots[16 + k : 17 + k, :]
        shares[k] = jnp.where(hit, values[32 + k : 33 + k, :], 0.0)
    for first in range(0, 16, SC_CHUNK // OWNERS):
        got = contract0(grad_patch, onehot(patches, slot_row(slots, first)))
        for k in range(SC_CHUNK // OWNERS):
            picked[first + k] = got[:, k * OWNERS : (k + 1) * OWNERS]
    for t in range(16):
        mine = picked[0] * shares[0, t : t + 1, :]
        for k in range(1, 16):
            mine += picked[k] * shares[k, t : t + 1, :]
        total[pl.ds(t, OWNERS, stride=16), :] = mine.T
    keep[...] = total[: SLOTS // 2]
    send[...] = total[SLOTS // 2 :].astype(BF)


def collect(here, sums, w, patch, target, weight, count):
    return pl.pallas_call(
        collect_kernel,
        in_specs=[SCALARS] + [WHOLE] * 6,
        out_specs=[WHOLE, WHOLE],
        out_shape=[
            jax.ShapeDtypeStruct((SLOTS // 2, CH), F32),
            jax.ShapeDtypeStruct((SLOTS // 2, CH), BF),
        ],
        scratch_shapes=[
            pltpu.VMEM((SLOTS, CH), F32),
            pltpu.VMEM((32, OWNERS), jnp.int32),
            pltpu.VMEM((16, 16, OWNERS), F32),
            pltpu.VMEM((16, CH, OWNERS), F32),
        ],
        compiler_params=params(16),
        cost_estimate=pl.CostEstimate(flops=2 * 2048 * 2048 * 128, bytes_accessed=2 * MB, transcendentals=0),
        name="collect",
    )(here, sums.reshape(EXT * PC, 3 * CH), w, patch, target, weight, count)


def halve_kernel(kept, got, keep, send):
    half = keep.shape[0]
    total = kept[...] + got[...].astype(F32)
    keep[...] = total[:half]
    send[...] = total[half:].astype(BF)


def halve(kept, got):
    half = kept.shape[0] // 2
    return pl.pallas_call(
        halve_kernel,
        in_specs=[WHOLE] * 2,
        out_specs=[WHOLE, WHOLE],
        out_shape=[jax.ShapeDtypeStruct((half, CH), F32), jax.ShapeDtypeStruct((half, CH), BF)],
        compiler_params=params(4),
        name="halve",
    )(kept, got)


def settle_kernel(kept, got, even, odd):
    total = (kept[...] + got[...].astype(F32)).astype(BF)
    even[:16] = total[:16]
    even[16:] = total[32:48]
    odd[:16] = total[16:32]
    odd[16:] = total[48:]


def settle(kept, got):
    half = jax.ShapeDtypeStruct((32, CH), BF)
    return pl.pallas_call(
        settle_kernel,
        in_specs=[WHOLE] * 2,
        out_specs=[WHOLE, WHOLE],
        out_shape=[half, half],
        compiler_params=params(4),
        name="settle",
    )(kept, got)


def finish_kernel(here, even, got, last, w_ref, out):
    rows = jnp.concatenate([even[:16], got[:16], last[...]], axis=0)
    value = contract1(rows, w_ref[...])
    for k in range(4):
        to = pl.multiple_of((here[0] ^ k) * 16, 16)
        out[pl.ds(to, 16), :] = value[16 * k : 16 * k + 16]


def finish(here, even, got, last, cond_weight):
    return pl.pallas_call(
        finish_kernel,
        in_specs=[pl.BlockSpec(memory_space=pltpu.SMEM)] + [WHOLE] * 4,
        out_specs=WHOLE,
        out_shape=jax.ShapeDtypeStruct((64, cond_weight.shape[0]), F32),
        compiler_params=params(4),
        name="finish",
    )(here, even, got, last, cond_weight)


def from_neighbours(head, tail):
    count = lax.axis_size(BOTH)
    up = lax.ppermute(tail, BOTH, [(i, i + 1) for i in range(count - 1)])
    down = lax.ppermute(head, BOTH, [(i + 1, i) for i in range(count - 1)])
    return up, down


def swap(value, axis, bit):
    return lax.ppermute(value, axis, [(i, i ^ bit) for i in range(lax.axis_size(axis))])


def after(value, *earlier):
    return lax.optimization_barrier((value,) + earlier)[0]


def body(
    fine_state,
    cotangent,
    coarse,
    conv_weight,
    cond_weight,
    slot_patch,
    slot_target,
    slot_weight,
    block_count,
    panel_perm,
):
    group = lax.axis_index("group")
    band = lax.axis_index("band")
    here = jnp.stack([group, band]).astype(jnp.int32)
    perm = lax.dynamic_index_in_dim(panel_perm, group, 0, keepdims=False).reshape(-1, 16).T
    patch, target, weight = slot_patch[0].T, slot_target[0].T, slot_weight[0].T

    panel = project(coarse, cond_weight)
    first = swap(panel, "band", MESH_BITS[0])
    panel = jnp.concatenate([panel, first], axis=0)
    packed, packed_back, w_back = pack(after(conv_weight, panel))
    panel = jnp.concatenate([panel, swap(panel, "band", MESH_BITS[1])], axis=0)
    head, tail = rims(fine_state, cotangent)
    panel, head, tail = lax.optimization_barrier((panel, head, tail))
    up, down = from_neighbours(head, tail)
    field = after(fine_state, panel)
    panel = jnp.concatenate([panel, swap(panel, "band", MESH_BITS[2])], axis=0)
    pre = conv_state_inner(field, packed, 1, 2)
    panel, pre = lax.optimization_barrier((panel, pre))
    panel = jnp.concatenate([panel, swap(panel, "band", MESH_BITS[3])], axis=0)
    pre = conv_state_inner(field, packed, 3, 2, pre)
    panel, pre = lax.optimization_barrier((panel, pre))
    far = swap(panel, "band", MESH_BITS[4])
    cond = spread(here, panel, far, perm, patch, target, weight, block_count)
    pre = after(pre, cond)
    cond_up, cond_down = from_neighbours(cond[: 2 * PC], cond[-2 * PC :])
    pre = conv_state_inner(field, packed, 5, 1, pre)
    pre = conv_state_rim(field, packed, up, down, pre)
    grad_pre, sums = silu_grad(pre, cotangent, up, down, cond, cond_up, cond_down, packed)

    keep, send = collect(here, sums, w_back, patch, target, weight, block_count)
    grad_pre = after(grad_pre, keep)
    grad_fine = None
    for step, bit in enumerate(MESH_BITS[:0:-1]):
        got = swap(send, "band", bit)
        if step < 3:
            grad_fine = conv_grad(grad_pre, packed_back, cotangent, 2 * step, 2, grad_fine)
            got, grad_fine = lax.optimization_barrier((got, grad_fine))
        keep, send = halve(keep, got)
    even, odd = settle(keep, swap(send, "band", MESH_BITS[0]))
    got = swap(odd, "group", 1)
    last = swap(jnp.concatenate([even[16:], got[16:]], axis=0), "group", 2)
    grad_owned = finish(here, even, got, last, cond_weight)
    return grad_fine, grad_owned


def solution(mesh):
    rows3 = P(BOTH, None, None)
    rows2 = P(BOTH, None)
    return jax.shard_map(
        body,
        mesh=mesh,
        in_specs=(rows3, rows3, rows2, P(), P(), rows3, rows3, rows3, rows2, P()),
        out_specs=(rows3, rows2),
        check_vma=False,
    )
```

```python
import functools

import jax
import jax.numpy as jnp
import numpy as np
from jax import lax
from jax.experimental import pallas as pl
from jax.experimental.pallas import tpu as pltpu
from jax.sharding import PartitionSpec as P

PW = 16
ROWS = 12
LON = 2048
PC = LON // PW
CH = 128
PAIRS = ROWS // 2
EXT = ROWS + 2
SLOTS = 2048
OWNERS = 128
BF = jnp.bfloat16
F32 = jnp.float32
MB = 1 << 20
BOTH = ("group", "band")


def dot(a, b):
    return jnp.dot(a, b, preferred_element_type=F32)


WHOLE = pl.BlockSpec(memory_space=pltpu.VMEM)


def params(mib):
    return pltpu.CompilerParams(vmem_limit_bytes=mib * MB)


ANYWHERE = pl.BlockSpec(memory_space=pl.ANY)
SCALARS = pl.BlockSpec(memory_space=pltpu.SMEM)
MESH_BITS = (4, 2, 16, 8, 1)


def block_of(other):
    place = 0
    for to, bit in enumerate(MESH_BITS):
        place += jnp.where((other & bit) != 0, 1 << to, 0)
    return place


def project_kernel(coarse, w_ref, out):
    out[...] = dot(coarse[...], w_ref[...]).astype(BF)


def project(coarse, cond_weight):
    return pl.pallas_call(
        project_kernel,
        in_specs=[WHOLE] * 2,
        out_specs=WHOLE,
        out_shape=jax.ShapeDtypeStruct((coarse.shape[0], CH), BF),
        compiler_params=params(4),
        name="project",
    )(coarse, cond_weight)


def rims_kernel(field, cot, head, tail, sems):
    copies = [
        pltpu.make_async_copy(field.at[pl.ds(0, 2)], head.at[pl.ds(0, 2)], sems.at[0]),
        pltpu.make_async_copy(cot.at[pl.ds(0, 1)], head.at[pl.ds(2, 1)], sems.at[1]),
        pltpu.make_async_copy(field.at[pl.ds(ROWS - 2, 2)], tail.at[pl.ds(0, 2)], sems.at[2]),
        pltpu.make_async_copy(cot.at[pl.ds(ROWS - 1, 1)], tail.at[pl.ds(2, 1)], sems.at[3]),
    ]
    for copy in copies:
        copy.start()
    for copy in copies:
        copy.wait()


def rims(field, cot):
    rim = jax.ShapeDtypeStruct((3, LON, CH), BF)
    return pl.pallas_call(
        rims_kernel,
        in_specs=[ANYWHERE] * 2,
        out_specs=[ANYWHERE] * 2,
        out_shape=[rim, rim],
        scratch_shapes=[pltpu.SemaphoreType.DMA((4,))],
        compiler_params=params(60),
        name="rims",
    )(field, cot)


def pack_kernel(w_ref, packed, back, w_back):
    zero = jnp.zeros((CH, CH), BF)
    left, right = slice(0, CH), slice(CH, 2 * CH)
    for kx in range(3):
        flipped = []
        for ky in range(3):
            turned = w_ref[2 - ky, 2 - kx].astype(F32).T.astype(BF)
            w_back[ky, kx * CH : (kx + 1) * CH, :] = turned
            flipped.append(turned)
        for r in range(4):
            rows = slice(r * CH, (r + 1) * CH)
            packed[kx, rows, left] = w_ref[r, kx] if r < 3 else zero
            packed[kx, rows, right] = w_ref[r - 1, kx] if r >= 1 else zero
            back[kx, rows, left] = flipped[r] if r < 3 else zero
            back[kx, rows, right] = flipped[r - 1] if r >= 1 else zero


def pack(conv_weight):
    both = jax.ShapeDtypeStruct((3, 4 * CH, 2 * CH), BF)
    return pl.pallas_call(
        pack_kernel,
        in_specs=[WHOLE],
        out_specs=[WHOLE] * 3,
        out_shape=[both, both, jax.ShapeDtypeStruct((3, 3 * CH, CH), BF)],
        compiler_params=params(4),
        name="pack",
    )(conv_weight)


def conv_pair(rows, w_ref, write):
    lhs = jnp.concatenate(rows, axis=1)
    left = dot(lhs, w_ref[0])
    right = dot(lhs, w_ref[2])
    place = lax.broadcasted_iota(jnp.int32, (LON, 1), 0)
    total = dot(lhs, w_ref[1])
    total += jnp.where(place == 0, 0.0, pltpu.roll(left, 1, 0))
    total += jnp.where(place == LON - 1, 0.0, pltpu.roll(right, LON - 1, 0))
    write(0, total[:, :CH])
    write(1, total[:, CH:])


def conv_state_inner_kernel(start, *refs):
    field, w_ref, out = refs[0], refs[1], refs[-1]
    q = start + pl.program_id(0)

    def write(r, value):
        out[2 * q + r] = value

    conv_pair([field[2 * q - 2 + r] for r in range(4)], w_ref, write)


def conv_state_rim_kernel(field, w_ref, up, down, before, out):
    def write_to(at):
        def write(r, value):
            out[at + r] = value

        return write

    @pl.when(pl.program_id(0) == 0)
    def _():
        conv_pair([up[0], up[1], field[0], field[1]], w_ref, write_to(0))

    @pl.when(pl.program_id(0) == 1)
    def _():
        conv_pair([field[ROWS - 2], field[ROWS - 1], down[0], down[1]], w_ref, write_to(ROWS))


def conv_cost(pairs):
    return pl.CostEstimate(
        flops=4 * pairs * LON * 12 * CH * CH, bytes_accessed=pairs * LON * CH * 12, transcendentals=0
    )


PRE = pltpu.VMEM((EXT, LON, CH), F32)


def conv_state_inner(field, packed, start, count, before=None):
    args = (field, packed) if before is None else (field, packed, before)
    return pl.pallas_call(
        functools.partial(conv_state_inner_kernel, start),
        grid=(count,),
        in_specs=[WHOLE] * len(args),
        out_specs=WHOLE,
        out_shape=PRE,
        input_output_aliases={} if before is None else {2: 0},
        compiler_params=params(8),
        cost_estimate=conv_cost(count),
        name="conv_state",
    )(*args)


def conv_state_rim(field, packed, up, down, before):
    return pl.pallas_call(
        conv_state_rim_kernel,
        grid=(2,),
        in_specs=[WHOLE] * 5,
        out_specs=WHOLE,
        out_shape=PRE,
        input_output_aliases={4: 0},
        compiler_params=params(8),
        cost_estimate=conv_cost(2),
        name="conv_state_rim",
    )(field, packed, up, down, before)


def conv_grad_kernel(start, *refs):
    field, w_ref, cot, out = refs[0], refs[1], refs[2], refs[-1]
    p = start + pl.program_id(0)

    def write(r, value):
        out[r] = (cot[2 * p + r].astype(F32) + value).astype(BF)

    conv_pair([field[2 * p + r] for r in range(4)], w_ref, write)


def conv_grad(field, packed, cotangent, start, count, before=None):
    args = [field, packed, cotangent] + ([] if before is None else [before])
    specs = [WHOLE] * 3 + ([] if before is None else [pl.BlockSpec(memory_space=pl.ANY)])
    return pl.pallas_call(
        functools.partial(conv_grad_kernel, start),
        grid=(count,),
        in_specs=specs,
        out_specs=pl.BlockSpec((2, LON, CH), lambda i: (start + i, 0, 0)),
        out_shape=jax.ShapeDtypeStruct((ROWS, LON, CH), BF),
        input_output_aliases={} if before is None else {3: 0},
        compiler_params=params(8),
        cost_estimate=conv_cost(count),
        name="conv_grad",
    )(*args)


SC_CHUNK = 512


def onehot(height, index_row):
    place = lax.broadcasted_iota(jnp.int32, (height, index_row.shape[1]), 0)
    return jnp.where(place == index_row, 1.0, 0.0).astype(BF)


def contract0(a, b):
    return lax.dot_general(a, b, (((0,), (0,)), ((), ())), preferred_element_type=F32)


def contract1(a, b):
    return lax.dot_general(a, b, (((1,), (1,)), ((), ())), preferred_element_type=F32)


def slot_row(ref, first):
    return jnp.concatenate([ref[first + k : first + k + 1, :] for k in range(SC_CHUNK // OWNERS)], axis=1)


def live_weight(weight, count):
    slot = lax.broadcasted_iota(jnp.int32, weight.shape, 0)
    return jnp.where(slot < count[...], weight[...], 0.0)


def spread_kernel(here, near, far, perm, patch, target, weight, count, out, source, live):
    live[...] = live_weight(weight, count)
    row = jnp.zeros(target.shape, jnp.int32)
    for t in range(16):
        row += jnp.where(target[...] == t, perm[t : t + 1, :], 0)
    source[...] = block_of((row >> 6) ^ here[1]) * 64 + (row & 63)
    patches = ROWS * PC
    panel = jnp.concatenate([near[...], far[...]], axis=0)
    total = jnp.zeros((patches, CH), F32)
    for first in range(0, 16, SC_CHUNK // OWNERS):
        picked = contract0(panel, onehot(SLOTS, slot_row(source, first)))
        picked = (picked * slot_row(live, first)).astype(BF)
        total += contract1(onehot(patches, slot_row(patch, first)), picked)
    out[...] = total.astype(BF)


def spread(here, near, far, perm, patch, target, weight, count):
    return pl.pallas_call(
        spread_kernel,
        in_specs=[SCALARS] + [WHOLE] * 7,
        out_specs=WHOLE,
        out_shape=jax.ShapeDtypeStruct((ROWS * PC, CH), BF),
        scratch_shapes=[pltpu.VMEM((16, OWNERS), jnp.int32), pltpu.VMEM((16, OWNERS), F32)],
        compiler_params=params(16),
        cost_estimate=pl.CostEstimate(flops=4 * 2048 * 2048 * 128, bytes_accessed=MB, transcendentals=0),
        name="spread",
    )(here, near, far, perm, patch, target, weight, count)


EX_CELLS = 1024
RD_CELLS = 256


def patch_marks(count):
    cells = np.arange(count)[:, None]
    inside = cells // PW == np.arange(count // PW)[None, :]
    marks = [inside, inside & (cells % PW == 0), inside & (cells % PW == PW - 1)]
    return np.concatenate(marks, axis=1).astype(np.float32)


def shift_patch(value, step):
    place = lax.broadcasted_iota(jnp.int32, (PC, 1), 0)
    if step > 0:
        return jnp.where(place == 0, 0.0, pltpu.roll(value, 1, 0))
    return jnp.where(place == PC - 1, 0.0, pltpu.roll(value, PC - 1, 0))


def silu_kernel(pre, cot, up, down, cond, c_up, c_down, w_ref, ex_ref, rd_ref, out, sums):
    q = pl.program_id(0)
    above = jnp.where(q == 0, c_up[...], cond[jnp.maximum(q - 1, 0)])
    below = jnp.where(q == PAIRS, c_down[...], cond[jnp.minimum(q, PAIRS - 1)])
    lhs = jnp.concatenate([above[:PC], above[PC:], below[:PC], below[PC:]], axis=1)
    west, here, east = [dot(lhs, w_ref[k]) for k in range(3)]
    inner = (west + here + east).astype(BF)
    at_first = (shift_patch(west, 1) - west).astype(BF)
    at_last = (shift_patch(east, -1) - east).astype(BF)
    per = EX_CELLS // PW
    part_sum, part_first, part_last = [], [], []
    for lo in range(0, LON, EX_CELLS):
        cells = slice(lo, lo + EX_CELLS)
        cut = slice(lo // PW, lo // PW + per)
        terms = jnp.concatenate([inner[cut], at_first[cut], at_last[cut]], axis=0)
        spread_terms = dot(ex_ref[...], terms)
        weights = [
            jnp.where(q == 0, up[2, cells], cot[jnp.maximum(2 * q - 1, 0), cells]),
            jnp.where(q == PAIRS, down[2, cells], cot[jnp.minimum(2 * q, ROWS - 1), cells]),
        ]
        grads = []
        for r in range(2):
            half = 0.5 * (pre[2 * q + r, cells] + spread_terms[:, r * CH : (r + 1) * CH])
            t = jnp.tanh(half)
            slope = (0.5 + 0.5 * t) * (1.0 + half * (1.0 - t))
            g = (weights[r].astype(F32) * slope).astype(BF)
            out[2 * q + r, cells] = g
            grads.append(g)
        grads = jnp.concatenate(grads, axis=1)
        for at in range(0, EX_CELLS, RD_CELLS):
            reduced = dot(rd_ref[...], grads[at : at + RD_CELLS])
            part_sum.append(reduced[:PW])
            part_first.append(reduced[PW : 2 * PW])
            part_last.append(reduced[2 * PW :])
    whole, firsts, lasts = [jnp.concatenate(p, axis=0) for p in (part_sum, part_first, part_last)]
    from_west = (whole - lasts + shift_patch(lasts, 1)).astype(BF)
    from_east = (whole - firsts + shift_patch(firsts, -1)).astype(BF)
    whole = whole.astype(BF)
    for r in range(2):
        cut = slice(r * CH, (r + 1) * CH)
        sums[2 * q + r] = jnp.concatenate([from_west[:, cut], whole[:, cut], from_east[:, cut]], axis=1)


def silu_grad(pre, cotangent, up, down, cond, c_up, c_down, packed):
    expand = jnp.asarray(patch_marks(EX_CELLS), BF)
    reduce_m = jnp.asarray(patch_marks(RD_CELLS).T, BF)
    cond = cond.reshape(PAIRS, 2 * PC, CH)
    return pl.pallas_call(
        silu_kernel,
        grid=(PAIRS + 1,),
        in_specs=[WHOLE] * 10,
        out_specs=[WHOLE, WHOLE],
        out_shape=[pltpu.VMEM((EXT, LON, CH), BF), pltpu.VMEM((EXT, PC, 3 * CH), BF)],
        compiler_params=params(8),
        cost_estimate=pl.CostEstimate(flops=10**9, bytes_accessed=8 * ROWS * LON * CH, transcendentals=0),
        name="silu_grad",
    )(pre, cotangent, up, down, cond, c_up, c_down, packed, expand, reduce_m)


def collect_kernel(here, sums, w_ref, patch, target, weight, count, keep, send, total, slots, shares, picked):
    patches = ROWS * PC
    grad_patch = dot(sums[:patches], w_ref[0])
    grad_patch += dot(sums[PC : PC + patches], w_ref[1])
    grad_patch += dot(sums[2 * PC :], w_ref[2])
    grad_patch = grad_patch.astype(BF)
    owner = lax.broadcasted_iota(jnp.int32, (OWNERS, OWNERS), 0)
    place = block_of((owner & 31) ^ here[1]) * 4 + ((owner >> 5) ^ here[0])
    order = jnp.where(place == lax.broadcasted_iota(jnp.int32, (OWNERS, OWNERS), 1), 1.0, 0.0)
    values = jnp.concatenate(
        [patch[...].astype(F32), target[...].astype(F32), live_weight(weight, count)], axis=0
    )
    values = jnp.dot(values, order, preferred_element_type=F32, precision=lax.Precision.HIGHEST)
    slots[...] = (values[:32] + 0.5).astype(jnp.int32)
    step = lax.broadcasted_iota(jnp.int32, (16, OWNERS), 0)
    for k in range(16):
        hit = step == slots[16 + k : 17 + k, :]
        shares[k] = jnp.where(hit, values[32 + k : 33 + k, :], 0.0)
    for first in range(0, 16, SC_CHUNK // OWNERS):
        got = contract0(grad_patch, onehot(patches, slot_row(slots, first)))
        for k in range(SC_CHUNK // OWNERS):
            picked[first + k] = got[:, k * OWNERS : (k + 1) * OWNERS]
    for t in range(16):
        mine = picked[0] * shares[0, t : t + 1, :]
        for k in range(1, 16):
            mine += picked[k] * shares[k, t : t + 1, :]
        total[pl.ds(t, OWNERS, stride=16), :] = mine.T
    keep[...] = total[: SLOTS // 2]
    send[...] = total[SLOTS // 2 :].astype(BF)


def collect(here, sums, w, patch, target, weight, count):
    return pl.pallas_call(
        collect_kernel,
        in_specs=[SCALARS] + [WHOLE] * 6,
        out_specs=[WHOLE, WHOLE],
        out_shape=[
            jax.ShapeDtypeStruct((SLOTS // 2, CH), F32),
            jax.ShapeDtypeStruct((SLOTS // 2, CH), BF),
        ],
        scratch_shapes=[
            pltpu.VMEM((SLOTS, CH), F32),
            pltpu.VMEM((32, OWNERS), jnp.int32),
            pltpu.VMEM((16, 16, OWNERS), F32),
            pltpu.VMEM((16, CH, OWNERS), F32),
        ],
        compiler_params=params(16),
        cost_estimate=pl.CostEstimate(flops=2 * 2048 * 2048 * 128, bytes_accessed=2 * MB, transcendentals=0),
        name="collect",
    )(here, sums.reshape(EXT * PC, 3 * CH), w, patch, target, weight, count)


def halve_kernel(kept, got, keep, send):
    half = keep.shape[0]
    total = kept[...] + got[...].astype(F32)
    keep[...] = total[:half]
    send[...] = total[half:].astype(BF)


def halve(kept, got):
    half = kept.shape[0] // 2
    return pl.pallas_call(
        halve_kernel,
        in_specs=[WHOLE] * 2,
        out_specs=[WHOLE, WHOLE],
        out_shape=[jax.ShapeDtypeStruct((half, CH), F32), jax.ShapeDtypeStruct((half, CH), BF)],
        compiler_params=params(4),
        name="halve",
    )(kept, got)


def settle_kernel(kept, got, even, odd):
    total = (kept[...] + got[...].astype(F32)).astype(BF)
    even[:16] = total[:16]
    even[16:] = total[32:48]
    odd[:16] = total[16:32]
    odd[16:] = total[48:]


def settle(kept, got):
    half = jax.ShapeDtypeStruct((32, CH), BF)
    return pl.pallas_call(
        settle_kernel,
        in_specs=[WHOLE] * 2,
        out_specs=[WHOLE, WHOLE],
        out_shape=[half, half],
        compiler_params=params(4),
        name="settle",
    )(kept, got)


def finish_kernel(here, even, got, last, w_ref, out):
    rows = jnp.concatenate([even[:16], got[:16], last[...]], axis=0)
    value = contract1(rows, w_ref[...])
    for k in range(4):
        to = pl.multiple_of((here[0] ^ k) * 16, 16)
        out[pl.ds(to, 16), :] = value[16 * k : 16 * k + 16]


def finish(here, even, got, last, cond_weight):
    return pl.pallas_call(
        finish_kernel,
        in_specs=[pl.BlockSpec(memory_space=pltpu.SMEM)] + [WHOLE] * 4,
        out_specs=WHOLE,
        out_shape=jax.ShapeDtypeStruct((64, cond_weight.shape[0]), F32),
        compiler_params=params(4),
        name="finish",
    )(here, even, got, last, cond_weight)


def from_neighbours(head, tail):
    count = lax.axis_size(BOTH)
    up = lax.ppermute(tail, BOTH, [(i, i + 1) for i in range(count - 1)])
    down = lax.ppermute(head, BOTH, [(i + 1, i) for i in range(count - 1)])
    return up, down


def swap(value, axis, bit):
    return lax.ppermute(value, axis, [(i, i ^ bit) for i in range(lax.axis_size(axis))])


def after(value, *earlier):
    return lax.optimization_barrier((value,) + earlier)[0]


def body(
    fine_state,
    cotangent,
    coarse,
    conv_weight,
    cond_weight,
    slot_patch,
    slot_target,
    slot_weight,
    block_count,
    panel_perm,
):
    group = lax.axis_index("group")
    band = lax.axis_index("band")
    here = jnp.stack([group, band]).astype(jnp.int32)
    perm = lax.dynamic_index_in_dim(panel_perm, group, 0, keepdims=False).reshape(-1, 16).T
    patch, target, weight = slot_patch[0].T, slot_target[0].T, slot_weight[0].T

    panel = project(coarse, cond_weight)
    first = swap(panel, "band", MESH_BITS[0])
    panel = jnp.concatenate([panel, first], axis=0)
    panel, here, perm = lax.optimization_barrier((panel, here, perm))
    packed, packed_back, w_back = pack(after(conv_weight, panel))
    head, tail = rims(after(fine_state, panel), cotangent)
    panel = jnp.concatenate([panel, swap(panel, "band", MESH_BITS[1])], axis=0)
    panel, head, tail = lax.optimization_barrier((panel, head, tail))
    up, down = from_neighbours(head, tail)
    field = after(fine_state, panel)
    panel = jnp.concatenate([panel, swap(panel, "band", MESH_BITS[2])], axis=0)
    pre = conv_state_inner(field, packed, 1, 2)
    panel, pre = lax.optimization_barrier((panel, pre))
    panel = jnp.concatenate([panel, swap(panel, "band", MESH_BITS[3])], axis=0)
    pre = conv_state_inner(field, packed, 3, 2, pre)
    panel, pre = lax.optimization_barrier((panel, pre))
    far = swap(panel, "band", MESH_BITS[4])
    pre = conv_state_inner(field, packed, 5, 1, pre)
    far, pre = lax.optimization_barrier((far, pre))
    cond = spread(here, panel, far, perm, patch, target, weight, block_count)
    pre = after(pre, cond)
    cond_up, cond_down = from_neighbours(cond[: 2 * PC], cond[-2 * PC :])
    pre = conv_state_rim(field, packed, up, down, pre)
    grad_pre, sums = silu_grad(pre, cotangent, up, down, cond, cond_up, cond_down, packed)

    keep, send = collect(here, sums, w_back, patch, target, weight, block_count)
    grad_fine = None

    def meanwhile(got, pair, grad_fine):
        grad_fine = conv_grad(after(grad_pre, keep), packed_back, cotangent, pair, 1, grad_fine)
        return lax.optimization_barrier((got, grad_fine))

    for pair, bit in enumerate(MESH_BITS[:0:-1]):
        got = swap(send, "band", bit)
        got, grad_fine = meanwhile(got, pair, grad_fine)
        keep, send = halve(keep, got)
    got = swap(send, "band", MESH_BITS[0])
    got, grad_fine = meanwhile(got, 4, grad_fine)
    even, odd = settle(keep, got)
    got = swap(odd, "group", 1)
    got, grad_fine = meanwhile(got, 5, grad_fine)
    last = swap(jnp.concatenate([even[16:], got[16:]], axis=0), "group", 2)
    grad_owned = finish(here, even, got, last, cond_weight)
    return grad_fine, grad_owned


def solution(mesh):
    rows3 = P(BOTH, None, None)
    rows2 = P(BOTH, None)
    return jax.shard_map(
        body,
        mesh=mesh,
        in_specs=(rows3, rows3, rows2, P(), P(), rows3, rows3, rows3, rows2, P()),
        out_specs=(rows3, rows2),
        check_vma=False,
    )
```

```python
import functools

import jax
import jax.numpy as jnp
import numpy as np
from jax import lax
from jax.experimental import pallas as pl
from jax.experimental.pallas import tpu as pltpu
from jax.sharding import PartitionSpec as P

PW = 16
ROWS = 12
LON = 2048
PC = LON // PW
CH = 128
PAIRS = ROWS // 2
EXT = ROWS + 2
SLOTS = 2048
OWNERS = 128
BF = jnp.bfloat16
F32 = jnp.float32
MB = 1 << 20
BOTH = ("group", "band")


def dot(a, b):
    return jnp.dot(a, b, preferred_element_type=F32)


WHOLE = pl.BlockSpec(memory_space=pltpu.VMEM)


def params(mib):
    return pltpu.CompilerParams(vmem_limit_bytes=mib * MB)


ANYWHERE = pl.BlockSpec(memory_space=pl.ANY)
SCALARS = pl.BlockSpec(memory_space=pltpu.SMEM)
MESH_BITS = (4, 2, 16, 8, 1)


def block_of(other):
    place = 0
    for to, bit in enumerate(MESH_BITS):
        place += jnp.where((other & bit) != 0, 1 << to, 0)
    return place


def project_kernel(coarse, w_ref, out):
    out[...] = dot(coarse[...], w_ref[...]).astype(BF)


def project(coarse, cond_weight):
    return pl.pallas_call(
        project_kernel,
        in_specs=[WHOLE] * 2,
        out_specs=WHOLE,
        out_shape=jax.ShapeDtypeStruct((coarse.shape[0], CH), BF),
        compiler_params=params(4),
        name="project",
    )(coarse, cond_weight)


def rims_kernel(field, cot, head, tail, sems):
    copies = [
        pltpu.make_async_copy(field.at[pl.ds(0, 2)], head.at[pl.ds(0, 2)], sems.at[0]),
        pltpu.make_async_copy(cot.at[pl.ds(0, 1)], head.at[pl.ds(2, 1)], sems.at[1]),
        pltpu.make_async_copy(field.at[pl.ds(ROWS - 2, 2)], tail.at[pl.ds(0, 2)], sems.at[2]),
        pltpu.make_async_copy(cot.at[pl.ds(ROWS - 1, 1)], tail.at[pl.ds(2, 1)], sems.at[3]),
    ]
    for copy in copies:
        copy.start()
    for copy in copies:
        copy.wait()


def rims(field, cot):
    rim = jax.ShapeDtypeStruct((3, LON, CH), BF)
    return pl.pallas_call(
        rims_kernel,
        in_specs=[ANYWHERE] * 2,
        out_specs=[WHOLE] * 2,
        out_shape=[rim, rim],
        scratch_shapes=[pltpu.SemaphoreType.DMA((4,))],
        compiler_params=params(54),
        name="rims",
    )(field, cot)


def pack_kernel(w_ref, packed, back, w_back):
    zero = jnp.zeros((CH, CH), BF)
    left, right = slice(0, CH), slice(CH, 2 * CH)
    for kx in range(3):
        flipped = []
        for ky in range(3):
            turned = w_ref[2 - ky, 2 - kx].astype(F32).T.astype(BF)
            w_back[ky, kx * CH : (kx + 1) * CH, :] = turned
            flipped.append(turned)
        for r in range(4):
            rows = slice(r * CH, (r + 1) * CH)
            packed[kx, rows, left] = w_ref[r, kx] if r < 3 else zero
            packed[kx, rows, right] = w_ref[r - 1, kx] if r >= 1 else zero
            back[kx, rows, left] = flipped[r] if r < 3 else zero
            back[kx, rows, right] = flipped[r - 1] if r >= 1 else zero


def pack(conv_weight):
    both = jax.ShapeDtypeStruct((3, 4 * CH, 2 * CH), BF)
    return pl.pallas_call(
        pack_kernel,
        in_specs=[WHOLE],
        out_specs=[WHOLE] * 3,
        out_shape=[both, both, jax.ShapeDtypeStruct((3, 3 * CH, CH), BF)],
        compiler_params=params(4),
        name="pack",
    )(conv_weight)


def conv_pair(rows, w_ref, write):
    lhs = jnp.concatenate(rows, axis=1)
    left = dot(lhs, w_ref[0])
    right = dot(lhs, w_ref[2])
    place = lax.broadcasted_iota(jnp.int32, (LON, 1), 0)
    total = dot(lhs, w_ref[1])
    total += jnp.where(place == 0, 0.0, pltpu.roll(left, 1, 0))
    total += jnp.where(place == LON - 1, 0.0, pltpu.roll(right, LON - 1, 0))
    write(0, total[:, :CH])
    write(1, total[:, CH:])


def conv_state_inner_kernel(start, *refs):
    field, w_ref, out = refs[0], refs[1], refs[-1]
    q = start + pl.program_id(0)

    def write(r, value):
        out[2 * q + r] = value

    conv_pair([field[2 * q - 2 + r] for r in range(4)], w_ref, write)


def conv_state_rim_kernel(field, w_ref, up, down, before, out):
    def write_to(at):
        def write(r, value):
            out[at + r] = value

        return write

    @pl.when(pl.program_id(0) == 0)
    def _():
        conv_pair([up[0], up[1], field[0], field[1]], w_ref, write_to(0))

    @pl.when(pl.program_id(0) == 1)
    def _():
        conv_pair([field[ROWS - 2], field[ROWS - 1], down[0], down[1]], w_ref, write_to(ROWS))


def conv_cost(pairs):
    return pl.CostEstimate(
        flops=4 * pairs * LON * 12 * CH * CH, bytes_accessed=pairs * LON * CH * 12, transcendentals=0
    )


PRE = pltpu.VMEM((EXT, LON, CH), F32)


def conv_state_inner(field, packed, start, count, before=None):
    args = (field, packed) if before is None else (field, packed, before)
    return pl.pallas_call(
        functools.partial(conv_state_inner_kernel, start),
        grid=(count,),
        in_specs=[WHOLE] * len(args),
        out_specs=WHOLE,
        out_shape=PRE,
        input_output_aliases={} if before is None else {2: 0},
        compiler_params=params(8),
        cost_estimate=conv_cost(count),
        name="conv_state",
    )(*args)


def conv_state_rim(field, packed, up, down, before):
    return pl.pallas_call(
        conv_state_rim_kernel,
        grid=(2,),
        in_specs=[WHOLE] * 5,
        out_specs=WHOLE,
        out_shape=PRE,
        input_output_aliases={4: 0},
        compiler_params=params(8),
        cost_estimate=conv_cost(2),
        name="conv_state_rim",
    )(field, packed, up, down, before)


def conv_grad_kernel(start, *refs):
    field, w_ref, cot, out = refs[0], refs[1], refs[2], refs[-1]
    p = start + pl.program_id(0)

    def write(r, value):
        out[r] = (cot[2 * p + r].astype(F32) + value).astype(BF)

    conv_pair([field[2 * p + r] for r in range(4)], w_ref, write)


def conv_grad(field, packed, cotangent, start, count, before=None):
    args = [field, packed, cotangent] + ([] if before is None else [before])
    specs = [WHOLE] * 3 + ([] if before is None else [pl.BlockSpec(memory_space=pl.ANY)])
    return pl.pallas_call(
        functools.partial(conv_grad_kernel, start),
        grid=(count,),
        in_specs=specs,
        out_specs=pl.BlockSpec((2, LON, CH), lambda i: (start + i, 0, 0)),
        out_shape=jax.ShapeDtypeStruct((ROWS, LON, CH), BF),
        input_output_aliases={} if before is None else {3: 0},
        compiler_params=params(8),
        cost_estimate=conv_cost(count),
        name="conv_grad",
    )(*args)


SC_CHUNK = 512


def onehot(height, index_row):
    place = lax.broadcasted_iota(jnp.int32, (height, index_row.shape[1]), 0)
    return jnp.where(place == index_row, 1.0, 0.0).astype(BF)


def contract0(a, b):
    return lax.dot_general(a, b, (((0,), (0,)), ((), ())), preferred_element_type=F32)


def contract1(a, b):
    return lax.dot_general(a, b, (((1,), (1,)), ((), ())), preferred_element_type=F32)


def slot_row(ref, first):
    return jnp.concatenate([ref[first + k : first + k + 1, :] for k in range(SC_CHUNK // OWNERS)], axis=1)


def live_weight(weight, count):
    slot = lax.broadcasted_iota(jnp.int32, weight.shape, 0)
    return jnp.where(slot < count[...], weight[...], 0.0)


def spread_kernel(here, near, far, perm, patch, target, weight, count, kept, out, kept_on, source, live):
    live[...] = live_weight(weight, count)
    row = jnp.zeros(target.shape, jnp.int32)
    for t in range(16):
        row += jnp.where(target[...] == t, perm[t : t + 1, :], 0)
    source[...] = block_of((row >> 6) ^ here[1]) * 64 + (row & 63)
    patches = ROWS * PC
    panel = jnp.concatenate([near[...], far[...]], axis=0)
    total = jnp.zeros((patches, CH), F32)
    for first in range(0, 16, SC_CHUNK // OWNERS):
        picked = contract0(panel, onehot(SLOTS, slot_row(source, first)))
        picked = (picked * slot_row(live, first)).astype(BF)
        total += contract1(onehot(patches, slot_row(patch, first)), picked)
    out[...] = total.astype(BF)


def spread(here, near, far, perm, patch, target, weight, count, kept):
    return pl.pallas_call(
        spread_kernel,
        in_specs=[SCALARS] + [WHOLE] * 8,
        out_specs=[WHOLE, WHOLE],
        out_shape=[jax.ShapeDtypeStruct((ROWS * PC, CH), BF), PRE],
        input_output_aliases={8: 1},
        scratch_shapes=[pltpu.VMEM((16, OWNERS), jnp.int32), pltpu.VMEM((16, OWNERS), F32)],
        compiler_params=params(12),
        cost_estimate=pl.CostEstimate(flops=4 * 2048 * 2048 * 128, bytes_accessed=MB, transcendentals=0),
        name="spread",
    )(here, near, far, perm, patch, target, weight, count, kept)


EX_CELLS = 1024
RD_CELLS = 256


def patch_marks(count):
    cells = np.arange(count)[:, None]
    inside = cells // PW == np.arange(count // PW)[None, :]
    marks = [inside, inside & (cells % PW == 0), inside & (cells % PW == PW - 1)]
    return np.concatenate(marks, axis=1).astype(np.float32)


def shift_patch(value, step):
    place = lax.broadcasted_iota(jnp.int32, (PC, 1), 0)
    if step > 0:
        return jnp.where(place == 0, 0.0, pltpu.roll(value, 1, 0))
    return jnp.where(place == PC - 1, 0.0, pltpu.roll(value, PC - 1, 0))


def silu_kernel(pre, cot, up, down, cond, c_up, c_down, w_ref, ex_ref, rd_ref, out, sums):
    q = pl.program_id(0)
    above = jnp.where(q == 0, c_up[...], cond[jnp.maximum(q - 1, 0)])
    below = jnp.where(q == PAIRS, c_down[...], cond[jnp.minimum(q, PAIRS - 1)])
    lhs = jnp.concatenate([above[:PC], above[PC:], below[:PC], below[PC:]], axis=1)
    west, here, east = [dot(lhs, w_ref[k]) for k in range(3)]
    inner = (west + here + east).astype(BF)
    at_first = (shift_patch(west, 1) - west).astype(BF)
    at_last = (shift_patch(east, -1) - east).astype(BF)
    per = EX_CELLS // PW
    part_sum, part_first, part_last = [], [], []
    for lo in range(0, LON, EX_CELLS):
        cells = slice(lo, lo + EX_CELLS)
        cut = slice(lo // PW, lo // PW + per)
        terms = jnp.concatenate([inner[cut], at_first[cut], at_last[cut]], axis=0)
        spread_terms = dot(ex_ref[...], terms)
        weights = [
            jnp.where(q == 0, up[2, cells], cot[jnp.maximum(2 * q - 1, 0), cells]),
            jnp.where(q == PAIRS, down[2, cells], cot[jnp.minimum(2 * q, ROWS - 1), cells]),
        ]
        grads = []
        for r in range(2):
            half = 0.5 * (pre[2 * q + r, cells] + spread_terms[:, r * CH : (r + 1) * CH])
            t = jnp.tanh(half)
            slope = (0.5 + 0.5 * t) * (1.0 + half * (1.0 - t))
            g = (weights[r].astype(F32) * slope).astype(BF)
            out[2 * q + r, cells] = g
            grads.append(g)
        grads = jnp.concatenate(grads, axis=1)
        for at in range(0, EX_CELLS, RD_CELLS):
            reduced = dot(rd_ref[...], grads[at : at + RD_CELLS])
            part_sum.append(reduced[:PW])
            part_first.append(reduced[PW : 2 * PW])
            part_last.append(reduced[2 * PW :])
    whole, firsts, lasts = [jnp.concatenate(p, axis=0) for p in (part_sum, part_first, part_last)]
    from_west = (whole - lasts + shift_patch(lasts, 1)).astype(BF)
    from_east = (whole - firsts + shift_patch(firsts, -1)).astype(BF)
    whole = whole.astype(BF)
    for r in range(2):
        cut = slice(r * CH, (r + 1) * CH)
        sums[2 * q + r] = jnp.concatenate([from_west[:, cut], whole[:, cut], from_east[:, cut]], axis=1)


def silu_grad(pre, cotangent, up, down, cond, c_up, c_down, packed):
    expand = jnp.asarray(patch_marks(EX_CELLS), BF)
    reduce_m = jnp.asarray(patch_marks(RD_CELLS).T, BF)
    cond = cond.reshape(PAIRS, 2 * PC, CH)
    return pl.pallas_call(
        silu_kernel,
        grid=(PAIRS + 1,),
        in_specs=[WHOLE] * 10,
        out_specs=[WHOLE, WHOLE],
        out_shape=[pltpu.VMEM((EXT, LON, CH), BF), pltpu.VMEM((EXT, PC, 3 * CH), BF)],
        compiler_params=params(8),
        cost_estimate=pl.CostEstimate(flops=10**9, bytes_accessed=8 * ROWS * LON * CH, transcendentals=0),
        name="silu_grad",
    )(pre, cotangent, up, down, cond, c_up, c_down, packed, expand, reduce_m)


def collect_kernel(here, sums, w_ref, patch, target, weight, count, keep, send, total, slots, shares, picked):
    patches = ROWS * PC
    grad_patch = dot(sums[:patches], w_ref[0])
    grad_patch += dot(sums[PC : PC + patches], w_ref[1])
    grad_patch += dot(sums[2 * PC :], w_ref[2])
    grad_patch = grad_patch.astype(BF)
    owner = lax.broadcasted_iota(jnp.int32, (OWNERS, OWNERS), 0)
    place = block_of((owner & 31) ^ here[1]) * 4 + ((owner >> 5) ^ here[0])
    order = jnp.where(place == lax.broadcasted_iota(jnp.int32, (OWNERS, OWNERS), 1), 1.0, 0.0)
    values = jnp.concatenate(
        [patch[...].astype(F32), target[...].astype(F32), live_weight(weight, count)], axis=0
    )
    values = jnp.dot(values, order, preferred_element_type=F32, precision=lax.Precision.HIGHEST)
    slots[...] = (values[:32] + 0.5).astype(jnp.int32)
    step = lax.broadcasted_iota(jnp.int32, (16, OWNERS), 0)
    for k in range(16):
        hit = step == slots[16 + k : 17 + k, :]
        shares[k] = jnp.where(hit, values[32 + k : 33 + k, :], 0.0)
    for first in range(0, 16, SC_CHUNK // OWNERS):
        got = contract0(grad_patch, onehot(patches, slot_row(slots, first)))
        for k in range(SC_CHUNK // OWNERS):
            picked[first + k] = got[:, k * OWNERS : (k + 1) * OWNERS]
    for t in range(16):
        mine = picked[0] * shares[0, t : t + 1, :]
        for k in range(1, 16):
            mine += picked[k] * shares[k, t : t + 1, :]
        total[pl.ds(t, OWNERS, stride=16), :] = mine.T
    keep[...] = total[: SLOTS // 2]
    send[...] = total[SLOTS // 2 :].astype(BF)


def collect(here, sums, w, patch, target, weight, count):
    return pl.pallas_call(
        collect_kernel,
        in_specs=[SCALARS] + [WHOLE] * 6,
        out_specs=[WHOLE, WHOLE],
        out_shape=[
            jax.ShapeDtypeStruct((SLOTS // 2, CH), F32),
            jax.ShapeDtypeStruct((SLOTS // 2, CH), BF),
        ],
        scratch_shapes=[
            pltpu.VMEM((SLOTS, CH), F32),
            pltpu.VMEM((32, OWNERS), jnp.int32),
            pltpu.VMEM((16, 16, OWNERS), F32),
            pltpu.VMEM((16, CH, OWNERS), F32),
        ],
        compiler_params=params(16),
        cost_estimate=pl.CostEstimate(flops=2 * 2048 * 2048 * 128, bytes_accessed=2 * MB, transcendentals=0),
        name="collect",
    )(here, sums.reshape(EXT * PC, 3 * CH), w, patch, target, weight, count)


def halve_kernel(kept, got, keep, send):
    half = keep.shape[0]
    total = kept[...] + got[...].astype(F32)
    keep[...] = total[:half]
    send[...] = total[half:].astype(BF)


def halve(kept, got):
    half = kept.shape[0] // 2
    return pl.pallas_call(
        halve_kernel,
        in_specs=[WHOLE] * 2,
        out_specs=[WHOLE, WHOLE],
        out_shape=[jax.ShapeDtypeStruct((half, CH), F32), jax.ShapeDtypeStruct((half, CH), BF)],
        compiler_params=params(4),
        name="halve",
    )(kept, got)


def settle_kernel(kept, got, even, odd):
    total = (kept[...] + got[...].astype(F32)).astype(BF)
    even[:16] = total[:16]
    even[16:] = total[32:48]
    odd[:16] = total[16:32]
    odd[16:] = total[48:]


def settle(kept, got):
    half = jax.ShapeDtypeStruct((32, CH), BF)
    return pl.pallas_call(
        settle_kernel,
        in_specs=[WHOLE] * 2,
        out_specs=[WHOLE, WHOLE],
        out_shape=[half, half],
        compiler_params=params(4),
        name="settle",
    )(kept, got)


def finish_kernel(here, even, got, last, w_ref, out):
    rows = jnp.concatenate([even[:16], got[:16], last[...]], axis=0)
    value = contract1(rows, w_ref[...])
    for k in range(4):
        to = pl.multiple_of((here[0] ^ k) * 16, 16)
        out[pl.ds(to, 16), :] = value[16 * k : 16 * k + 16]


def finish(here, even, got, last, cond_weight):
    return pl.pallas_call(
        finish_kernel,
        in_specs=[pl.BlockSpec(memory_space=pltpu.SMEM)] + [WHOLE] * 4,
        out_specs=WHOLE,
        out_shape=jax.ShapeDtypeStruct((64, cond_weight.shape[0]), F32),
        compiler_params=params(4),
        name="finish",
    )(here, even, got, last, cond_weight)


def from_neighbours(head, tail):
    count = lax.axis_size(BOTH)
    up = lax.ppermute(tail, BOTH, [(i, i + 1) for i in range(count - 1)])
    down = lax.ppermute(head, BOTH, [(i + 1, i) for i in range(count - 1)])
    return up, down


def swap(value, axis, bit):
    return lax.ppermute(value, axis, [(i, i ^ bit) for i in range(lax.axis_size(axis))])


def after(value, *earlier):
    return lax.optimization_barrier((value,) + earlier)[0]


def body(
    fine_state,
    cotangent,
    coarse,
    conv_weight,
    cond_weight,
    slot_patch,
    slot_target,
    slot_weight,
    block_count,
    panel_perm,
):
    group = lax.axis_index("group")
    band = lax.axis_index("band")
    here = jnp.stack([group, band]).astype(jnp.int32)
    perm = lax.dynamic_index_in_dim(panel_perm, group, 0, keepdims=False).reshape(-1, 16).T
    patch, target, weight = slot_patch[0].T, slot_target[0].T, slot_weight[0].T

    panel = project(coarse, cond_weight)
    first = swap(panel, "band", MESH_BITS[0])
    panel = jnp.concatenate([panel, first], axis=0)
    panel, here, perm = lax.optimization_barrier((panel, here, perm))
    head, tail = rims(after(fine_state, panel), cotangent)
    panel = jnp.concatenate([panel, swap(panel, "band", MESH_BITS[1])], axis=0)
    panel, head, tail = lax.optimization_barrier((panel, head, tail))
    packed, packed_back, w_back = pack(after(conv_weight, panel))
    field = after(fine_state, panel)
    panel = jnp.concatenate([panel, swap(panel, "band", MESH_BITS[2])], axis=0)
    pre = conv_state_inner(field, packed, 1, 1)
    panel, pre = lax.optimization_barrier((panel, pre))
    panel = jnp.concatenate([panel, swap(panel, "band", MESH_BITS[3])], axis=0)
    pre = conv_state_inner(field, packed, 2, 1, pre)
    panel, pre, head, tail = lax.optimization_barrier((panel, pre, head, tail))
    far = swap(panel, "band", MESH_BITS[4])
    up, down = from_neighbours(head, tail)
    cond, pre = spread(here, panel, far, perm, patch, target, weight, block_count, pre)
    cond_up, cond_down = from_neighbours(cond[: 2 * PC], cond[-2 * PC :])
    pre = conv_state_inner(field, packed, 3, 3, pre)
    pre = conv_state_rim(field, packed, up, down, pre)
    grad_pre, sums = silu_grad(pre, cotangent, up, down, cond, cond_up, cond_down, packed)

    keep, send = collect(here, sums, w_back, patch, target, weight, block_count)
    grad_fine = None

    def meanwhile(got, pair, grad_fine):
        grad_fine = conv_grad(after(grad_pre, keep), packed_back, cotangent, pair, 1, grad_fine)
        return lax.optimization_barrier((got, grad_fine))

    for pair, bit in enumerate(MESH_BITS[:0:-1]):
        got = swap(send, "band", bit)
        got, grad_fine = meanwhile(got, pair, grad_fine)
        keep, send = halve(keep, got)
    got = swap(send, "band", MESH_BITS[0])
    got, grad_fine = meanwhile(got, 4, grad_fine)
    even, odd = settle(keep, got)
    got = swap(odd, "group", 1)
    got, grad_fine = meanwhile(got, 5, grad_fine)
    last = swap(jnp.concatenate([even[16:], got[16:]], axis=0), "group", 2)
    grad_owned = finish(here, even, got, last, cond_weight)
    return grad_fine, grad_owned


def solution(mesh):
    rows3 = P(BOTH, None, None)
    rows2 = P(BOTH, None)
    return jax.shard_map(
        body,
        mesh=mesh,
        in_specs=(rows3, rows3, rows2, P(), P(), rows3, rows3, rows3, rows2, P()),
        out_specs=(rows3, rows2),
        check_vma=False,
    )
```

```python
import functools

import jax
import jax.numpy as jnp
import numpy as np
from jax import lax
from jax.experimental import pallas as pl
from jax.experimental.pallas import tpu as pltpu
from jax.sharding import PartitionSpec as P

PW = 16
ROWS = 12
LON = 2048
PC = LON // PW
CH = 128
PAIRS = ROWS // 2
EXT = ROWS + 2
SLOTS = 2048
OWNERS = 128
BF = jnp.bfloat16
F32 = jnp.float32
MB = 1 << 20
BOTH = ("group", "band")


def dot(a, b):
    return jnp.dot(a, b, preferred_element_type=F32)


WHOLE = pl.BlockSpec(memory_space=pltpu.VMEM)


def params(mib):
    return pltpu.CompilerParams(vmem_limit_bytes=mib * MB)


ANYWHERE = pl.BlockSpec(memory_space=pl.ANY)
SCALARS = pl.BlockSpec(memory_space=pltpu.SMEM)
MESH_BITS = (4, 2, 16, 8, 1)


def block_of(other):
    place = 0
    for to, bit in enumerate(MESH_BITS):
        place += jnp.where((other & bit) != 0, 1 << to, 0)
    return place


def project_kernel(coarse, w_ref, out):
    out[...] = dot(coarse[...], w_ref[...]).astype(BF)


def project(coarse, cond_weight):
    return pl.pallas_call(
        project_kernel,
        in_specs=[WHOLE] * 2,
        out_specs=WHOLE,
        out_shape=jax.ShapeDtypeStruct((coarse.shape[0], CH), BF),
        compiler_params=params(4),
        name="project",
    )(coarse, cond_weight)


def pack_kernel(w_ref, packed, back, w_back):
    zero = jnp.zeros((CH, CH), BF)
    left, right = slice(0, CH), slice(CH, 2 * CH)
    for kx in range(3):
        flipped = []
        for ky in range(3):
            turned = w_ref[2 - ky, 2 - kx].astype(F32).T.astype(BF)
            w_back[ky, kx * CH : (kx + 1) * CH, :] = turned
            flipped.append(turned)
        for r in range(4):
            rows = slice(r * CH, (r + 1) * CH)
            packed[kx, rows, left] = w_ref[r, kx] if r < 3 else zero
            packed[kx, rows, right] = w_ref[r - 1, kx] if r >= 1 else zero
            back[kx, rows, left] = flipped[r] if r < 3 else zero
            back[kx, rows, right] = flipped[r - 1] if r >= 1 else zero


def pack(conv_weight):
    both = jax.ShapeDtypeStruct((3, 4 * CH, 2 * CH), BF)
    return pl.pallas_call(
        pack_kernel,
        in_specs=[WHOLE],
        out_specs=[WHOLE] * 3,
        out_shape=[both, both, jax.ShapeDtypeStruct((3, 3 * CH, CH), BF)],
        compiler_params=params(4),
        name="pack",
    )(conv_weight)


def conv_pair(rows, w_ref, write):
    lhs = jnp.concatenate(rows, axis=1)
    left = dot(lhs, w_ref[0])
    right = dot(lhs, w_ref[2])
    place = lax.broadcasted_iota(jnp.int32, (LON, 1), 0)
    total = dot(lhs, w_ref[1])
    total += jnp.where(place == 0, 0.0, pltpu.roll(left, 1, 0))
    total += jnp.where(place == LON - 1, 0.0, pltpu.roll(right, LON - 1, 0))
    write(0, total[:, :CH])
    write(1, total[:, CH:])


def conv_state_inner_kernel(start, *refs):
    field, w_ref, out = refs[0], refs[1], refs[-1]
    q = start + pl.program_id(0)

    def write(r, value):
        out[2 * q + r] = value

    conv_pair([field[2 * q - 2 + r] for r in range(4)], w_ref, write)


def conv_state_rim_kernel(field, w_ref, up, down, before, out):
    def write_to(at):
        def write(r, value):
            out[at + r] = value

        return write

    @pl.when(pl.program_id(0) == 0)
    def _():
        conv_pair([up[:LON], up[LON : 2 * LON], field[0], field[1]], w_ref, write_to(0))

    @pl.when(pl.program_id(0) == 1)
    def _():
        conv_pair([field[ROWS - 2], field[ROWS - 1], down[:LON], down[LON : 2 * LON]], w_ref, write_to(ROWS))


def conv_cost(pairs):
    return pl.CostEstimate(
        flops=4 * pairs * LON * 12 * CH * CH, bytes_accessed=pairs * LON * CH * 12, transcendentals=0
    )


PRE = pltpu.VMEM((EXT, LON, CH), F32)


def conv_state_inner(field, packed, start, count, before=None):
    args = (field, packed) if before is None else (field, packed, before)
    return pl.pallas_call(
        functools.partial(conv_state_inner_kernel, start),
        grid=(count,),
        in_specs=[WHOLE] * len(args),
        out_specs=WHOLE,
        out_shape=PRE,
        input_output_aliases={} if before is None else {2: 0},
        compiler_params=params(8),
        cost_estimate=conv_cost(count),
        name="conv_state",
    )(*args)


def conv_state_rim(field, packed, up, down, before):
    return pl.pallas_call(
        conv_state_rim_kernel,
        grid=(2,),
        in_specs=[WHOLE] * 5,
        out_specs=WHOLE,
        out_shape=PRE,
        input_output_aliases={4: 0},
        compiler_params=params(8),
        cost_estimate=conv_cost(2),
        name="conv_state_rim",
    )(field, packed, up, down, before)


PART = 512


def conv_grad_kernel(p, *refs):
    field, w_ref, cot, out, held, sems = refs[0], refs[1], refs[2], refs[-3], refs[-2], refs[-1]
    copies = []
    for part, lo in enumerate(range(0, LON, PART)):
        begin, end = max(lo - 16, 0), min(lo + PART + 16, LON)
        size = end - begin
        lhs = jnp.concatenate([field[2 * p + r, begin:end] for r in range(4)], axis=1)
        place = lax.broadcasted_iota(jnp.int32, (size, 1), 0) + begin
        left = pltpu.roll(dot(lhs, w_ref[0]), 1, 0)
        right = pltpu.roll(dot(lhs, w_ref[2]), size - 1, 0)
        if lo == 0:
            left = jnp.where(place == 0, 0.0, left)
        if end == LON:
            right = jnp.where(place == LON - 1, 0.0, right)
        total = (dot(lhs, w_ref[1]) + left + right)[lo - begin : lo - begin + PART]
        for r in range(2):
            value = cot[2 * p + r, lo : lo + PART].astype(F32) + total[:, r * CH : (r + 1) * CH]
            held[r, lo : lo + PART] = value.astype(BF)
        copy = pltpu.make_async_copy(
            held.at[:, pl.ds(lo, PART)], out.at[pl.ds(2 * p, 2), pl.ds(lo, PART)], sems.at[part]
        )
        copy.start()
        copies.append(copy)
    for copy in copies:
        copy.wait()


def conv_grad(field, packed, cotangent, pair, before=None):
    args = [field, packed, cotangent] + ([] if before is None else [before])
    specs = [WHOLE] * 3 + ([] if before is None else [ANYWHERE])
    return pl.pallas_call(
        functools.partial(conv_grad_kernel, pair),
        in_specs=specs,
        out_specs=ANYWHERE,
        out_shape=jax.ShapeDtypeStruct((ROWS, LON, CH), BF),
        input_output_aliases={} if before is None else {3: 0},
        scratch_shapes=[pltpu.VMEM((2, LON, CH), BF), pltpu.SemaphoreType.DMA((LON // PART,))],
        compiler_params=params(8),
        cost_estimate=conv_cost(1),
        name="conv_grad",
    )(*args)


SC_CHUNK = 512


def onehot(height, index_row):
    place = lax.broadcasted_iota(jnp.int32, (height, index_row.shape[1]), 0)
    return jnp.where(place == index_row, 1.0, 0.0).astype(BF)


def contract0(a, b):
    return lax.dot_general(a, b, (((0,), (0,)), ((), ())), preferred_element_type=F32)


def contract1(a, b):
    return lax.dot_general(a, b, (((1,), (1,)), ((), ())), preferred_element_type=F32)


def slot_row(ref, first):
    return jnp.concatenate([ref[first + k : first + k + 1, :] for k in range(SC_CHUNK // OWNERS)], axis=1)


def live_weight(weight, count):
    slot = lax.broadcasted_iota(jnp.int32, weight.shape, 0)
    return jnp.where(slot < count[...], weight[...], 0.0)


RIM = 3 * LON + 2 * PC


def spread_kernel(
    here, near, far, perm, patch, target, weight, count, kept, field, cot, out, kept_on, head, tail, source, live, sems
):
    copies = []
    for to, (buffer, rows) in enumerate(((head, (0, 1, 0)), (tail, (ROWS - 2, ROWS - 1, ROWS - 1)))):
        for j, (array, row) in enumerate(zip((field, field, cot), rows)):
            copies.append(
                pltpu.make_async_copy(array.at[row], buffer.at[pl.ds(j * LON, LON)], sems.at[3 * to + j])
            )
    for copy in copies:
        copy.start()
    live[...] = live_weight(weight, count)
    row = jnp.zeros(target.shape, jnp.int32)
    for t in range(16):
        row += jnp.where(target[...] == t, perm[t : t + 1, :], 0)
    source[...] = block_of((row >> 6) ^ here[1]) * 64 + (row & 63)
    patches = ROWS * PC
    panel = jnp.concatenate([near[...], far[...]], axis=0)
    total = jnp.zeros((patches, CH), F32)
    for first in range(0, 16, SC_CHUNK // OWNERS):
        picked = contract0(panel, onehot(SLOTS, slot_row(source, first)))
        picked = (picked * slot_row(live, first)).astype(BF)
        total += contract1(onehot(patches, slot_row(patch, first)), picked)
    total = total.astype(BF)
    out[...] = total
    for copy in copies:
        copy.wait()
    head[3 * LON :] = total[: 2 * PC]
    tail[3 * LON :] = total[-2 * PC :]


def spread(here, near, far, perm, patch, target, weight, count, kept, field, cot):
    rim = pltpu.VMEM((RIM, CH), BF)
    return pl.pallas_call(
        spread_kernel,
        in_specs=[SCALARS] + [WHOLE] * 8 + [ANYWHERE] * 2,
        out_specs=[WHOLE] * 4,
        out_shape=[jax.ShapeDtypeStruct((ROWS * PC, CH), BF), PRE, rim, rim],
        input_output_aliases={8: 1},
        scratch_shapes=[
            pltpu.VMEM((16, OWNERS), jnp.int32),
            pltpu.VMEM((16, OWNERS), F32),
            pltpu.SemaphoreType.DMA((6,)),
        ],
        compiler_params=params(12),
        cost_estimate=pl.CostEstimate(flops=4 * 2048 * 2048 * 128, bytes_accessed=MB, transcendentals=0),
        name="spread",
    )(here, near, far, perm, patch, target, weight, count, kept, field, cot)


EX_CELLS = 1024
RD_CELLS = 256


def patch_marks(count):
    cells = np.arange(count)[:, None]
    inside = cells // PW == np.arange(count // PW)[None, :]
    marks = [inside, inside & (cells % PW == 0), inside & (cells % PW == PW - 1)]
    return np.concatenate(marks, axis=1).astype(np.float32)


def shift_patch(value, step):
    place = lax.broadcasted_iota(jnp.int32, (PC, 1), 0)
    if step > 0:
        return jnp.where(place == 0, 0.0, pltpu.roll(value, 1, 0))
    return jnp.where(place == PC - 1, 0.0, pltpu.roll(value, PC - 1, 0))


def silu_inner_kernel(pre, cot, cond, w_ref, ex_ref, rd_ref, out, sums):
    q = pl.program_id(0) + 1
    silu_pair(
        q, pre, cond[q - 1], cond[q], lambda cells: (cot[2 * q - 1, cells], cot[2 * q, cells]), w_ref, ex_ref, rd_ref, out, sums
    )


def silu_rim_kernel(pre, cot, cond, w_ref, ex_ref, rd_ref, up, down, before, before_sums, out, sums):
    @pl.when(pl.program_id(0) == 0)
    def _():
        def weights(cells):
            return up[2 * LON + cells.start : 2 * LON + cells.stop], cot[0, cells]

        silu_pair(0, pre, up[3 * LON :], cond[0], weights, w_ref, ex_ref, rd_ref, out, sums)

    @pl.when(pl.program_id(0) == 1)
    def _():
        def weights(cells):
            return cot[ROWS - 1, cells], down[2 * LON + cells.start : 2 * LON + cells.stop]

        silu_pair(PAIRS, pre, cond[PAIRS - 1], down[3 * LON :], weights, w_ref, ex_ref, rd_ref, out, sums)


def silu_pair(q, pre, above, below, cot_pair, w_ref, ex_ref, rd_ref, out, sums):
    lhs = jnp.concatenate([above[:PC], above[PC:], below[:PC], below[PC:]], axis=1)
    west, here, east = [dot(lhs, w_ref[k]) for k in range(3)]
    inner = (west + here + east).astype(BF)
    at_first = (shift_patch(west, 1) - west).astype(BF)
    at_last = (shift_patch(east, -1) - east).astype(BF)
    per = EX_CELLS // PW
    part_sum, part_first, part_last = [], [], []
    for lo in range(0, LON, EX_CELLS):
        cells = slice(lo, lo + EX_CELLS)
        cut = slice(lo // PW, lo // PW + per)
        terms = jnp.concatenate([inner[cut], at_first[cut], at_last[cut]], axis=0)
        spread_terms = dot(ex_ref[...], terms)
        weights = cot_pair(cells)
        grads = []
        for r in range(2):
            half = 0.5 * (pre[2 * q + r, cells] + spread_terms[:, r * CH : (r + 1) * CH])
            t = jnp.tanh(half)
            slope = (0.5 + 0.5 * t) * (1.0 + half * (1.0 - t))
            g = (weights[r].astype(F32) * slope).astype(BF)
            out[2 * q + r, cells] = g
            grads.append(g)
        grads = jnp.concatenate(grads, axis=1)
        for at in range(0, EX_CELLS, RD_CELLS):
            reduced = dot(rd_ref[...], grads[at : at + RD_CELLS])
            part_sum.append(reduced[:PW])
            part_first.append(reduced[PW : 2 * PW])
            part_last.append(reduced[2 * PW :])
    whole, firsts, lasts = [jnp.concatenate(p, axis=0) for p in (part_sum, part_first, part_last)]
    from_west = (whole - lasts + shift_patch(lasts, 1)).astype(BF)
    from_east = (whole - firsts + shift_patch(firsts, -1)).astype(BF)
    whole = whole.astype(BF)
    for r in range(2):
        cut = slice(r * CH, (r + 1) * CH)
        sums[2 * q + r] = jnp.concatenate([from_west[:, cut], whole[:, cut], from_east[:, cut]], axis=1)


def silu_grad(pre, cotangent, cond, packed, rims=None, before=None):
    expand = jnp.asarray(patch_marks(EX_CELLS), BF)
    reduce_m = jnp.asarray(patch_marks(RD_CELLS).T, BF)
    args = [pre, cotangent, cond.reshape(PAIRS, 2 * PC, CH), packed, expand, reduce_m]
    if rims is not None:
        args += [*rims, *before]
    return pl.pallas_call(
        silu_inner_kernel if rims is None else silu_rim_kernel,
        grid=(PAIRS - 1 if rims is None else 2,),
        in_specs=[WHOLE] * len(args),
        out_specs=[WHOLE, WHOLE],
        out_shape=[pltpu.VMEM((EXT, LON, CH), BF), pltpu.VMEM((EXT, PC, 3 * CH), BF)],
        input_output_aliases={} if rims is None else {8: 0, 9: 1},
        compiler_params=params(8),
        cost_estimate=pl.CostEstimate(flops=10**9, bytes_accessed=8 * ROWS * LON * CH, transcendentals=0),
        name="silu_grad",
    )(*args)


def collect_kernel(here, sums, w_ref, patch, target, weight, count, keep, send, total, slots, shares, picked):
    patches = ROWS * PC
    grad_patch = dot(sums[:patches], w_ref[0])
    grad_patch += dot(sums[PC : PC + patches], w_ref[1])
    grad_patch += dot(sums[2 * PC :], w_ref[2])
    grad_patch = grad_patch.astype(BF)
    owner = lax.broadcasted_iota(jnp.int32, (OWNERS, OWNERS), 0)
    place = block_of((owner & 31) ^ here[1]) * 4 + ((owner >> 5) ^ here[0])
    order = jnp.where(place == lax.broadcasted_iota(jnp.int32, (OWNERS, OWNERS), 1), 1.0, 0.0)
    values = jnp.concatenate(
        [patch[...].astype(F32), target[...].astype(F32), live_weight(weight, count)], axis=0
    )
    values = jnp.dot(values, order, preferred_element_type=F32, precision=lax.Precision.HIGHEST)
    slots[...] = (values[:32] + 0.5).astype(jnp.int32)
    step = lax.broadcasted_iota(jnp.int32, (16, OWNERS), 0)
    for k in range(16):
        hit = step == slots[16 + k : 17 + k, :]
        shares[k] = jnp.where(hit, values[32 + k : 33 + k, :], 0.0)
    for first in range(0, 16, SC_CHUNK // OWNERS):
        got = contract0(grad_patch, onehot(patches, slot_row(slots, first)))
        for k in range(SC_CHUNK // OWNERS):
            picked[first + k] = got[:, k * OWNERS : (k + 1) * OWNERS]
    for t in range(16):
        mine = picked[0] * shares[0, t : t + 1, :]
        for k in range(1, 16):
            mine += picked[k] * shares[k, t : t + 1, :]
        total[pl.ds(t, OWNERS, stride=16), :] = mine.T
    keep[...] = total[: SLOTS // 2]
    send[...] = total[SLOTS // 2 :].astype(BF)


def collect(here, sums, w, patch, target, weight, count):
    return pl.pallas_call(
        collect_kernel,
        in_specs=[SCALARS] + [WHOLE] * 6,
        out_specs=[WHOLE, WHOLE],
        out_shape=[
            jax.ShapeDtypeStruct((SLOTS // 2, CH), F32),
            jax.ShapeDtypeStruct((SLOTS // 2, CH), BF),
        ],
        scratch_shapes=[
            pltpu.VMEM((SLOTS, CH), F32),
            pltpu.VMEM((32, OWNERS), jnp.int32),
            pltpu.VMEM((16, 16, OWNERS), F32),
            pltpu.VMEM((16, CH, OWNERS), F32),
        ],
        compiler_params=params(16),
        cost_estimate=pl.CostEstimate(flops=2 * 2048 * 2048 * 128, bytes_accessed=2 * MB, transcendentals=0),
        name="collect",
    )(here, sums.reshape(EXT * PC, 3 * CH), w, patch, target, weight, count)


def halve_kernel(kept, got, keep, send):
    half = keep.shape[0]
    total = kept[...] + got[...].astype(F32)
    keep[...] = total[:half]
    send[...] = total[half:].astype(BF)


def halve(kept, got):
    half = kept.shape[0] // 2
    return pl.pallas_call(
        halve_kernel,
        in_specs=[WHOLE] * 2,
        out_specs=[WHOLE, WHOLE],
        out_shape=[jax.ShapeDtypeStruct((half, CH), F32), jax.ShapeDtypeStruct((half, CH), BF)],
        compiler_params=params(4),
        name="halve",
    )(kept, got)


def settle_kernel(kept, got, even, odd):
    total = (kept[...] + got[...].astype(F32)).astype(BF)
    even[:16] = total[:16]
    even[16:] = total[32:48]
    odd[:16] = total[16:32]
    odd[16:] = total[48:]


def settle(kept, got):
    half = jax.ShapeDtypeStruct((32, CH), BF)
    return pl.pallas_call(
        settle_kernel,
        in_specs=[WHOLE] * 2,
        out_specs=[WHOLE, WHOLE],
        out_shape=[half, half],
        compiler_params=params(4),
        name="settle",
    )(kept, got)


def finish_kernel(here, even, got, last, w_ref, out):
    rows = jnp.concatenate([even[:16], got[:16], last[...]], axis=0)
    value = contract1(rows, w_ref[...])
    for k in range(4):
        to = pl.multiple_of((here[0] ^ k) * 16, 16)
        out[pl.ds(to, 16), :] = value[16 * k : 16 * k + 16]


def finish(here, even, got, last, cond_weight):
    return pl.pallas_call(
        finish_kernel,
        in_specs=[pl.BlockSpec(memory_space=pltpu.SMEM)] + [WHOLE] * 4,
        out_specs=WHOLE,
        out_shape=jax.ShapeDtypeStruct((64, cond_weight.shape[0]), F32),
        compiler_params=params(4),
        name="finish",
    )(here, even, got, last, cond_weight)


def from_neighbours(head, tail):
    count = lax.axis_size(BOTH)
    up = lax.ppermute(tail, BOTH, [(i, i + 1) for i in range(count - 1)])
    down = lax.ppermute(head, BOTH, [(i + 1, i) for i in range(count - 1)])
    return up, down


def swap(value, axis, bit):
    return lax.ppermute(value, axis, [(i, i ^ bit) for i in range(lax.axis_size(axis))])


def after(value, *earlier):
    return lax.optimization_barrier((value,) + earlier)[0]


def body(
    fine_state,
    cotangent,
    coarse,
    conv_weight,
    cond_weight,
    slot_patch,
    slot_target,
    slot_weight,
    block_count,
    panel_perm,
):
    group = lax.axis_index("group")
    band = lax.axis_index("band")
    here = jnp.stack([group, band]).astype(jnp.int32)
    perm = lax.dynamic_index_in_dim(panel_perm, group, 0, keepdims=False).reshape(-1, 16).T
    patch, target, weight = slot_patch[0].T, slot_target[0].T, slot_weight[0].T

    panel = project(coarse, cond_weight)
    first = swap(panel, "band", MESH_BITS[0])
    panel = jnp.concatenate([panel, first], axis=0)
    panel, here, perm = lax.optimization_barrier((panel, here, perm))
    panel = jnp.concatenate([panel, swap(panel, "band", MESH_BITS[1])], axis=0)
    packed, packed_back, w_back = pack(after(conv_weight, panel))
    field = after(fine_state, panel)
    panel = jnp.concatenate([panel, swap(panel, "band", MESH_BITS[2])], axis=0)
    pre = conv_state_inner(field, packed, 1, 1)
    panel, pre = lax.optimization_barrier((panel, pre))
    panel = jnp.concatenate([panel, swap(panel, "band", MESH_BITS[3])], axis=0)
    pre = conv_state_inner(field, packed, 2, 1, pre)
    panel, pre = lax.optimization_barrier((panel, pre))
    far = swap(panel, "band", MESH_BITS[4])
    cond, pre, head, tail = spread(
        here, panel, far, perm, patch, target, weight, block_count, pre, field, cotangent
    )
    up, down = from_neighbours(head, tail)
    pre = conv_state_inner(field, packed, 3, 3, pre)
    grad_pre, sums = silu_grad(pre, cotangent, cond, packed)
    pre, grad_pre, sums = lax.optimization_barrier((pre, grad_pre, sums))
    pre = conv_state_rim(field, packed, up, down, pre)
    grad_pre, sums = silu_grad(pre, cotangent, cond, packed, (up, down), (grad_pre, sums))

    keep, send = collect(here, sums, w_back, patch, target, weight, block_count)
    grad_fine = None

    def meanwhile(got, pair, grad_fine):
        grad_fine = conv_grad(after(grad_pre, keep), packed_back, cotangent, pair, grad_fine)
        return lax.optimization_barrier((got, grad_fine))

    for pair, bit in enumerate(MESH_BITS[:0:-1]):
        got = swap(send, "band", bit)
        got, grad_fine = meanwhile(got, pair, grad_fine)
        keep, send = halve(keep, got)
    got = swap(send, "band", MESH_BITS[0])
    got, grad_fine = meanwhile(got, 4, grad_fine)
    even, odd = settle(keep, got)
    got = swap(odd, "group", 1)
    got, grad_fine = meanwhile(got, 5, grad_fine)
    last = swap(jnp.concatenate([even[16:], got[16:]], axis=0), "group", 2)
    grad_owned = finish(here, even, got, last, cond_weight)
    return grad_fine, grad_owned


def solution(mesh):
    rows3 = P(BOTH, None, None)
    rows2 = P(BOTH, None)
    return jax.shard_map(
        body,
        mesh=mesh,
        in_specs=(rows3, rows3, rows2, P(), P(), rows3, rows3, rows3, rows2, P()),
        out_specs=(rows3, rows2),
        check_vma=False,
    )
```

```python
import functools

import jax
import jax.numpy as jnp
import numpy as np
from jax import lax
from jax.experimental import pallas as pl
from jax.experimental.pallas import tpu as pltpu
from jax.sharding import PartitionSpec as P

PW = 16
ROWS = 12
LON = 2048
PC = LON // PW
CH = 128
PAIRS = ROWS // 2
EXT = ROWS + 2
SLOTS = 2048
OWNERS = 128
BF = jnp.bfloat16
F32 = jnp.float32
MB = 1 << 20
BOTH = ("group", "band")


def dot(a, b):
    return jnp.dot(a, b, preferred_element_type=F32)


WHOLE = pl.BlockSpec(memory_space=pltpu.VMEM)


def params(mib):
    return pltpu.CompilerParams(vmem_limit_bytes=mib * MB)


ANYWHERE = pl.BlockSpec(memory_space=pl.ANY)
SCALARS = pl.BlockSpec(memory_space=pltpu.SMEM)
MESH_BITS = (4, 2, 16, 8, 1)


def block_of(other):
    place = 0
    for to, bit in enumerate(MESH_BITS):
        place += jnp.where((other & bit) != 0, 1 << to, 0)
    return place


CHIPS = 16


def project_kernel(coarse, w_ref, out):
    rows = coarse.shape[0]
    value = dot(coarse[...], w_ref[...]).astype(BF)
    for chip in range(CHIPS):
        out[chip * rows : (chip + 1) * rows] = value


def project(coarse, cond_weight):
    return pl.pallas_call(
        project_kernel,
        in_specs=[WHOLE] * 2,
        out_specs=WHOLE,
        out_shape=jax.ShapeDtypeStruct((CHIPS * coarse.shape[0], CH), BF),
        compiler_params=params(4),
        name="project",
    )(coarse, cond_weight)


def pack_kernel(w_ref, packed, back, w_back):
    zero = jnp.zeros((CH, CH), BF)
    left, right = slice(0, CH), slice(CH, 2 * CH)
    for kx in range(3):
        flipped = []
        for ky in range(3):
            turned = w_ref[2 - ky, 2 - kx].astype(F32).T.astype(BF)
            w_back[ky, kx * CH : (kx + 1) * CH, :] = turned
            flipped.append(turned)
        for r in range(4):
            rows = slice(r * CH, (r + 1) * CH)
            packed[kx, rows, left] = w_ref[r, kx] if r < 3 else zero
            packed[kx, rows, right] = w_ref[r - 1, kx] if r >= 1 else zero
            back[kx, rows, left] = flipped[r] if r < 3 else zero
            back[kx, rows, right] = flipped[r - 1] if r >= 1 else zero


def pack(conv_weight):
    both = jax.ShapeDtypeStruct((3, 4 * CH, 2 * CH), BF)
    return pl.pallas_call(
        pack_kernel,
        in_specs=[WHOLE],
        out_specs=[WHOLE] * 3,
        out_shape=[both, both, jax.ShapeDtypeStruct((3, 3 * CH, CH), BF)],
        compiler_params=params(4),
        name="pack",
    )(conv_weight)


def conv_pair(rows, w_ref, write):
    lhs = jnp.concatenate(rows, axis=1)
    left = dot(lhs, w_ref[0])
    right = dot(lhs, w_ref[2])
    place = lax.broadcasted_iota(jnp.int32, (LON, 1), 0)
    total = dot(lhs, w_ref[1])
    total += jnp.where(place == 0, 0.0, pltpu.roll(left, 1, 0))
    total += jnp.where(place == LON - 1, 0.0, pltpu.roll(right, LON - 1, 0))
    write(0, total[:, :CH])
    write(1, total[:, CH:])


def conv_state_inner_kernel(start, *refs):
    field, w_ref, out = refs[0], refs[1], refs[-1]
    q = start + pl.program_id(0)

    def write(r, value):
        out[2 * q - 2 + r] = value

    conv_pair([field[2 * q - 2 + r] for r in range(4)], w_ref, write)


def conv_state_rim_kernel(w_ref, up, down, head, tail, out):
    def conv_at(at, above, below):
        def write(r, value):
            out[at + r] = value

        conv_pair([above[:LON], above[LON : 2 * LON], below[:LON], below[LON : 2 * LON]], w_ref, write)

    @pl.when(pl.program_id(0) == 0)
    def _():
        conv_at(0, up, head)

    @pl.when(pl.program_id(0) == 1)
    def _():
        conv_at(2, tail, down)


def conv_cost(pairs):
    return pl.CostEstimate(
        flops=4 * pairs * LON * 12 * CH * CH, bytes_accessed=pairs * LON * CH * 12, transcendentals=0
    )


PRE = pltpu.VMEM((EXT - 4, LON, CH), F32)
PRE_RIM = pltpu.VMEM((4, LON, CH), F32)


def conv_state_inner(field, packed, start, count, before=None):
    args = (field, packed) if before is None else (field, packed, before)
    return pl.pallas_call(
        functools.partial(conv_state_inner_kernel, start),
        grid=(count,),
        in_specs=[WHOLE] * len(args),
        out_specs=WHOLE,
        out_shape=PRE,
        input_output_aliases={} if before is None else {2: 0},
        compiler_params=params(8),
        cost_estimate=conv_cost(count),
        name="conv_state",
    )(*args)


def conv_state_rim(packed, rims):
    return pl.pallas_call(
        conv_state_rim_kernel,
        grid=(2,),
        in_specs=[WHOLE] * 5,
        out_specs=WHOLE,
        out_shape=PRE_RIM,
        compiler_params=params(8),
        cost_estimate=conv_cost(2),
        name="conv_state_rim",
    )(packed, *rims)


PART = 512


def conv_grad_kernel(p, *refs):
    field, w_ref, cot, out, held, sems = refs[0], refs[1], refs[2], refs[-3], refs[-2], refs[-1]
    copies = []
    for part, lo in enumerate(range(0, LON, PART)):
        begin, end = max(lo - 16, 0), min(lo + PART + 16, LON)
        size = end - begin
        lhs = jnp.concatenate([field[2 * p + r, begin:end] for r in range(4)], axis=1)
        place = lax.broadcasted_iota(jnp.int32, (size, 1), 0) + begin
        left = pltpu.roll(dot(lhs, w_ref[0]), 1, 0)
        right = pltpu.roll(dot(lhs, w_ref[2]), size - 1, 0)
        if lo == 0:
            left = jnp.where(place == 0, 0.0, left)
        if end == LON:
            right = jnp.where(place == LON - 1, 0.0, right)
        total = (dot(lhs, w_ref[1]) + left + right)[lo - begin : lo - begin + PART]
        for r in range(2):
            value = cot[2 * p + r, lo : lo + PART].astype(F32) + total[:, r * CH : (r + 1) * CH]
            held[r, lo : lo + PART] = value.astype(BF)
        copy = pltpu.make_async_copy(
            held.at[:, pl.ds(lo, PART)], out.at[pl.ds(2 * p, 2), pl.ds(lo, PART)], sems.at[part]
        )
        copy.start()
        copies.append(copy)
    for copy in copies:
        copy.wait()


def conv_grad(field, packed, cotangent, pair, before=None):
    args = [field, packed, cotangent] + ([] if before is None else [before])
    specs = [WHOLE] * 3 + ([] if before is None else [ANYWHERE])
    return pl.pallas_call(
        functools.partial(conv_grad_kernel, pair),
        in_specs=specs,
        out_specs=ANYWHERE,
        out_shape=jax.ShapeDtypeStruct((ROWS, LON, CH), BF),
        input_output_aliases={} if before is None else {3: 0},
        scratch_shapes=[pltpu.VMEM((2, LON, CH), BF), pltpu.SemaphoreType.DMA((LON // PART,))],
        compiler_params=params(8),
        cost_estimate=conv_cost(1),
        name="conv_grad",
    )(*args)


SC_CHUNK = 512


def onehot(height, index_row):
    place = lax.broadcasted_iota(jnp.int32, (height, index_row.shape[1]), 0)
    return jnp.where(place == index_row, 1.0, 0.0).astype(BF)


def contract0(a, b):
    return lax.dot_general(a, b, (((0,), (0,)), ((), ())), preferred_element_type=F32)


def contract1(a, b):
    return lax.dot_general(a, b, (((1,), (1,)), ((), ())), preferred_element_type=F32)


def slot_row(ref, first):
    return jnp.concatenate([ref[first + k : first + k + 1, :] for k in range(SC_CHUNK // OWNERS)], axis=1)


def live_weight(weight, count):
    slot = lax.broadcasted_iota(jnp.int32, weight.shape, 0)
    return jnp.where(slot < count[...], weight[...], 0.0)


RIM = 3 * LON + 2 * PC


def spread_kernel(
    here,
    near,
    far,
    perm,
    patch,
    target,
    weight,
    count,
    fine_head,
    fine_tail,
    cot_head,
    cot_tail,
    out,
    head,
    tail,
    source,
    live,
    sems,
):
    copies = []
    for to, (buffer, rows) in enumerate(((head, (fine_head, cot_head)), (tail, (fine_tail, cot_tail)))):
        for j, row in enumerate((rows[0].at[0], rows[0].at[1], rows[1].at[0])):
            copies.append(
                pltpu.make_async_copy(row, buffer.at[pl.ds(j * LON, LON)], sems.at[3 * to + j])
            )
    for copy in copies:
        copy.start()
    live[...] = live_weight(weight, count)
    row = jnp.zeros(target.shape, jnp.int32)
    for t in range(16):
        row += jnp.where(target[...] == t, perm[t : t + 1, :], 0)
    source[...] = (row >> 7) * 64 + (row & 63) + jnp.where(((row >> 6) & 1) == (here[1] & 1), 0, SLOTS // 2)
    patches = ROWS * PC
    panel = jnp.concatenate([near[...], far[...]], axis=0)
    total = jnp.zeros((patches, CH), F32)
    for first in range(0, 16, SC_CHUNK // OWNERS):
        picked = contract0(panel, onehot(SLOTS, slot_row(source, first)))
        picked = (picked * slot_row(live, first)).astype(BF)
        total += contract1(onehot(patches, slot_row(patch, first)), picked)
    total = total.astype(BF)
    out[...] = total
    for copy in copies:
        copy.wait()
    head[3 * LON :] = total[: 2 * PC]
    tail[3 * LON :] = total[-2 * PC :]


def spread(here, near, far, perm, patch, target, weight, count, rims):
    rim = pltpu.VMEM((RIM, CH), BF)
    return pl.pallas_call(
        spread_kernel,
        in_specs=[SCALARS] + [WHOLE] * 7 + [ANYWHERE] * 4,
        out_specs=[WHOLE] * 3,
        out_shape=[jax.ShapeDtypeStruct((ROWS * PC, CH), BF), rim, rim],
        scratch_shapes=[
            pltpu.VMEM((16, OWNERS), jnp.int32),
            pltpu.VMEM((16, OWNERS), F32),
            pltpu.SemaphoreType.DMA((6,)),
        ],
        compiler_params=params(12),
        cost_estimate=pl.CostEstimate(flops=4 * 2048 * 2048 * 128, bytes_accessed=MB, transcendentals=0),
        name="spread",
    )(here, near, far, perm, patch, target, weight, count, *rims)


EX_CELLS = 1024
RD_CELLS = 256


def patch_marks(count):
    cells = np.arange(count)[:, None]
    inside = cells // PW == np.arange(count // PW)[None, :]
    marks = [inside, inside & (cells % PW == 0), inside & (cells % PW == PW - 1)]
    return np.concatenate(marks, axis=1).astype(np.float32)


def shift_patch(value, step):
    place = lax.broadcasted_iota(jnp.int32, (PC, 1), 0)
    if step > 0:
        return jnp.where(place == 0, 0.0, pltpu.roll(value, 1, 0))
    return jnp.where(place == PC - 1, 0.0, pltpu.roll(value, PC - 1, 0))


def silu_inner_kernel(pre, cond, w_ref, ex_ref, rd_ref, cot, out, sums):
    q = pl.program_id(0) + 1
    silu_pair(
        q, pre, 2 * q - 2, cond[q - 1], cond[q], lambda cells: (cot[2 * q - 1, cells], cot[2 * q, cells]), w_ref, ex_ref, rd_ref, out, sums
    )


def silu_rim_kernel(pre, cond, w_ref, ex_ref, rd_ref, up, down, head, tail, before, before_sums, out, sums):
    def weights_of(first, second):
        def weights(cells):
            rows = slice(2 * LON + cells.start, 2 * LON + cells.stop)
            return first[rows], second[rows]

        return weights

    @pl.when(pl.program_id(0) == 0)
    def _():
        silu_pair(0, pre, 0, up[3 * LON :], cond[0], weights_of(up, head), w_ref, ex_ref, rd_ref, out, sums)

    @pl.when(pl.program_id(0) == 1)
    def _():
        weights, below = weights_of(tail, down), down[3 * LON :]
        silu_pair(PAIRS, pre, 2, cond[PAIRS - 1], below, weights, w_ref, ex_ref, rd_ref, out, sums)


def silu_pair(q, pre, at, above, below, cot_pair, w_ref, ex_ref, rd_ref, out, sums):
    lhs = jnp.concatenate([above[:PC], above[PC:], below[:PC], below[PC:]], axis=1)
    west, here, east = [dot(lhs, w_ref[k]) for k in range(3)]
    inner = (west + here + east).astype(BF)
    at_first = (shift_patch(west, 1) - west).astype(BF)
    at_last = (shift_patch(east, -1) - east).astype(BF)
    per = EX_CELLS // PW
    part_sum, part_first, part_last = [], [], []
    for lo in range(0, LON, EX_CELLS):
        cells = slice(lo, lo + EX_CELLS)
        cut = slice(lo // PW, lo // PW + per)
        terms = jnp.concatenate([inner[cut], at_first[cut], at_last[cut]], axis=0)
        spread_terms = dot(ex_ref[...], terms)
        weights = cot_pair(cells)
        grads = []
        for r in range(2):
            half = 0.5 * (pre[at + r, cells] + spread_terms[:, r * CH : (r + 1) * CH])
            t = jnp.tanh(half)
            slope = (0.5 + 0.5 * t) * (1.0 + half * (1.0 - t))
            g = (weights[r].astype(F32) * slope).astype(BF)
            out[2 * q + r, cells] = g
            grads.append(g)
        grads = jnp.concatenate(grads, axis=1)
        for first in range(0, EX_CELLS, RD_CELLS):
            reduced = dot(rd_ref[...], grads[first : first + RD_CELLS])
            part_sum.append(reduced[:PW])
            part_first.append(reduced[PW : 2 * PW])
            part_last.append(reduced[2 * PW :])
    whole, firsts, lasts = [jnp.concatenate(p, axis=0) for p in (part_sum, part_first, part_last)]
    from_west = (whole - lasts + shift_patch(lasts, 1)).astype(BF)
    from_east = (whole - firsts + shift_patch(firsts, -1)).astype(BF)
    whole = whole.astype(BF)
    for r in range(2):
        cut = slice(r * CH, (r + 1) * CH)
        sums[2 * q + r] = jnp.concatenate([from_west[:, cut], whole[:, cut], from_east[:, cut]], axis=1)


def silu_grad(pre, cotangent, cond, packed, rims=None, before=None):
    expand = jnp.asarray(patch_marks(EX_CELLS), BF)
    reduce_m = jnp.asarray(patch_marks(RD_CELLS).T, BF)
    inner = rims is None
    args = [pre, cond.reshape(PAIRS, 2 * PC, CH), packed, expand, reduce_m]
    args += [cotangent] if inner else [*rims, *before]
    return pl.pallas_call(
        silu_inner_kernel if inner else silu_rim_kernel,
        grid=(PAIRS - 1 if inner else 2,),
        in_specs=[WHOLE] * len(args),
        out_specs=[WHOLE, WHOLE],
        out_shape=[pltpu.VMEM((EXT, LON, CH), BF), pltpu.VMEM((EXT, PC, 3 * CH), BF)],
        input_output_aliases={} if inner else {9: 0, 10: 1},
        compiler_params=params(8),
        cost_estimate=pl.CostEstimate(flops=10**9, bytes_accessed=8 * ROWS * LON * CH, transcendentals=0),
        name="silu_grad",
    )(*args)


def collect_kernel(here, sums, w_ref, patch, target, weight, count, keep, send, total, slots, shares, picked):
    patches = ROWS * PC
    grad_patch = dot(sums[:patches], w_ref[0])
    grad_patch += dot(sums[PC : PC + patches], w_ref[1])
    grad_patch += dot(sums[2 * PC :], w_ref[2])
    grad_patch = grad_patch.astype(BF)
    owner = lax.broadcasted_iota(jnp.int32, (OWNERS, OWNERS), 0)
    place = block_of((owner & 31) ^ here[1]) * 4 + ((owner >> 5) ^ here[0])
    order = jnp.where(place == lax.broadcasted_iota(jnp.int32, (OWNERS, OWNERS), 1), 1.0, 0.0)
    values = jnp.concatenate(
        [patch[...].astype(F32), target[...].astype(F32), live_weight(weight, count)], axis=0
    )
    values = jnp.dot(values, order, preferred_element_type=F32, precision=lax.Precision.HIGHEST)
    slots[...] = (values[:32] + 0.5).astype(jnp.int32)
    step = lax.broadcasted_iota(jnp.int32, (16, OWNERS), 0)
    for k in range(16):
        hit = step == slots[16 + k : 17 + k, :]
        shares[k] = jnp.where(hit, values[32 + k : 33 + k, :], 0.0)
    for first in range(0, 16, SC_CHUNK // OWNERS):
        got = contract0(grad_patch, onehot(patches, slot_row(slots, first)))
        for k in range(SC_CHUNK // OWNERS):
            picked[first + k] = got[:, k * OWNERS : (k + 1) * OWNERS]
    for t in range(16):
        mine = picked[0] * shares[0, t : t + 1, :]
        for k in range(1, 16):
            mine += picked[k] * shares[k, t : t + 1, :]
        total[pl.ds(t, OWNERS, stride=16), :] = mine.T
    keep[...] = total[: SLOTS // 2]
    send[...] = total[SLOTS // 2 :].astype(BF)


def collect(here, sums, w, patch, target, weight, count):
    return pl.pallas_call(
        collect_kernel,
        in_specs=[SCALARS] + [WHOLE] * 6,
        out_specs=[WHOLE, WHOLE],
        out_shape=[
            jax.ShapeDtypeStruct((SLOTS // 2, CH), F32),
            jax.ShapeDtypeStruct((SLOTS // 2, CH), BF),
        ],
        scratch_shapes=[
            pltpu.VMEM((SLOTS, CH), F32),
            pltpu.VMEM((32, OWNERS), jnp.int32),
            pltpu.VMEM((16, 16, OWNERS), F32),
            pltpu.VMEM((16, CH, OWNERS), F32),
        ],
        compiler_params=params(16),
        cost_estimate=pl.CostEstimate(flops=2 * 2048 * 2048 * 128, bytes_accessed=2 * MB, transcendentals=0),
        name="collect",
    )(here, sums.reshape(EXT * PC, 3 * CH), w, patch, target, weight, count)


def halve_kernel(kept, got, keep, send):
    half = keep.shape[0]
    total = kept[...] + got[...].astype(F32)
    keep[...] = total[:half]
    send[...] = total[half:].astype(BF)


def halve(kept, got):
    half = kept.shape[0] // 2
    return pl.pallas_call(
        halve_kernel,
        in_specs=[WHOLE] * 2,
        out_specs=[WHOLE, WHOLE],
        out_shape=[jax.ShapeDtypeStruct((half, CH), F32), jax.ShapeDtypeStruct((half, CH), BF)],
        compiler_params=params(4),
        name="halve",
    )(kept, got)


def settle_kernel(kept, got, even, odd):
    total = (kept[...] + got[...].astype(F32)).astype(BF)
    even[:16] = total[:16]
    even[16:] = total[32:48]
    odd[:16] = total[16:32]
    odd[16:] = total[48:]


def settle(kept, got):
    half = jax.ShapeDtypeStruct((32, CH), BF)
    return pl.pallas_call(
        settle_kernel,
        in_specs=[WHOLE] * 2,
        out_specs=[WHOLE, WHOLE],
        out_shape=[half, half],
        compiler_params=params(4),
        name="settle",
    )(kept, got)


def finish_kernel(here, even, got, last, w_ref, out):
    rows = jnp.concatenate([even[:16], got[:16], last[...]], axis=0)
    value = contract1(rows, w_ref[...])
    for k in range(4):
        to = pl.multiple_of((here[0] ^ k) * 16, 16)
        out[pl.ds(to, 16), :] = value[16 * k : 16 * k + 16]


def finish(here, even, got, last, cond_weight):
    return pl.pallas_call(
        finish_kernel,
        in_specs=[pl.BlockSpec(memory_space=pltpu.SMEM)] + [WHOLE] * 4,
        out_specs=WHOLE,
        out_shape=jax.ShapeDtypeStruct((64, cond_weight.shape[0]), F32),
        compiler_params=params(4),
        name="finish",
    )(here, even, got, last, cond_weight)


def from_neighbours(head, tail):
    count = lax.axis_size(BOTH)
    up = lax.ppermute(tail, BOTH, [(i, i + 1) for i in range(count - 1)])
    down = lax.ppermute(head, BOTH, [(i + 1, i) for i in range(count - 1)])
    return up, down


def swap(value, axis, bit):
    return lax.ppermute(value, axis, [(i, i ^ bit) for i in range(lax.axis_size(axis))])


def after(value, *earlier):
    return lax.optimization_barrier((value,) + earlier)[0]


def body(
    fine_state,
    cotangent,
    coarse,
    conv_weight,
    cond_weight,
    slot_patch,
    slot_target,
    slot_weight,
    block_count,
    panel_perm,
):
    group = lax.axis_index("group")
    band = lax.axis_index("band")
    here = jnp.stack([group, band]).astype(jnp.int32)
    perm = lax.dynamic_index_in_dim(panel_perm, group, 0, keepdims=False).reshape(-1, 16).T
    patch, target, weight = slot_patch[0].T, slot_target[0].T, slot_weight[0].T

    same_core = [[2 * chip + core for chip in range(CHIPS)] for core in range(2)]
    near = lax.all_to_all(
        project(coarse, cond_weight), "band", 0, 0, axis_index_groups=same_core, tiled=True
    )
    far = swap(near, "band", 1)
    field, cot = fine_state, cotangent
    _, here, perm, weights, field, cot = lax.optimization_barrier((near, here, perm, conv_weight, field, cot))
    packed, packed_back, w_back = pack(weights)
    cut = (field[:2], field[-2:], cot[:1], cot[-1:])
    far, here, perm, packed, cut = lax.optimization_barrier((far, here, perm, packed, cut))
    cond, head, tail = spread(here, near, far, perm, patch, target, weight, block_count, cut)
    up, down = from_neighbours(head, tail)
    pre = conv_state_inner(after(fine_state, far), packed, 1, 5)
    grad_pre, sums = silu_grad(pre, cotangent, cond, packed)
    grad_pre, sums, up, down = lax.optimization_barrier((grad_pre, sums, up, down))
    rims = (up, down, head, tail)
    pre = conv_state_rim(packed, rims)
    grad_pre, sums = silu_grad(pre, cotangent, cond, packed, rims, (grad_pre, sums))

    keep, send = collect(here, sums, w_back, patch, target, weight, block_count)
    grad_fine = None

    def meanwhile(got, pair, grad_fine):
        grad_fine = conv_grad(after(grad_pre, keep), packed_back, cotangent, pair, grad_fine)
        return lax.optimization_barrier((got, grad_fine))

    for pair, bit in enumerate(MESH_BITS[:0:-1]):
        got = swap(send, "band", bit)
        got, grad_fine = meanwhile(got, pair, grad_fine)
        keep, send = halve(keep, got)
    got = swap(send, "band", MESH_BITS[0])
    got, grad_fine = meanwhile(got, 4, grad_fine)
    even, odd = settle(keep, got)
    got = swap(odd, "group", 1)
    got, grad_fine = meanwhile(got, 5, grad_fine)
    last = swap(jnp.concatenate([even[16:], got[16:]], axis=0), "group", 2)
    grad_owned = finish(here, even, got, last, cond_weight)
    return grad_fine, grad_owned


def solution(mesh):
    rows3 = P(BOTH, None, None)
    rows2 = P(BOTH, None)
    return jax.shard_map(
        body,
        mesh=mesh,
        in_specs=(rows3, rows3, rows2, P(), P(), rows3, rows3, rows3, rows2, P()),
        out_specs=(rows3, rows2),
        check_vma=False,
    )
```

```python
import functools

import jax
import jax.numpy as jnp
import numpy as np
from jax import lax
from jax.experimental import pallas as pl
from jax.experimental.pallas import tpu as pltpu
from jax.sharding import PartitionSpec as P

PW = 16
ROWS = 12
LON = 2048
PC = LON // PW
CH = 128
PAIRS = ROWS // 2
EXT = ROWS + 2
SLOTS = 2048
OWNERS = 128
BF = jnp.bfloat16
F32 = jnp.float32
MB = 1 << 20
BOTH = ("group", "band")


def dot(a, b):
    return jnp.dot(a, b, preferred_element_type=F32)


WHOLE = pl.BlockSpec(memory_space=pltpu.VMEM)


def params(mib):
    return pltpu.CompilerParams(vmem_limit_bytes=mib * MB)


ANYWHERE = pl.BlockSpec(memory_space=pl.ANY)
SCALARS = pl.BlockSpec(memory_space=pltpu.SMEM)


CHIPS = 16


def project_kernel(coarse, w_ref, out):
    rows = coarse.shape[0]
    value = dot(coarse[...], w_ref[...]).astype(BF)
    for chip in range(CHIPS):
        out[chip * rows : (chip + 1) * rows] = value


def project(coarse, cond_weight):
    return pl.pallas_call(
        project_kernel,
        in_specs=[WHOLE] * 2,
        out_specs=WHOLE,
        out_shape=jax.ShapeDtypeStruct((CHIPS * coarse.shape[0], CH), BF),
        compiler_params=params(4),
        name="project",
    )(coarse, cond_weight)


def pack_kernel(w_ref, packed, back, w_back):
    zero = jnp.zeros((CH, CH), BF)
    left, right = slice(0, CH), slice(CH, 2 * CH)
    for kx in range(3):
        flipped = []
        for ky in range(3):
            turned = w_ref[2 - ky, 2 - kx].astype(F32).T.astype(BF)
            w_back[ky, kx * CH : (kx + 1) * CH, :] = turned
            flipped.append(turned)
        for r in range(4):
            rows = slice(r * CH, (r + 1) * CH)
            packed[kx, rows, left] = w_ref[r, kx] if r < 3 else zero
            packed[kx, rows, right] = w_ref[r - 1, kx] if r >= 1 else zero
            back[kx, rows, left] = flipped[r] if r < 3 else zero
            back[kx, rows, right] = flipped[r - 1] if r >= 1 else zero


def pack(conv_weight):
    both = jax.ShapeDtypeStruct((3, 4 * CH, 2 * CH), BF)
    return pl.pallas_call(
        pack_kernel,
        in_specs=[WHOLE],
        out_specs=[WHOLE] * 3,
        out_shape=[both, both, jax.ShapeDtypeStruct((3, 3 * CH, CH), BF)],
        compiler_params=params(4),
        name="pack",
    )(conv_weight)


def conv_pair(rows, w_ref, write):
    lhs = jnp.concatenate(rows, axis=1)
    left = dot(lhs, w_ref[0])
    right = dot(lhs, w_ref[2])
    place = lax.broadcasted_iota(jnp.int32, (LON, 1), 0)
    total = dot(lhs, w_ref[1])
    total += jnp.where(place == 0, 0.0, pltpu.roll(left, 1, 0))
    total += jnp.where(place == LON - 1, 0.0, pltpu.roll(right, LON - 1, 0))
    write(0, total[:, :CH])
    write(1, total[:, CH:])


def conv_state_inner_kernel(start, *refs):
    field, w_ref, out = refs[0], refs[1], refs[-1]
    q = start + pl.program_id(0)

    def write(r, value):
        out[2 * q - 2 + r] = value

    conv_pair([field[2 * q - 2 + r] for r in range(4)], w_ref, write)


def conv_state_rim_kernel(w_ref, up, down, head, tail, out):
    def conv_at(at, above, below):
        def write(r, value):
            out[at + r] = value

        conv_pair([above[:LON], above[LON : 2 * LON], below[:LON], below[LON : 2 * LON]], w_ref, write)

    @pl.when(pl.program_id(0) == 0)
    def _():
        conv_at(0, up, head)

    @pl.when(pl.program_id(0) == 1)
    def _():
        conv_at(2, tail, down)


def conv_cost(pairs):
    return pl.CostEstimate(
        flops=4 * pairs * LON * 12 * CH * CH, bytes_accessed=pairs * LON * CH * 12, transcendentals=0
    )


PRE = pltpu.VMEM((EXT - 4, LON, CH), F32)
PRE_RIM = pltpu.VMEM((4, LON, CH), F32)


def conv_state_inner(field, packed, start, count, before=None):
    args = (field, packed) if before is None else (field, packed, before)
    return pl.pallas_call(
        functools.partial(conv_state_inner_kernel, start),
        grid=(count,),
        in_specs=[WHOLE] * len(args),
        out_specs=WHOLE,
        out_shape=PRE,
        input_output_aliases={} if before is None else {2: 0},
        compiler_params=params(8),
        cost_estimate=conv_cost(count),
        name="conv_state",
    )(*args)


def conv_state_rim(packed, rims):
    return pl.pallas_call(
        conv_state_rim_kernel,
        grid=(2,),
        in_specs=[WHOLE] * 5,
        out_specs=WHOLE,
        out_shape=PRE_RIM,
        compiler_params=params(8),
        cost_estimate=conv_cost(2),
        name="conv_state_rim",
    )(packed, *rims)


def conv_grad_kernel(start, *refs):
    field, w_ref, cot, out = refs[0], refs[1], refs[2], refs[-1]
    p = start + pl.program_id(0)

    def write(r, value):
        out[r] = (cot[2 * p + r].astype(F32) + value).astype(BF)

    conv_pair([field[2 * p + r] for r in range(4)], w_ref, write)


def conv_grad(field, packed, cotangent, start, count, before=None):
    args = [field, packed, cotangent] + ([] if before is None else [before])
    return pl.pallas_call(
        functools.partial(conv_grad_kernel, start),
        grid=(count,),
        in_specs=[WHOLE] * 3 + ([] if before is None else [ANYWHERE]),
        out_specs=pl.BlockSpec((2, LON, CH), lambda i: (start + i, 0, 0)),
        out_shape=jax.ShapeDtypeStruct((ROWS, LON, CH), BF),
        input_output_aliases={} if before is None else {3: 0},
        compiler_params=params(8),
        cost_estimate=conv_cost(count),
        name="conv_grad",
    )(*args)


SC_CHUNK = 512


def onehot(height, index_row):
    place = lax.broadcasted_iota(jnp.int32, (height, index_row.shape[1]), 0)
    return jnp.where(place == index_row, 1.0, 0.0).astype(BF)


def contract0(a, b):
    return lax.dot_general(a, b, (((0,), (0,)), ((), ())), preferred_element_type=F32)


def contract1(a, b):
    return lax.dot_general(a, b, (((1,), (1,)), ((), ())), preferred_element_type=F32)


def slot_row(ref, first):
    return jnp.concatenate([ref[first + k : first + k + 1, :] for k in range(SC_CHUNK // OWNERS)], axis=1)


def live_weight(weight, count):
    slot = lax.broadcasted_iota(jnp.int32, weight.shape, 0)
    return jnp.where(slot < count[...], weight[...], 0.0)


RIM = 3 * LON + 2 * PC


def spread_kernel(
    here,
    near,
    far,
    perm,
    patch,
    target,
    weight,
    count,
    fine_head,
    fine_tail,
    cot_head,
    cot_tail,
    out,
    head,
    tail,
    source,
    live,
    sems,
):
    copies = []
    for to, (buffer, rows) in enumerate(((head, (fine_head, cot_head)), (tail, (fine_tail, cot_tail)))):
        for j, row in enumerate((rows[0].at[0], rows[0].at[1], rows[1].at[0])):
            copies.append(
                pltpu.make_async_copy(row, buffer.at[pl.ds(j * LON, LON)], sems.at[3 * to + j])
            )
    for copy in copies:
        copy.start()
    live[...] = live_weight(weight, count)
    row = jnp.zeros(target.shape, jnp.int32)
    for t in range(16):
        row += jnp.where(target[...] == t, perm[t : t + 1, :], 0)
    source[...] = (row >> 7) * 64 + (row & 63) + jnp.where(((row >> 6) & 1) == (here[1] & 1), 0, SLOTS // 2)
    patches = ROWS * PC
    panel = jnp.concatenate([near[...], far[...]], axis=0)
    total = jnp.zeros((patches, CH), F32)
    for first in range(0, 16, SC_CHUNK // OWNERS):
        picked = contract0(panel, onehot(SLOTS, slot_row(source, first)))
        picked = (picked * slot_row(live, first)).astype(BF)
        total += contract1(onehot(patches, slot_row(patch, first)), picked)
    total = total.astype(BF)
    out[...] = total
    for copy in copies:
        copy.wait()
    head[3 * LON :] = total[: 2 * PC]
    tail[3 * LON :] = total[-2 * PC :]


def spread(here, near, far, perm, patch, target, weight, count, rims):
    rim = pltpu.VMEM((RIM, CH), BF)
    return pl.pallas_call(
        spread_kernel,
        in_specs=[SCALARS] + [WHOLE] * 7 + [ANYWHERE] * 4,
        out_specs=[WHOLE] * 3,
        out_shape=[jax.ShapeDtypeStruct((ROWS * PC, CH), BF), rim, rim],
        scratch_shapes=[
            pltpu.VMEM((16, OWNERS), jnp.int32),
            pltpu.VMEM((16, OWNERS), F32),
            pltpu.SemaphoreType.DMA((6,)),
        ],
        compiler_params=params(12),
        cost_estimate=pl.CostEstimate(flops=4 * 2048 * 2048 * 128, bytes_accessed=MB, transcendentals=0),
        name="spread",
    )(here, near, far, perm, patch, target, weight, count, *rims)


EX_CELLS = 1024
RD_CELLS = 256


def patch_marks(count):
    cells = np.arange(count)[:, None]
    inside = cells // PW == np.arange(count // PW)[None, :]
    marks = [inside, inside & (cells % PW == 0), inside & (cells % PW == PW - 1)]
    return np.concatenate(marks, axis=1).astype(np.float32)


def shift_patch(value, step):
    place = lax.broadcasted_iota(jnp.int32, (PC, 1), 0)
    if step > 0:
        return jnp.where(place == 0, 0.0, pltpu.roll(value, 1, 0))
    return jnp.where(place == PC - 1, 0.0, pltpu.roll(value, PC - 1, 0))


def silu_inner_kernel(pre, cond, w_ref, ex_ref, rd_ref, cot, out, sums):
    q = pl.program_id(0) + 1
    silu_pair(
        q, pre, 2 * q - 2, cond[q - 1], cond[q], lambda cells: (cot[2 * q - 1, cells], cot[2 * q, cells]), w_ref, ex_ref, rd_ref, out, sums
    )


def silu_rim_kernel(pre, cond, w_ref, ex_ref, rd_ref, up, down, head, tail, before, before_sums, out, sums):
    def weights_of(first, second):
        def weights(cells):
            rows = slice(2 * LON + cells.start, 2 * LON + cells.stop)
            return first[rows], second[rows]

        return weights

    @pl.when(pl.program_id(0) == 0)
    def _():
        silu_pair(0, pre, 0, up[3 * LON :], cond[0], weights_of(up, head), w_ref, ex_ref, rd_ref, out, sums)

    @pl.when(pl.program_id(0) == 1)
    def _():
        weights, below = weights_of(tail, down), down[3 * LON :]
        silu_pair(PAIRS, pre, 2, cond[PAIRS - 1], below, weights, w_ref, ex_ref, rd_ref, out, sums)


def silu_pair(q, pre, at, above, below, cot_pair, w_ref, ex_ref, rd_ref, out, sums):
    lhs = jnp.concatenate([above[:PC], above[PC:], below[:PC], below[PC:]], axis=1)
    west, here, east = [dot(lhs, w_ref[k]) for k in range(3)]
    inner = (west + here + east).astype(BF)
    at_first = (shift_patch(west, 1) - west).astype(BF)
    at_last = (shift_patch(east, -1) - east).astype(BF)
    per = EX_CELLS // PW
    part_sum, part_first, part_last = [], [], []
    for lo in range(0, LON, EX_CELLS):
        cells = slice(lo, lo + EX_CELLS)
        cut = slice(lo // PW, lo // PW + per)
        terms = jnp.concatenate([inner[cut], at_first[cut], at_last[cut]], axis=0)
        spread_terms = dot(ex_ref[...], terms)
        weights = cot_pair(cells)
        grads = []
        for r in range(2):
            half = 0.5 * (pre[at + r, cells] + spread_terms[:, r * CH : (r + 1) * CH])
            t = jnp.tanh(half)
            slope = (0.5 + 0.5 * t) * (1.0 + half * (1.0 - t))
            g = (weights[r].astype(F32) * slope).astype(BF)
            out[2 * q + r, cells] = g
            grads.append(g)
        grads = jnp.concatenate(grads, axis=1)
        for first in range(0, EX_CELLS, RD_CELLS):
            reduced = dot(rd_ref[...], grads[first : first + RD_CELLS])
            part_sum.append(reduced[:PW])
            part_first.append(reduced[PW : 2 * PW])
            part_last.append(reduced[2 * PW :])
    whole, firsts, lasts = [jnp.concatenate(p, axis=0) for p in (part_sum, part_first, part_last)]
    from_west = (whole - lasts + shift_patch(lasts, 1)).astype(BF)
    from_east = (whole - firsts + shift_patch(firsts, -1)).astype(BF)
    whole = whole.astype(BF)
    for r in range(2):
        cut = slice(r * CH, (r + 1) * CH)
        sums[2 * q + r] = jnp.concatenate([from_west[:, cut], whole[:, cut], from_east[:, cut]], axis=1)


def silu_grad(pre, cotangent, cond, packed, rims=None, before=None):
    expand = jnp.asarray(patch_marks(EX_CELLS), BF)
    reduce_m = jnp.asarray(patch_marks(RD_CELLS).T, BF)
    inner = rims is None
    args = [pre, cond.reshape(PAIRS, 2 * PC, CH), packed, expand, reduce_m]
    args += [cotangent] if inner else [*rims, *before]
    return pl.pallas_call(
        silu_inner_kernel if inner else silu_rim_kernel,
        grid=(PAIRS - 1 if inner else 2,),
        in_specs=[WHOLE] * len(args),
        out_specs=[WHOLE, WHOLE],
        out_shape=[pltpu.VMEM((EXT, LON, CH), BF), pltpu.VMEM((EXT, PC, 3 * CH), BF)],
        input_output_aliases={} if inner else {9: 0, 10: 1},
        compiler_params=params(8),
        cost_estimate=pl.CostEstimate(flops=10**9, bytes_accessed=8 * ROWS * LON * CH, transcendentals=0),
        name="silu_grad",
    )(*args)


def collect_kernel(here, sums, w_ref, patch, target, weight, count, keep, send, total, slots, shares, picked):
    patches = ROWS * PC
    grad_patch = dot(sums[:patches], w_ref[0])
    grad_patch += dot(sums[PC : PC + patches], w_ref[1])
    grad_patch += dot(sums[2 * PC :], w_ref[2])
    grad_patch = grad_patch.astype(BF)
    owner = lax.broadcasted_iota(jnp.int32, (OWNERS, OWNERS), 0)
    place = ((owner ^ here[1]) & 1) * (OWNERS // 2) + (owner >> 1)
    order = jnp.where(place == lax.broadcasted_iota(jnp.int32, (OWNERS, OWNERS), 1), 1.0, 0.0)
    values = jnp.concatenate(
        [patch[...].astype(F32), target[...].astype(F32), live_weight(weight, count)], axis=0
    )
    values = jnp.dot(values, order, preferred_element_type=F32, precision=lax.Precision.HIGHEST)
    slots[...] = (values[:32] + 0.5).astype(jnp.int32)
    step = lax.broadcasted_iota(jnp.int32, (16, OWNERS), 0)
    for k in range(16):
        hit = step == slots[16 + k : 17 + k, :]
        shares[k] = jnp.where(hit, values[32 + k : 33 + k, :], 0.0)
    for first in range(0, 16, SC_CHUNK // OWNERS):
        got = contract0(grad_patch, onehot(patches, slot_row(slots, first)))
        for k in range(SC_CHUNK // OWNERS):
            picked[first + k] = got[:, k * OWNERS : (k + 1) * OWNERS]
    for t in range(16):
        mine = picked[0] * shares[0, t : t + 1, :]
        for k in range(1, 16):
            mine += picked[k] * shares[k, t : t + 1, :]
        total[pl.ds(t, OWNERS, stride=16), :] = mine.T
    keep[...] = total[: SLOTS // 2]
    send[...] = total[SLOTS // 2 :].astype(BF)


def collect(here, sums, w, patch, target, weight, count):
    return pl.pallas_call(
        collect_kernel,
        in_specs=[SCALARS] + [WHOLE] * 6,
        out_specs=[WHOLE, WHOLE],
        out_shape=[
            jax.ShapeDtypeStruct((SLOTS // 2, CH), F32),
            jax.ShapeDtypeStruct((SLOTS // 2, CH), BF),
        ],
        scratch_shapes=[
            pltpu.VMEM((SLOTS, CH), F32),
            pltpu.VMEM((32, OWNERS), jnp.int32),
            pltpu.VMEM((16, 16, OWNERS), F32),
            pltpu.VMEM((16, CH, OWNERS), F32),
        ],
        compiler_params=params(16),
        cost_estimate=pl.CostEstimate(flops=2 * 2048 * 2048 * 128, bytes_accessed=2 * MB, transcendentals=0),
        name="collect",
    )(here, sums.reshape(EXT * PC, 3 * CH), w, patch, target, weight, count)


def merge_kernel(kept, got, out):
    out[...] = (kept[...] + got[...].astype(F32)).astype(BF)


def merge(kept, got):
    return pl.pallas_call(
        merge_kernel,
        in_specs=[WHOLE] * 2,
        out_specs=WHOLE,
        out_shape=jax.ShapeDtypeStruct(kept.shape, BF),
        compiler_params=params(4),
        name="merge",
    )(kept, got)


def finish_kernel(got, w_ref, out):
    rows = []
    for group in range(4):
        total = got[group * CHIPS].astype(F32)
        for chip in range(1, CHIPS):
            total += got[group * CHIPS + chip].astype(F32)
        rows.append(total.astype(BF))
    out[...] = contract1(jnp.concatenate(rows, axis=0), w_ref[...])


def finish(got, cond_weight):
    return pl.pallas_call(
        finish_kernel,
        in_specs=[WHOLE] * 2,
        out_specs=WHOLE,
        out_shape=jax.ShapeDtypeStruct((64, cond_weight.shape[0]), F32),
        compiler_params=params(4),
        name="finish",
    )(got, cond_weight)


def from_neighbours(head, tail):
    count = lax.axis_size(BOTH)
    up = lax.ppermute(tail, BOTH, [(i, i + 1) for i in range(count - 1)])
    down = lax.ppermute(head, BOTH, [(i + 1, i) for i in range(count - 1)])
    return up, down


def swap(value, axis, bit):
    return lax.ppermute(value, axis, [(i, i ^ bit) for i in range(lax.axis_size(axis))])


def after(value, *earlier):
    return lax.optimization_barrier((value,) + earlier)[0]


def body(
    fine_state,
    cotangent,
    coarse,
    conv_weight,
    cond_weight,
    slot_patch,
    slot_target,
    slot_weight,
    block_count,
    panel_perm,
):
    group = lax.axis_index("group")
    band = lax.axis_index("band")
    here = jnp.stack([group, band]).astype(jnp.int32)
    patch, target, weight = slot_patch[0].T, slot_target[0].T, slot_weight[0].T

    same_core = [[2 * chip + core for chip in range(CHIPS)] for core in range(2)]
    projected, perms, weights, field, cot = lax.optimization_barrier(
        (project(coarse, cond_weight), panel_perm, conv_weight, fine_state, cotangent)
    )
    perm = lax.dynamic_index_in_dim(perms, group, 0, keepdims=False).reshape(-1, 16).T
    near = lax.all_to_all(projected, "band", 0, 0, axis_index_groups=same_core, tiled=True)
    packed, packed_back, w_back = pack(weights)
    cut = (field[:2], field[-2:], cot[:1], cot[-1:])
    near, here, perm, packed, cut = lax.optimization_barrier((near, here, perm, packed, cut))
    far = swap(near, "band", 1)
    cond, head, tail = spread(here, near, far, perm, patch, target, weight, block_count, cut)
    up, down = from_neighbours(head, tail)
    pre = conv_state_inner(after(fine_state, far), packed, 1, 5)
    grad_pre, sums = silu_grad(pre, cotangent, cond, packed)
    grad_pre, sums, up, down = lax.optimization_barrier((grad_pre, sums, up, down))
    rims = (up, down, head, tail)
    pre = conv_state_rim(packed, rims)
    grad_pre, sums = silu_grad(pre, cotangent, cond, packed, rims, (grad_pre, sums))

    keep, send = collect(here, sums, w_back, patch, target, weight, block_count)
    got = swap(send, "band", 1)
    grad_fine = conv_grad(after(grad_pre, keep), packed_back, cotangent, 0, 1)
    got, grad_fine = lax.optimization_barrier((got, grad_fine))
    owned = merge(keep, got)
    count = lax.axis_size(BOTH)
    same_core = [list(range(core, count, 2)) for core in range(2)]
    received = lax.all_to_all(
        owned.reshape(count // 2, 16, CH), BOTH, 0, 0, axis_index_groups=same_core, tiled=True
    )
    grad_fine = conv_grad(after(grad_pre, owned), packed_back, cotangent, 1, 5, grad_fine)
    received, grad_fine = lax.optimization_barrier((received, grad_fine))
    grad_owned = finish(received, cond_weight)
    return grad_fine, grad_owned


def solution(mesh):
    rows3 = P(BOTH, None, None)
    rows2 = P(BOTH, None)
    return jax.shard_map(
        body,
        mesh=mesh,
        in_specs=(rows3, rows3, rows2, P(), P(), rows3, rows3, rows3, rows2, P()),
        out_specs=(rows3, rows2),
        check_vma=False,
    )
```

```python
import functools

import jax
import jax.numpy as jnp
import numpy as np
from jax import lax
from jax.experimental import pallas as pl
from jax.experimental.pallas import tpu as pltpu
from jax.sharding import PartitionSpec as P

PW = 16
ROWS = 12
LON = 2048
PC = LON // PW
CH = 128
PAIRS = ROWS // 2
EXT = ROWS + 2
SLOTS = 2048
OWNERS = 128
BF = jnp.bfloat16
F32 = jnp.float32
MB = 1 << 20
BOTH = ("group", "band")


def dot(a, b):
    return jnp.dot(a, b, preferred_element_type=F32)


WHOLE = pl.BlockSpec(memory_space=pltpu.VMEM)


def params(mib):
    return pltpu.CompilerParams(vmem_limit_bytes=mib * MB)


ANYWHERE = pl.BlockSpec(memory_space=pl.ANY)
SCALARS = pl.BlockSpec(memory_space=pltpu.SMEM)


CHIPS = 16


def project_kernel(coarse, w_ref, out):
    rows = coarse.shape[0]
    value = dot(coarse[...], w_ref[...]).astype(BF)
    for chip in range(CHIPS):
        out[chip * rows : (chip + 1) * rows] = value


def project(coarse, cond_weight):
    return pl.pallas_call(
        project_kernel,
        in_specs=[WHOLE] * 2,
        out_specs=WHOLE,
        out_shape=jax.ShapeDtypeStruct((CHIPS * coarse.shape[0], CH), BF),
        compiler_params=params(4),
        name="project",
    )(coarse, cond_weight)


def pack_kernel(w_ref, packed, back, w_back):
    zero = jnp.zeros((CH, CH), BF)
    left, right = slice(0, CH), slice(CH, 2 * CH)
    for kx in range(3):
        flipped = []
        for ky in range(3):
            turned = w_ref[2 - ky, 2 - kx].astype(F32).T.astype(BF)
            w_back[ky, kx * CH : (kx + 1) * CH, :] = turned
            flipped.append(turned)
        for r in range(4):
            rows = slice(r * CH, (r + 1) * CH)
            packed[kx, rows, left] = w_ref[r, kx] if r < 3 else zero
            packed[kx, rows, right] = w_ref[r - 1, kx] if r >= 1 else zero
            back[kx, rows, left] = flipped[r] if r < 3 else zero
            back[kx, rows, right] = flipped[r - 1] if r >= 1 else zero


def pack(conv_weight):
    both = jax.ShapeDtypeStruct((3, 4 * CH, 2 * CH), BF)
    return pl.pallas_call(
        pack_kernel,
        in_specs=[WHOLE],
        out_specs=[WHOLE] * 3,
        out_shape=[both, both, jax.ShapeDtypeStruct((3, 3 * CH, CH), BF)],
        compiler_params=params(4),
        name="pack",
    )(conv_weight)


def conv_pair(rows, w_ref, write):
    lhs = jnp.concatenate(rows, axis=1)
    left = dot(lhs, w_ref[0])
    right = dot(lhs, w_ref[2])
    place = lax.broadcasted_iota(jnp.int32, (LON, 1), 0)
    total = dot(lhs, w_ref[1])
    total += jnp.where(place == 0, 0.0, pltpu.roll(left, 1, 0))
    total += jnp.where(place == LON - 1, 0.0, pltpu.roll(right, LON - 1, 0))
    write(0, total[:, :CH])
    write(1, total[:, CH:])


def conv_state_inner_kernel(start, *refs):
    field, w_ref, out = refs[0], refs[1], refs[-1]
    q = start + pl.program_id(0)

    def write(r, value):
        out[2 * q - 2 + r] = value

    conv_pair([field[2 * q - 2 + r] for r in range(4)], w_ref, write)


def conv_state_rim_kernel(w_ref, up, down, head, tail, out):
    def conv_at(at, above, below):
        def write(r, value):
            out[at + r] = value

        conv_pair([above[:LON], above[LON : 2 * LON], below[:LON], below[LON : 2 * LON]], w_ref, write)

    @pl.when(pl.program_id(0) == 0)
    def _():
        conv_at(0, up, head)

    @pl.when(pl.program_id(0) == 1)
    def _():
        conv_at(2, tail, down)


def conv_cost(pairs):
    return pl.CostEstimate(
        flops=4 * pairs * LON * 12 * CH * CH, bytes_accessed=pairs * LON * CH * 12, transcendentals=0
    )


PRE = pltpu.VMEM((EXT - 4, LON, CH), F32)
PRE_RIM = pltpu.VMEM((4, LON, CH), F32)


def conv_state_inner(field, packed, start, count, before=None):
    args = (field, packed) if before is None else (field, packed, before)
    return pl.pallas_call(
        functools.partial(conv_state_inner_kernel, start),
        grid=(count,),
        in_specs=[WHOLE] * len(args),
        out_specs=WHOLE,
        out_shape=PRE,
        input_output_aliases={} if before is None else {2: 0},
        compiler_params=params(8),
        cost_estimate=conv_cost(count),
        name="conv_state",
    )(*args)


def conv_state_rim(packed, rims):
    return pl.pallas_call(
        conv_state_rim_kernel,
        grid=(2,),
        in_specs=[WHOLE] * 5,
        out_specs=WHOLE,
        out_shape=PRE_RIM,
        compiler_params=params(8),
        cost_estimate=conv_cost(2),
        name="conv_state_rim",
    )(packed, *rims)


def conv_grad_kernel(start, *refs):
    field, w_ref, cot, out = refs[0], refs[1], refs[2], refs[-1]
    p = start + pl.program_id(0)

    def write(r, value):
        out[r] = (cot[2 * p + r].astype(F32) + value).astype(BF)

    conv_pair([field[2 * p + r] for r in range(4)], w_ref, write)


def conv_grad(field, packed, cotangent, start, count, before=None):
    args = [field, packed, cotangent] + ([] if before is None else [before])
    return pl.pallas_call(
        functools.partial(conv_grad_kernel, start),
        grid=(count,),
        in_specs=[WHOLE] * 3 + ([] if before is None else [ANYWHERE]),
        out_specs=pl.BlockSpec((2, LON, CH), lambda i: (start + i, 0, 0)),
        out_shape=jax.ShapeDtypeStruct((ROWS, LON, CH), BF),
        input_output_aliases={} if before is None else {3: 0},
        compiler_params=params(8),
        cost_estimate=conv_cost(count),
        name="conv_grad",
    )(*args)


def conv_grad_rest_kernel(upper, lower, w_ref, cot, before, out):
    def write(r, value):
        out[r] = (cot[r].astype(F32) + value).astype(BF)

    conv_pair([upper[0], upper[1], lower[0], lower[1]], w_ref, write)


def conv_grad_rest(field, packed, cotangent, start, before):
    return pl.pallas_call(
        conv_grad_rest_kernel,
        grid=(PAIRS - start,),
        in_specs=[
            pl.BlockSpec((2, LON, CH), lambda i: (start + i, 0, 0)),
            pl.BlockSpec((2, LON, CH), lambda i: (start + i + 1, 0, 0)),
            pl.BlockSpec((3, 4 * CH, 2 * CH), lambda i: (0, 0, 0)),
            pl.BlockSpec((2, LON, CH), lambda i: (start + i, 0, 0)),
            ANYWHERE,
        ],
        out_specs=pl.BlockSpec((2, LON, CH), lambda i: (start + i, 0, 0)),
        out_shape=jax.ShapeDtypeStruct((ROWS, LON, CH), BF),
        input_output_aliases={4: 0},
        compiler_params=params(58),
        cost_estimate=conv_cost(PAIRS - start),
        name="conv_grad_rest",
    )(field, field, packed, cotangent, before)


SC_CHUNK = 512


def onehot(height, index_row):
    place = lax.broadcasted_iota(jnp.int32, (height, index_row.shape[1]), 0)
    return jnp.where(place == index_row, 1.0, 0.0).astype(BF)


def contract0(a, b):
    return lax.dot_general(a, b, (((0,), (0,)), ((), ())), preferred_element_type=F32)


def contract1(a, b):
    return lax.dot_general(a, b, (((1,), (1,)), ((), ())), preferred_element_type=F32)


def slot_row(ref, first):
    return jnp.concatenate([ref[first + k : first + k + 1, :] for k in range(SC_CHUNK // OWNERS)], axis=1)


def live_weight(weight, count):
    slot = lax.broadcasted_iota(jnp.int32, weight.shape, 0)
    return jnp.where(slot < count[...], weight[...], 0.0)


RIM = 3 * LON + 2 * PC


def spread_kernel(
    here,
    near,
    far,
    perm,
    patch,
    target,
    weight,
    count,
    field,
    cot_head,
    cot_tail,
    out,
    head,
    tail,
    source,
    live,
    sems,
):
    copies = []
    for to, (buffer, rows) in enumerate(((head, (field.at[0], field.at[1], cot_head.at[0])), (tail, (field.at[ROWS - 2], field.at[ROWS - 1], cot_tail.at[0])))):
        for j, row in enumerate(rows):
            copies.append(
                pltpu.make_async_copy(row, buffer.at[pl.ds(j * LON, LON)], sems.at[3 * to + j])
            )
    for copy in copies:
        copy.start()
    live[...] = live_weight(weight, count)
    row = jnp.zeros(target.shape, jnp.int32)
    for t in range(16):
        row += jnp.where(target[...] == t, perm[t : t + 1, :], 0)
    source[...] = (row >> 7) * 64 + (row & 63) + jnp.where(((row >> 6) & 1) == (here[1] & 1), 0, SLOTS // 2)
    patches = ROWS * PC
    panel = jnp.concatenate([near[...], far[...]], axis=0)
    total = jnp.zeros((patches, CH), F32)
    for first in range(0, 16, SC_CHUNK // OWNERS):
        picked = contract0(panel, onehot(SLOTS, slot_row(source, first)))
        picked = (picked * slot_row(live, first)).astype(BF)
        total += contract1(onehot(patches, slot_row(patch, first)), picked)
    total = total.astype(BF)
    out[...] = total
    for copy in copies:
        copy.wait()
    head[3 * LON :] = total[: 2 * PC]
    tail[3 * LON :] = total[-2 * PC :]


def spread(here, near, far, perm, patch, target, weight, count, rims):
    rim = pltpu.VMEM((RIM, CH), BF)
    return pl.pallas_call(
        spread_kernel,
        in_specs=[SCALARS] + [WHOLE] * 8 + [ANYWHERE] * 2,
        out_specs=[WHOLE] * 3,
        out_shape=[jax.ShapeDtypeStruct((ROWS * PC, CH), BF), rim, rim],
        scratch_shapes=[
            pltpu.VMEM((16, OWNERS), jnp.int32),
            pltpu.VMEM((16, OWNERS), F32),
            pltpu.SemaphoreType.DMA((6,)),
        ],
        compiler_params=params(12),
        cost_estimate=pl.CostEstimate(flops=4 * 2048 * 2048 * 128, bytes_accessed=MB, transcendentals=0),
        name="spread",
    )(here, near, far, perm, patch, target, weight, count, *rims)


EX_CELLS = 1024
RD_CELLS = 256


def patch_marks(count):
    cells = np.arange(count)[:, None]
    inside = cells // PW == np.arange(count // PW)[None, :]
    marks = [inside, inside & (cells % PW == 0), inside & (cells % PW == PW - 1)]
    return np.concatenate(marks, axis=1).astype(np.float32)


def shift_patch(value, step):
    place = lax.broadcasted_iota(jnp.int32, (PC, 1), 0)
    if step > 0:
        return jnp.where(place == 0, 0.0, pltpu.roll(value, 1, 0))
    return jnp.where(place == PC - 1, 0.0, pltpu.roll(value, PC - 1, 0))


def silu_inner_kernel(pre, cond, w_ref, ex_ref, rd_ref, cot, out, sums):
    q = pl.program_id(0) + 1
    silu_pair(
        q, pre, 2 * q - 2, cond[q - 1], cond[q], lambda cells: (cot[2 * q - 1, cells], cot[2 * q, cells]), w_ref, ex_ref, rd_ref, out, sums
    )


def silu_rim_kernel(pre, cond, w_ref, ex_ref, rd_ref, up, down, head, tail, before, before_sums, out, sums):
    def weights_of(first, second):
        def weights(cells):
            rows = slice(2 * LON + cells.start, 2 * LON + cells.stop)
            return first[rows], second[rows]

        return weights

    @pl.when(pl.program_id(0) == 0)
    def _():
        silu_pair(0, pre, 0, up[3 * LON :], cond[0], weights_of(up, head), w_ref, ex_ref, rd_ref, out, sums)

    @pl.when(pl.program_id(0) == 1)
    def _():
        weights, below = weights_of(tail, down), down[3 * LON :]
        silu_pair(PAIRS, pre, 2, cond[PAIRS - 1], below, weights, w_ref, ex_ref, rd_ref, out, sums)


def silu_pair(q, pre, at, above, below, cot_pair, w_ref, ex_ref, rd_ref, out, sums):
    lhs = jnp.concatenate([above[:PC], above[PC:], below[:PC], below[PC:]], axis=1)
    west, here, east = [dot(lhs, w_ref[k]) for k in range(3)]
    inner = (west + here + east).astype(BF)
    at_first = (shift_patch(west, 1) - west).astype(BF)
    at_last = (shift_patch(east, -1) - east).astype(BF)
    per = EX_CELLS // PW
    part_sum, part_first, part_last = [], [], []
    for lo in range(0, LON, EX_CELLS):
        cells = slice(lo, lo + EX_CELLS)
        cut = slice(lo // PW, lo // PW + per)
        terms = jnp.concatenate([inner[cut], at_first[cut], at_last[cut]], axis=0)
        spread_terms = dot(ex_ref[...], terms)
        weights = cot_pair(cells)
        grads = []
        for r in range(2):
            half = 0.5 * (pre[at + r, cells] + spread_terms[:, r * CH : (r + 1) * CH])
            t = jnp.tanh(half)
            slope = (0.5 + 0.5 * t) * (1.0 + half * (1.0 - t))
            g = (weights[r].astype(F32) * slope).astype(BF)
            out[2 * q + r, cells] = g
            grads.append(g)
        grads = jnp.concatenate(grads, axis=1)
        for first in range(0, EX_CELLS, RD_CELLS):
            reduced = dot(rd_ref[...], grads[first : first + RD_CELLS])
            part_sum.append(reduced[:PW])
            part_first.append(reduced[PW : 2 * PW])
            part_last.append(reduced[2 * PW :])
    whole, firsts, lasts = [jnp.concatenate(p, axis=0) for p in (part_sum, part_first, part_last)]
    from_west = (whole - lasts + shift_patch(lasts, 1)).astype(BF)
    from_east = (whole - firsts + shift_patch(firsts, -1)).astype(BF)
    whole = whole.astype(BF)
    for r in range(2):
        cut = slice(r * CH, (r + 1) * CH)
        sums[2 * q + r] = jnp.concatenate([from_west[:, cut], whole[:, cut], from_east[:, cut]], axis=1)


def silu_grad(pre, cotangent, cond, packed, rims=None, before=None):
    expand = jnp.asarray(patch_marks(EX_CELLS), BF)
    reduce_m = jnp.asarray(patch_marks(RD_CELLS).T, BF)
    inner = rims is None
    args = [pre, cond.reshape(PAIRS, 2 * PC, CH), packed, expand, reduce_m]
    args += [cotangent] if inner else [*rims, *before]
    return pl.pallas_call(
        silu_inner_kernel if inner else silu_rim_kernel,
        grid=(PAIRS - 1 if inner else 2,),
        in_specs=[WHOLE] * len(args),
        out_specs=[WHOLE, WHOLE],
        out_shape=[pltpu.VMEM((EXT, LON, CH), BF), pltpu.VMEM((EXT, PC, 3 * CH), BF)],
        input_output_aliases={} if inner else {9: 0, 10: 1},
        compiler_params=params(8),
        cost_estimate=pl.CostEstimate(flops=10**9, bytes_accessed=8 * ROWS * LON * CH, transcendentals=0),
        name="silu_grad",
    )(*args)


def collect_kernel(here, sums, w_ref, patch, target, weight, count, keep, send, total, slots, shares, picked):
    patches = ROWS * PC
    grad_patch = dot(sums[:patches], w_ref[0])
    grad_patch += dot(sums[PC : PC + patches], w_ref[1])
    grad_patch += dot(sums[2 * PC :], w_ref[2])
    grad_patch = grad_patch.astype(BF)
    owner = lax.broadcasted_iota(jnp.int32, (OWNERS, OWNERS), 0)
    place = ((owner ^ here[1]) & 1) * (OWNERS // 2) + (owner >> 1)
    order = jnp.where(place == lax.broadcasted_iota(jnp.int32, (OWNERS, OWNERS), 1), 1.0, 0.0)
    values = jnp.concatenate(
        [patch[...].astype(F32), target[...].astype(F32), live_weight(weight, count)], axis=0
    )
    values = jnp.dot(values, order, preferred_element_type=F32, precision=lax.Precision.HIGHEST)
    slots[...] = (values[:32] + 0.5).astype(jnp.int32)
    step = lax.broadcasted_iota(jnp.int32, (16, OWNERS), 0)
    for k in range(16):
        hit = step == slots[16 + k : 17 + k, :]
        shares[k] = jnp.where(hit, values[32 + k : 33 + k, :], 0.0)
    for first in range(0, 16, SC_CHUNK // OWNERS):
        got = contract0(grad_patch, onehot(patches, slot_row(slots, first)))
        for k in range(SC_CHUNK // OWNERS):
            picked[first + k] = got[:, k * OWNERS : (k + 1) * OWNERS]
    for t in range(16):
        mine = picked[0] * shares[0, t : t + 1, :]
        for k in range(1, 16):
            mine += picked[k] * shares[k, t : t + 1, :]
        total[pl.ds(t, OWNERS, stride=16), :] = mine.T
    keep[...] = total[: SLOTS // 2]
    send[...] = total[SLOTS // 2 :].astype(BF)


def collect(here, sums, w, patch, target, weight, count):
    return pl.pallas_call(
        collect_kernel,
        in_specs=[SCALARS] + [WHOLE] * 6,
        out_specs=[WHOLE, WHOLE],
        out_shape=[
            jax.ShapeDtypeStruct((SLOTS // 2, CH), F32),
            jax.ShapeDtypeStruct((SLOTS // 2, CH), BF),
        ],
        scratch_shapes=[
            pltpu.VMEM((SLOTS, CH), F32),
            pltpu.VMEM((32, OWNERS), jnp.int32),
            pltpu.VMEM((16, 16, OWNERS), F32),
            pltpu.VMEM((16, CH, OWNERS), F32),
        ],
        compiler_params=params(16),
        cost_estimate=pl.CostEstimate(flops=2 * 2048 * 2048 * 128, bytes_accessed=2 * MB, transcendentals=0),
        name="collect",
    )(here, sums.reshape(EXT * PC, 3 * CH), w, patch, target, weight, count)


def merge_kernel(kept, got, out):
    out[...] = (kept[...] + got[...].astype(F32)).astype(BF)


def merge(kept, got):
    return pl.pallas_call(
        merge_kernel,
        in_specs=[WHOLE] * 2,
        out_specs=WHOLE,
        out_shape=jax.ShapeDtypeStruct(kept.shape, BF),
        compiler_params=params(4),
        name="merge",
    )(kept, got)


def finish_kernel(got, w_ref, out):
    rows = []
    for group in range(4):
        total = got[group * CHIPS].astype(F32)
        for chip in range(1, CHIPS):
            total += got[group * CHIPS + chip].astype(F32)
        rows.append(total.astype(BF))
    out[...] = contract1(jnp.concatenate(rows, axis=0), w_ref[...])


def finish(got, cond_weight):
    return pl.pallas_call(
        finish_kernel,
        in_specs=[WHOLE] * 2,
        out_specs=WHOLE,
        out_shape=jax.ShapeDtypeStruct((64, cond_weight.shape[0]), F32),
        compiler_params=params(4),
        name="finish",
    )(got, cond_weight)


def from_neighbours(head, tail):
    count = lax.axis_size(BOTH)
    up = lax.ppermute(tail, BOTH, [(i, i + 1) for i in range(count - 1)])
    down = lax.ppermute(head, BOTH, [(i + 1, i) for i in range(count - 1)])
    return up, down


def swap(value, axis, bit):
    return lax.ppermute(value, axis, [(i, i ^ bit) for i in range(lax.axis_size(axis))])


def after(value, *earlier):
    return lax.optimization_barrier((value,) + earlier)[0]


def body(
    fine_state,
    cotangent,
    coarse,
    conv_weight,
    cond_weight,
    slot_patch,
    slot_target,
    slot_weight,
    block_count,
    panel_perm,
):
    group = lax.axis_index("group")
    band = lax.axis_index("band")
    here = jnp.stack([group, band]).astype(jnp.int32)
    patch, target, weight = slot_patch[0].T, slot_target[0].T, slot_weight[0].T

    same_core = [[2 * chip + core for chip in range(CHIPS)] for core in range(2)]
    projected, perms, cot = lax.optimization_barrier((project(coarse, cond_weight), panel_perm, cotangent))
    perm = lax.dynamic_index_in_dim(perms, group, 0, keepdims=False).reshape(-1, 16).T
    near = lax.all_to_all(projected, "band", 0, 0, axis_index_groups=same_core, tiled=True)
    rims = (cot[:1], cot[-1:])
    near, here, perm, rims, weights, field = lax.optimization_barrier(
        (near, here, perm, rims, conv_weight, fine_state)
    )
    far = swap(near, "band", 1)
    packed, packed_back, w_back = pack(weights)
    far, packed = lax.optimization_barrier((far, packed))
    cond, head, tail = spread(here, near, far, perm, patch, target, weight, block_count, (field, *rims))
    up, down = from_neighbours(head, tail)
    pre = conv_state_inner(field, packed, 1, 5)
    grad_pre, sums = silu_grad(pre, cotangent, cond, packed)
    grad_pre, sums, up, down = lax.optimization_barrier((grad_pre, sums, up, down))
    rims = (up, down, head, tail)
    pre = conv_state_rim(packed, rims)
    grad_pre, sums = silu_grad(pre, cotangent, cond, packed, rims, (grad_pre, sums))

    keep, send = collect(here, sums, w_back, patch, target, weight, block_count)
    got = swap(send, "band", 1)
    grad_fine = conv_grad(after(grad_pre, keep), packed_back, cotangent, 0, 1)
    got, grad_fine = lax.optimization_barrier((got, grad_fine))
    owned = merge(keep, got)
    count = lax.axis_size(BOTH)
    same_core = [list(range(core, count, 2)) for core in range(2)]
    received = lax.all_to_all(
        owned.reshape(count // 2, 16, CH), BOTH, 0, 0, axis_index_groups=same_core, tiled=True
    )
    grad_fine = conv_grad_rest(after(grad_pre, owned), packed_back, cotangent, 1, grad_fine)
    received, grad_fine = lax.optimization_barrier((received, grad_fine))
    grad_owned = finish(received, cond_weight)
    return grad_fine, grad_owned


def solution(mesh):
    rows3 = P(BOTH, None, None)
    rows2 = P(BOTH, None)
    return jax.shard_map(
        body,
        mesh=mesh,
        in_specs=(rows3, rows3, rows2, P(), P(), rows3, rows3, rows3, rows2, P()),
        out_specs=(rows3, rows2),
        check_vma=False,
    )
```

```python
import functools

import jax
import jax.numpy as jnp
import numpy as np
from jax import lax
from jax.experimental import pallas as pl
from jax.experimental.pallas import tpu as pltpu
from jax.sharding import PartitionSpec as P

PW = 16
ROWS = 12
LON = 2048
PC = LON // PW
CH = 128
PAIRS = ROWS // 2
EXT = ROWS + 2
SLOTS = 2048
OWNERS = 128
BF = jnp.bfloat16
F32 = jnp.float32
MB = 1 << 20
BOTH = ("group", "band")


def dot(a, b):
    return jnp.dot(a, b, preferred_element_type=F32)


WHOLE = pl.BlockSpec(memory_space=pltpu.VMEM)


def params(mib):
    return pltpu.CompilerParams(vmem_limit_bytes=mib * MB)


ANYWHERE = pl.BlockSpec(memory_space=pl.ANY)
SCALARS = pl.BlockSpec(memory_space=pltpu.SMEM)


CHIPS = 16


def project_kernel(coarse, w_ref, out):
    rows = coarse.shape[0]
    value = dot(coarse[...], w_ref[...]).astype(BF)
    for chip in range(CHIPS):
        out[chip * rows : (chip + 1) * rows] = value


def project(coarse, cond_weight):
    return pl.pallas_call(
        project_kernel,
        in_specs=[WHOLE] * 2,
        out_specs=WHOLE,
        out_shape=jax.ShapeDtypeStruct((CHIPS * coarse.shape[0], CH), BF),
        compiler_params=params(4),
        name="project",
    )(coarse, cond_weight)


def pack_kernel(w_ref, packed, back, w_back):
    zero = jnp.zeros((CH, CH), BF)
    left, right = slice(0, CH), slice(CH, 2 * CH)
    for kx in range(3):
        flipped = []
        for ky in range(3):
            turned = w_ref[2 - ky, 2 - kx].astype(F32).T.astype(BF)
            w_back[ky, kx * CH : (kx + 1) * CH, :] = turned
            flipped.append(turned)
        for r in range(4):
            rows = slice(r * CH, (r + 1) * CH)
            packed[kx, rows, left] = w_ref[r, kx] if r < 3 else zero
            packed[kx, rows, right] = w_ref[r - 1, kx] if r >= 1 else zero
            back[kx, rows, left] = flipped[r] if r < 3 else zero
            back[kx, rows, right] = flipped[r - 1] if r >= 1 else zero


def pack(conv_weight):
    both = jax.ShapeDtypeStruct((3, 4 * CH, 2 * CH), BF)
    return pl.pallas_call(
        pack_kernel,
        in_specs=[WHOLE],
        out_specs=[WHOLE] * 3,
        out_shape=[both, both, jax.ShapeDtypeStruct((3, 3 * CH, CH), BF)],
        compiler_params=params(4),
        name="pack",
    )(conv_weight)


def conv_pair(rows, w_ref, write):
    lhs = jnp.concatenate(rows, axis=1)
    left = dot(lhs, w_ref[0])
    right = dot(lhs, w_ref[2])
    place = lax.broadcasted_iota(jnp.int32, (LON, 1), 0)
    total = dot(lhs, w_ref[1])
    total += jnp.where(place == 0, 0.0, pltpu.roll(left, 1, 0))
    total += jnp.where(place == LON - 1, 0.0, pltpu.roll(right, LON - 1, 0))
    write(0, total[:, :CH])
    write(1, total[:, CH:])


def conv_state_inner_kernel(start, *refs):
    field, w_ref, out = refs[0], refs[1], refs[-1]
    q = start + pl.program_id(0)

    def write(r, value):
        out[2 * q - 2 + r] = value

    conv_pair([field[2 * q - 2 + r] for r in range(4)], w_ref, write)


def conv_state_rim_kernel(w_ref, up, down, head, tail, out):
    def conv_at(at, above, below):
        def write(r, value):
            out[at + r] = value

        conv_pair([above[:LON], above[LON : 2 * LON], below[:LON], below[LON : 2 * LON]], w_ref, write)

    @pl.when(pl.program_id(0) == 0)
    def _():
        conv_at(0, up, head)

    @pl.when(pl.program_id(0) == 1)
    def _():
        conv_at(2, tail, down)


def conv_cost(pairs):
    return pl.CostEstimate(
        flops=4 * pairs * LON * 12 * CH * CH, bytes_accessed=pairs * LON * CH * 12, transcendentals=0
    )


PRE = pltpu.VMEM((EXT - 4, LON, CH), F32)
PRE_RIM = pltpu.VMEM((4, LON, CH), F32)


def conv_state_inner(field, packed, start, count, before=None):
    args = (field, packed) if before is None else (field, packed, before)
    return pl.pallas_call(
        functools.partial(conv_state_inner_kernel, start),
        grid=(count,),
        in_specs=[WHOLE] * len(args),
        out_specs=WHOLE,
        out_shape=PRE,
        input_output_aliases={} if before is None else {2: 0},
        compiler_params=params(8),
        cost_estimate=conv_cost(count),
        name="conv_state",
    )(*args)


def conv_state_rim(packed, rims):
    return pl.pallas_call(
        conv_state_rim_kernel,
        grid=(2,),
        in_specs=[WHOLE] * 5,
        out_specs=WHOLE,
        out_shape=PRE_RIM,
        compiler_params=params(8),
        cost_estimate=conv_cost(2),
        name="conv_state_rim",
    )(packed, *rims)


def conv_grad_kernel(start, *refs):
    field, w_ref, cot, out = refs[0], refs[1], refs[2], refs[-1]
    p = start + pl.program_id(0)

    def write(r, value):
        out[r] = (cot[2 * p + r].astype(F32) + value).astype(BF)

    conv_pair([field[2 * p + r] for r in range(4)], w_ref, write)


def conv_grad(field, packed, cotangent, start, count, before=None):
    args = [field, packed, cotangent] + ([] if before is None else [before])
    return pl.pallas_call(
        functools.partial(conv_grad_kernel, start),
        grid=(count,),
        in_specs=[WHOLE] * 3 + ([] if before is None else [ANYWHERE]),
        out_specs=pl.BlockSpec((2, LON, CH), lambda i: (start + i, 0, 0)),
        out_shape=jax.ShapeDtypeStruct((ROWS, LON, CH), BF),
        input_output_aliases={} if before is None else {3: 0},
        compiler_params=params(8),
        cost_estimate=conv_cost(count),
        name="conv_grad",
    )(*args)


def conv_grad_rest_kernel(field, w_ref, cot, before, out, held):
    @pl.when(pl.program_id(0) > 0)
    def _():
        def write(r, value):
            out[r] = (cot[r].astype(F32) + value).astype(BF)

        conv_pair([held[0], held[1], field[0], field[1]], w_ref, write)

    held[...] = field[...]


def conv_grad_rest(field, packed, cotangent, start, before):
    done = pl.BlockSpec((2, LON, CH), lambda i: (start + jnp.maximum(i - 1, 0), 0, 0))
    return pl.pallas_call(
        conv_grad_rest_kernel,
        grid=(PAIRS - start + 1,),
        in_specs=[
            pl.BlockSpec((2, LON, CH), lambda i: (start + i, 0, 0)),
            pl.BlockSpec((3, 4 * CH, 2 * CH), lambda i: (0, 0, 0)),
            done,
            ANYWHERE,
        ],
        out_specs=done,
        out_shape=jax.ShapeDtypeStruct((ROWS, LON, CH), BF),
        input_output_aliases={3: 0},
        scratch_shapes=[pltpu.VMEM((2, LON, CH), BF)],
        compiler_params=params(58),
        cost_estimate=conv_cost(PAIRS - start),
        name="conv_grad_rest",
    )(field, packed, cotangent, before)


SC_CHUNK = 512


def onehot(height, index_row):
    place = lax.broadcasted_iota(jnp.int32, (height, index_row.shape[1]), 0)
    return jnp.where(place == index_row, 1.0, 0.0).astype(BF)


def contract0(a, b):
    return lax.dot_general(a, b, (((0,), (0,)), ((), ())), preferred_element_type=F32)


def contract1(a, b):
    return lax.dot_general(a, b, (((1,), (1,)), ((), ())), preferred_element_type=F32)


def slot_row(ref, first):
    return jnp.concatenate([ref[first + k : first + k + 1, :] for k in range(SC_CHUNK // OWNERS)], axis=1)


def live_weight(weight, count):
    slot = lax.broadcasted_iota(jnp.int32, weight.shape, 0)
    return jnp.where(slot < count[...], weight[...], 0.0)


RIM = 3 * LON + 2 * PC


def spread_kernel(
    here,
    near,
    far,
    perm,
    patch,
    target,
    weight,
    count,
    fine_head,
    fine_tail,
    cot_head,
    cot_tail,
    out,
    head,
    tail,
    source,
    live,
    sems,
):
    copies = []
    for to, (buffer, rows) in enumerate(((head, (fine_head, cot_head)), (tail, (fine_tail, cot_tail)))):
        for j, row in enumerate((rows[0].at[0], rows[0].at[1], rows[1].at[0])):
            copies.append(
                pltpu.make_async_copy(row, buffer.at[pl.ds(j * LON, LON)], sems.at[3 * to + j])
            )
    for copy in copies:
        copy.start()
    live[...] = live_weight(weight, count)
    row = jnp.zeros(target.shape, jnp.int32)
    for t in range(16):
        row += jnp.where(target[...] == t, perm[t : t + 1, :], 0)
    source[...] = (row >> 7) * 64 + (row & 63) + jnp.where(((row >> 6) & 1) == (here[1] & 1), 0, SLOTS // 2)
    patches = ROWS * PC
    panel = jnp.concatenate([near[...], far[...]], axis=0)
    total = jnp.zeros((patches, CH), F32)
    for first in range(0, 16, SC_CHUNK // OWNERS):
        picked = contract0(panel, onehot(SLOTS, slot_row(source, first)))
        picked = (picked * slot_row(live, first)).astype(BF)
        total += contract1(onehot(patches, slot_row(patch, first)), picked)
    total = total.astype(BF)
    out[...] = total
    for copy in copies:
        copy.wait()
    head[3 * LON :] = total[: 2 * PC]
    tail[3 * LON :] = total[-2 * PC :]


def spread(here, near, far, perm, patch, target, weight, count, rims):
    rim = pltpu.VMEM((RIM, CH), BF)
    return pl.pallas_call(
        spread_kernel,
        in_specs=[SCALARS] + [WHOLE] * 7 + [ANYWHERE] * 4,
        out_specs=[WHOLE] * 3,
        out_shape=[jax.ShapeDtypeStruct((ROWS * PC, CH), BF), rim, rim],
        scratch_shapes=[
            pltpu.VMEM((16, OWNERS), jnp.int32),
            pltpu.VMEM((16, OWNERS), F32),
            pltpu.SemaphoreType.DMA((6,)),
        ],
        compiler_params=params(12),
        cost_estimate=pl.CostEstimate(flops=4 * 2048 * 2048 * 128, bytes_accessed=MB, transcendentals=0),
        name="spread",
    )(here, near, far, perm, patch, target, weight, count, *rims)


EX_CELLS = 1024
RD_CELLS = 256


def patch_marks(count):
    cells = np.arange(count)[:, None]
    inside = cells // PW == np.arange(count // PW)[None, :]
    marks = [inside, inside & (cells % PW == 0), inside & (cells % PW == PW - 1)]
    return np.concatenate(marks, axis=1).astype(np.float32)


def shift_patch(value, step):
    place = lax.broadcasted_iota(jnp.int32, (PC, 1), 0)
    if step > 0:
        return jnp.where(place == 0, 0.0, pltpu.roll(value, 1, 0))
    return jnp.where(place == PC - 1, 0.0, pltpu.roll(value, PC - 1, 0))


def silu_inner_kernel(pre, cond, w_ref, ex_ref, rd_ref, cot, out, sums):
    q = pl.program_id(0) + 1
    silu_pair(
        q, pre, 2 * q - 2, cond[q - 1], cond[q], lambda cells: (cot[2 * q - 1, cells], cot[2 * q, cells]), w_ref, ex_ref, rd_ref, out, sums
    )


def silu_rim_kernel(pre, cond, w_ref, ex_ref, rd_ref, up, down, head, tail, before, before_sums, out, sums):
    def weights_of(first, second):
        def weights(cells):
            rows = slice(2 * LON + cells.start, 2 * LON + cells.stop)
            return first[rows], second[rows]

        return weights

    @pl.when(pl.program_id(0) == 0)
    def _():
        silu_pair(0, pre, 0, up[3 * LON :], cond[0], weights_of(up, head), w_ref, ex_ref, rd_ref, out, sums)

    @pl.when(pl.program_id(0) == 1)
    def _():
        weights, below = weights_of(tail, down), down[3 * LON :]
        silu_pair(PAIRS, pre, 2, cond[PAIRS - 1], below, weights, w_ref, ex_ref, rd_ref, out, sums)


def silu_pair(q, pre, at, above, below, cot_pair, w_ref, ex_ref, rd_ref, out, sums):
    lhs = jnp.concatenate([above[:PC], above[PC:], below[:PC], below[PC:]], axis=1)
    west, here, east = [dot(lhs, w_ref[k]) for k in range(3)]
    inner = (west + here + east).astype(BF)
    at_first = (shift_patch(west, 1) - west).astype(BF)
    at_last = (shift_patch(east, -1) - east).astype(BF)
    per = EX_CELLS // PW
    part_sum, part_first, part_last = [], [], []
    for lo in range(0, LON, EX_CELLS):
        cells = slice(lo, lo + EX_CELLS)
        cut = slice(lo // PW, lo // PW + per)
        terms = jnp.concatenate([inner[cut], at_first[cut], at_last[cut]], axis=0)
        spread_terms = dot(ex_ref[...], terms)
        weights = cot_pair(cells)
        grads = []
        for r in range(2):
            half = 0.5 * (pre[at + r, cells] + spread_terms[:, r * CH : (r + 1) * CH])
            t = jnp.tanh(half)
            slope = (0.5 + 0.5 * t) * (1.0 + half * (1.0 - t))
            g = (weights[r].astype(F32) * slope).astype(BF)
            out[2 * q + r, cells] = g
            grads.append(g)
        grads = jnp.concatenate(grads, axis=1)
        for first in range(0, EX_CELLS, RD_CELLS):
            reduced = dot(rd_ref[...], grads[first : first + RD_CELLS])
            part_sum.append(reduced[:PW])
            part_first.append(reduced[PW : 2 * PW])
            part_last.append(reduced[2 * PW :])
    whole, firsts, lasts = [jnp.concatenate(p, axis=0) for p in (part_sum, part_first, part_last)]
    from_west = (whole - lasts + shift_patch(lasts, 1)).astype(BF)
    from_east = (whole - firsts + shift_patch(firsts, -1)).astype(BF)
    whole = whole.astype(BF)
    for r in range(2):
        cut = slice(r * CH, (r + 1) * CH)
        sums[2 * q + r] = jnp.concatenate([from_west[:, cut], whole[:, cut], from_east[:, cut]], axis=1)


def silu_grad(pre, cotangent, cond, packed, rims=None, before=None):
    expand = jnp.asarray(patch_marks(EX_CELLS), BF)
    reduce_m = jnp.asarray(patch_marks(RD_CELLS).T, BF)
    inner = rims is None
    args = [pre, cond.reshape(PAIRS, 2 * PC, CH), packed, expand, reduce_m]
    args += [cotangent] if inner else [*rims, *before]
    return pl.pallas_call(
        silu_inner_kernel if inner else silu_rim_kernel,
        grid=(PAIRS - 1 if inner else 2,),
        in_specs=[WHOLE] * len(args),
        out_specs=[WHOLE, WHOLE],
        out_shape=[pltpu.VMEM((EXT, LON, CH), BF), pltpu.VMEM((EXT, PC, 3 * CH), BF)],
        input_output_aliases={} if inner else {9: 0, 10: 1},
        compiler_params=params(8),
        cost_estimate=pl.CostEstimate(flops=10**9, bytes_accessed=8 * ROWS * LON * CH, transcendentals=0),
        name="silu_grad",
    )(*args)


def collect_kernel(here, sums, w_ref, patch, target, weight, count, keep, send, total, slots, shares, picked):
    patches = ROWS * PC
    grad_patch = dot(sums[:patches], w_ref[0])
    grad_patch += dot(sums[PC : PC + patches], w_ref[1])
    grad_patch += dot(sums[2 * PC :], w_ref[2])
    grad_patch = grad_patch.astype(BF)
    owner = lax.broadcasted_iota(jnp.int32, (OWNERS, OWNERS), 0)
    place = ((owner ^ here[1]) & 1) * (OWNERS // 2) + (owner >> 1)
    order = jnp.where(place == lax.broadcasted_iota(jnp.int32, (OWNERS, OWNERS), 1), 1.0, 0.0)
    values = jnp.concatenate(
        [patch[...].astype(F32), target[...].astype(F32), live_weight(weight, count)], axis=0
    )
    values = jnp.dot(values, order, preferred_element_type=F32, precision=lax.Precision.HIGHEST)
    slots[...] = (values[:32] + 0.5).astype(jnp.int32)
    step = lax.broadcasted_iota(jnp.int32, (16, OWNERS), 0)
    for k in range(16):
        hit = step == slots[16 + k : 17 + k, :]
        shares[k] = jnp.where(hit, values[32 + k : 33 + k, :], 0.0)
    for first in range(0, 16, SC_CHUNK // OWNERS):
        got = contract0(grad_patch, onehot(patches, slot_row(slots, first)))
        for k in range(SC_CHUNK // OWNERS):
            picked[first + k] = got[:, k * OWNERS : (k + 1) * OWNERS]
    for t in range(16):
        mine = picked[0] * shares[0, t : t + 1, :]
        for k in range(1, 16):
            mine += picked[k] * shares[k, t : t + 1, :]
        total[pl.ds(t, OWNERS, stride=16), :] = mine.T
    keep[...] = total[: SLOTS // 2]
    send[...] = total[SLOTS // 2 :].astype(BF)


def collect(here, sums, w, patch, target, weight, count):
    return pl.pallas_call(
        collect_kernel,
        in_specs=[SCALARS] + [WHOLE] * 6,
        out_specs=[WHOLE, WHOLE],
        out_shape=[
            jax.ShapeDtypeStruct((SLOTS // 2, CH), F32),
            jax.ShapeDtypeStruct((SLOTS // 2, CH), BF),
        ],
        scratch_shapes=[
            pltpu.VMEM((SLOTS, CH), F32),
            pltpu.VMEM((32, OWNERS), jnp.int32),
            pltpu.VMEM((16, 16, OWNERS), F32),
            pltpu.VMEM((16, CH, OWNERS), F32),
        ],
        compiler_params=params(16),
        cost_estimate=pl.CostEstimate(flops=2 * 2048 * 2048 * 128, bytes_accessed=2 * MB, transcendentals=0),
        name="collect",
    )(here, sums.reshape(EXT * PC, 3 * CH), w, patch, target, weight, count)


def merge_kernel(kept, got, out):
    out[...] = (kept[...] + got[...].astype(F32)).astype(BF)


def merge(kept, got):
    return pl.pallas_call(
        merge_kernel,
        in_specs=[WHOLE] * 2,
        out_specs=WHOLE,
        out_shape=jax.ShapeDtypeStruct(kept.shape, BF),
        compiler_params=params(4),
        name="merge",
    )(kept, got)


def finish_kernel(got, w_ref, out):
    rows = []
    for group in range(4):
        total = got[group * CHIPS].astype(F32)
        for chip in range(1, CHIPS):
            total += got[group * CHIPS + chip].astype(F32)
        rows.append(total.astype(BF))
    out[...] = contract1(jnp.concatenate(rows, axis=0), w_ref[...])


def finish(got, cond_weight):
    return pl.pallas_call(
        finish_kernel,
        in_specs=[WHOLE] * 2,
        out_specs=WHOLE,
        out_shape=jax.ShapeDtypeStruct((64, cond_weight.shape[0]), F32),
        compiler_params=params(4),
        name="finish",
    )(got, cond_weight)


def from_neighbours(head, tail):
    count = lax.axis_size(BOTH)
    up = lax.ppermute(tail, BOTH, [(i, i + 1) for i in range(count - 1)])
    down = lax.ppermute(head, BOTH, [(i + 1, i) for i in range(count - 1)])
    return up, down


def swap(value, axis, bit):
    return lax.ppermute(value, axis, [(i, i ^ bit) for i in range(lax.axis_size(axis))])


def after(value, *earlier):
    return lax.optimization_barrier((value,) + earlier)[0]


def body(
    fine_state,
    cotangent,
    coarse,
    conv_weight,
    cond_weight,
    slot_patch,
    slot_target,
    slot_weight,
    block_count,
    panel_perm,
):
    group = lax.axis_index("group")
    band = lax.axis_index("band")
    here = jnp.stack([group, band]).astype(jnp.int32)
    patch, target, weight = slot_patch[0].T, slot_target[0].T, slot_weight[0].T

    same_core = [[2 * chip + core for chip in range(CHIPS)] for core in range(2)]
    projected, perms, weights, field, cot = lax.optimization_barrier(
        (project(coarse, cond_weight), panel_perm, conv_weight, fine_state, cotangent)
    )
    perm = lax.dynamic_index_in_dim(perms, group, 0, keepdims=False).reshape(-1, 16).T
    near = lax.all_to_all(projected, "band", 0, 0, axis_index_groups=same_core, tiled=True)
    packed, packed_back, w_back = pack(weights)
    cut = (field[:2], field[-2:], cot[:1], cot[-1:])
    near, here, perm, packed, cut = lax.optimization_barrier((near, here, perm, packed, cut))
    far = swap(near, "band", 1)
    cond, head, tail = spread(here, near, far, perm, patch, target, weight, block_count, cut)
    up, down = from_neighbours(head, tail)
    pre = conv_state_inner(after(fine_state, far), packed, 1, 5)
    grad_pre, sums = silu_grad(pre, cotangent, cond, packed)
    grad_pre, sums, up, down = lax.optimization_barrier((grad_pre, sums, up, down))
    rims = (up, down, head, tail)
    pre = conv_state_rim(packed, rims)
    grad_pre, sums = silu_grad(pre, cotangent, cond, packed, rims, (grad_pre, sums))

    keep, send = collect(here, sums, w_back, patch, target, weight, block_count)
    got = swap(send, "band", 1)
    grad_fine = conv_grad(after(grad_pre, keep), packed_back, cotangent, 0, 1)
    got, grad_fine = lax.optimization_barrier((got, grad_fine))
    owned = merge(keep, got)
    count = lax.axis_size(BOTH)
    same_core = [list(range(core, count, 2)) for core in range(2)]
    received = lax.all_to_all(
        owned.reshape(count // 2, 16, CH), BOTH, 0, 0, axis_index_groups=same_core, tiled=True
    )
    grad_fine = conv_grad_rest(after(grad_pre, owned), packed_back, cotangent, 1, grad_fine)
    received, grad_fine = lax.optimization_barrier((received, grad_fine))
    grad_owned = finish(received, cond_weight)
    return grad_fine, grad_owned


def solution(mesh):
    rows3 = P(BOTH, None, None)
    rows2 = P(BOTH, None)
    return jax.shard_map(
        body,
        mesh=mesh,
        in_specs=(rows3, rows3, rows2, P(), P(), rows3, rows3, rows3, rows2, P()),
        out_specs=(rows3, rows2),
        check_vma=False,
    )
```

```python
import functools

import jax
import jax.numpy as jnp
import numpy as np
from jax import lax
from jax.experimental import pallas as pl
from jax.experimental.pallas import tpu as pltpu
from jax.sharding import PartitionSpec as P

PW = 16
ROWS = 12
LON = 2048
PC = LON // PW
CH = 128
PAIRS = ROWS // 2
EXT = ROWS + 2
SLOTS = 2048
OWNERS = 128
BF = jnp.bfloat16
F32 = jnp.float32
MB = 1 << 20
BOTH = ("group", "band")


def dot(a, b):
    return jnp.dot(a, b, preferred_element_type=F32)


WHOLE = pl.BlockSpec(memory_space=pltpu.VMEM)


def params(mib):
    return pltpu.CompilerParams(vmem_limit_bytes=mib * MB)


ANYWHERE = pl.BlockSpec(memory_space=pl.ANY)
SCALARS = pl.BlockSpec(memory_space=pltpu.SMEM)


CHIPS = 16


def project_kernel(coarse, w_ref, out):
    rows = coarse.shape[0]
    value = dot(coarse[...], w_ref[...]).astype(BF)
    for chip in range(CHIPS):
        out[chip * rows : (chip + 1) * rows] = value


def project(coarse, cond_weight):
    return pl.pallas_call(
        project_kernel,
        in_specs=[WHOLE] * 2,
        out_specs=WHOLE,
        out_shape=jax.ShapeDtypeStruct((CHIPS * coarse.shape[0], CH), BF),
        compiler_params=params(4),
        name="project",
    )(coarse, cond_weight)


def pack_kernel(w_ref, packed, back, w_back):
    zero = jnp.zeros((CH, CH), BF)
    left, right = slice(0, CH), slice(CH, 2 * CH)
    for kx in range(3):
        flipped = []
        for ky in range(3):
            turned = w_ref[2 - ky, 2 - kx].astype(F32).T.astype(BF)
            w_back[ky, kx * CH : (kx + 1) * CH, :] = turned
            flipped.append(turned)
        for r in range(4):
            rows = slice(r * CH, (r + 1) * CH)
            packed[kx, rows, left] = w_ref[r, kx] if r < 3 else zero
            packed[kx, rows, right] = w_ref[r - 1, kx] if r >= 1 else zero
            back[kx, rows, left] = flipped[r] if r < 3 else zero
            back[kx, rows, right] = flipped[r - 1] if r >= 1 else zero


def pack(conv_weight):
    both = jax.ShapeDtypeStruct((3, 4 * CH, 2 * CH), BF)
    return pl.pallas_call(
        pack_kernel,
        in_specs=[WHOLE],
        out_specs=[WHOLE] * 3,
        out_shape=[both, both, jax.ShapeDtypeStruct((3, 3 * CH, CH), BF)],
        compiler_params=params(4),
        name="pack",
    )(conv_weight)


def conv_pair(rows, w_ref, write):
    lhs = jnp.concatenate(rows, axis=1)
    left = dot(lhs, w_ref[0])
    right = dot(lhs, w_ref[2])
    place = lax.broadcasted_iota(jnp.int32, (LON, 1), 0)
    total = dot(lhs, w_ref[1])
    total += jnp.where(place == 0, 0.0, pltpu.roll(left, 1, 0))
    total += jnp.where(place == LON - 1, 0.0, pltpu.roll(right, LON - 1, 0))
    write(0, total[:, :CH])
    write(1, total[:, CH:])


def conv_state_inner_kernel(start, *refs):
    field, w_ref, out = refs[0], refs[1], refs[-1]
    q = start + pl.program_id(0)

    def write(r, value):
        out[2 * q - 2 + r] = value

    conv_pair([field[2 * q - 2 + r] for r in range(4)], w_ref, write)


def conv_state_rim_kernel(w_ref, up, down, head, tail, out):
    def conv_at(at, above, below):
        def write(r, value):
            out[at + r] = value

        conv_pair([above[:LON], above[LON : 2 * LON], below[:LON], below[LON : 2 * LON]], w_ref, write)

    @pl.when(pl.program_id(0) == 0)
    def _():
        conv_at(0, up, head)

    @pl.when(pl.program_id(0) == 1)
    def _():
        conv_at(2, tail, down)


def conv_cost(pairs):
    return pl.CostEstimate(
        flops=4 * pairs * LON * 12 * CH * CH, bytes_accessed=pairs * LON * CH * 12, transcendentals=0
    )


PRE = pltpu.VMEM((EXT - 4, LON, CH), F32)
PRE_RIM = pltpu.VMEM((4, LON, CH), F32)


def conv_state_inner(field, packed, start, count, before=None):
    args = (field, packed) if before is None else (field, packed, before)
    return pl.pallas_call(
        functools.partial(conv_state_inner_kernel, start),
        grid=(count,),
        in_specs=[WHOLE] * len(args),
        out_specs=WHOLE,
        out_shape=PRE,
        input_output_aliases={} if before is None else {2: 0},
        compiler_params=params(8),
        cost_estimate=conv_cost(count),
        name="conv_state",
    )(*args)


def conv_state_rim(packed, rims):
    return pl.pallas_call(
        conv_state_rim_kernel,
        grid=(2,),
        in_specs=[WHOLE] * 5,
        out_specs=WHOLE,
        out_shape=PRE_RIM,
        compiler_params=params(8),
        cost_estimate=conv_cost(2),
        name="conv_state_rim",
    )(packed, *rims)


def conv_grad_kernel(start, *refs):
    field, w_ref, cot, out = refs[0], refs[1], refs[2], refs[-1]
    p = start + pl.program_id(0)

    def write(r, value):
        out[r] = (cot[2 * p + r].astype(F32) + value).astype(BF)

    conv_pair([field[2 * p + r] for r in range(4)], w_ref, write)


def conv_grad(field, packed, cotangent, start, count, before=None):
    args = [field, packed, cotangent] + ([] if before is None else [before])
    return pl.pallas_call(
        functools.partial(conv_grad_kernel, start),
        grid=(count,),
        in_specs=[WHOLE] * 3 + ([] if before is None else [ANYWHERE]),
        out_specs=pl.BlockSpec((2, LON, CH), lambda i: (start + i, 0, 0)),
        out_shape=jax.ShapeDtypeStruct((ROWS, LON, CH), BF),
        input_output_aliases={} if before is None else {3: 0},
        compiler_params=params(8),
        cost_estimate=conv_cost(count),
        name="conv_grad",
    )(*args)


def conv_grad_rest_kernel(field, w_ref, cot, before, out, held):
    @pl.when(pl.program_id(0) > 0)
    def _():
        def write(r, value):
            out[r] = (cot[r].astype(F32) + value).astype(BF)

        conv_pair([held[0], held[1], field[0], field[1]], w_ref, write)

    held[...] = field[...]


def conv_grad_rest(field, packed, cotangent, start, before):
    done = pl.BlockSpec((2, LON, CH), lambda i: (start + jnp.maximum(i - 1, 0), 0, 0))
    return pl.pallas_call(
        conv_grad_rest_kernel,
        grid=(PAIRS - start + 1,),
        in_specs=[
            pl.BlockSpec((2, LON, CH), lambda i: (start + i, 0, 0)),
            pl.BlockSpec((3, 4 * CH, 2 * CH), lambda i: (0, 0, 0)),
            done,
            ANYWHERE,
        ],
        out_specs=done,
        out_shape=jax.ShapeDtypeStruct((ROWS, LON, CH), BF),
        input_output_aliases={3: 0},
        scratch_shapes=[pltpu.VMEM((2, LON, CH), BF)],
        compiler_params=params(58),
        cost_estimate=conv_cost(PAIRS - start),
        name="conv_grad_rest",
    )(field, packed, cotangent, before)


SC_CHUNK = 512


def onehot(height, index_row):
    place = lax.broadcasted_iota(jnp.int32, (height, index_row.shape[1]), 0)
    return jnp.where(place == index_row, 1.0, 0.0).astype(BF)


def contract0(a, b):
    return lax.dot_general(a, b, (((0,), (0,)), ((), ())), preferred_element_type=F32)


def contract1(a, b):
    return lax.dot_general(a, b, (((1,), (1,)), ((), ())), preferred_element_type=F32)


def slot_row(ref, first):
    return jnp.concatenate([ref[first + k : first + k + 1, :] for k in range(SC_CHUNK // OWNERS)], axis=1)


def live_weight(weight, count):
    slot = lax.broadcasted_iota(jnp.int32, weight.shape, 0)
    return jnp.where(slot < count[...], weight[...], 0.0)


RIM = 3 * LON + 2 * PC


def spread_kernel(
    here,
    near,
    far,
    perm,
    patch,
    target,
    weight,
    count,
    fine_head,
    fine_tail,
    cot_head,
    cot_tail,
    out,
    head,
    tail,
    source,
    live,
    sems,
):
    copies = []
    for to, (buffer, rows) in enumerate(((head, (fine_head, cot_head)), (tail, (fine_tail, cot_tail)))):
        for j, row in enumerate((rows[0].at[0], rows[0].at[1], rows[1].at[0])):
            copies.append(
                pltpu.make_async_copy(row, buffer.at[pl.ds(j * LON, LON)], sems.at[3 * to + j])
            )
    for copy in copies:
        copy.start()
    live[...] = live_weight(weight, count)
    row = jnp.zeros(target.shape, jnp.int32)
    for t in range(16):
        row += jnp.where(target[...] == t, perm[t : t + 1, :], 0)
    source[...] = (row >> 7) * 64 + (row & 63) + jnp.where(((row >> 6) & 1) == (here[1] & 1), 0, SLOTS // 2)
    patches = ROWS * PC
    panel = jnp.concatenate([near[...], far[...]], axis=0)
    total = jnp.zeros((patches, CH), F32)
    for first in range(0, 16, SC_CHUNK // OWNERS):
        picked = contract0(panel, onehot(SLOTS, slot_row(source, first)))
        picked = (picked * slot_row(live, first)).astype(BF)
        total += contract1(onehot(patches, slot_row(patch, first)), picked)
    total = total.astype(BF)
    out[...] = total
    for copy in copies:
        copy.wait()
    head[3 * LON :] = total[: 2 * PC]
    tail[3 * LON :] = total[-2 * PC :]


def spread(here, near, far, perm, patch, target, weight, count, rims):
    rim = pltpu.VMEM((RIM, CH), BF)
    return pl.pallas_call(
        spread_kernel,
        in_specs=[SCALARS] + [WHOLE] * 7 + [ANYWHERE] * 4,
        out_specs=[WHOLE] * 3,
        out_shape=[jax.ShapeDtypeStruct((ROWS * PC, CH), BF), rim, rim],
        scratch_shapes=[
            pltpu.VMEM((16, OWNERS), jnp.int32),
            pltpu.VMEM((16, OWNERS), F32),
            pltpu.SemaphoreType.DMA((6,)),
        ],
        compiler_params=params(12),
        cost_estimate=pl.CostEstimate(flops=4 * 2048 * 2048 * 128, bytes_accessed=MB, transcendentals=0),
        name="spread",
    )(here, near, far, perm, patch, target, weight, count, *rims)


EX_CELLS = 1024
RD_CELLS = 256


def patch_marks(count):
    cells = np.arange(count)[:, None]
    inside = cells // PW == np.arange(count // PW)[None, :]
    marks = [inside, inside & (cells % PW == 0), inside & (cells % PW == PW - 1)]
    return np.concatenate(marks, axis=1).astype(np.float32)


def shift_patch(value, step):
    place = lax.broadcasted_iota(jnp.int32, (PC, 1), 0)
    if step > 0:
        return jnp.where(place == 0, 0.0, pltpu.roll(value, 1, 0))
    return jnp.where(place == PC - 1, 0.0, pltpu.roll(value, PC - 1, 0))


def silu_inner_kernel(pre, cond, w_ref, ex_ref, rd_ref, cot, out, sums):
    q = pl.program_id(0) + 1
    silu_pair(
        q, pre, 2 * q - 2, cond[q - 1], cond[q], lambda cells: (cot[2 * q - 1, cells], cot[2 * q, cells]), w_ref, ex_ref, rd_ref, out, sums
    )


def silu_rim_kernel(pre, cond, w_ref, ex_ref, rd_ref, up, down, head, tail, before, before_sums, out, sums):
    def weights_of(first, second):
        def weights(cells):
            rows = slice(2 * LON + cells.start, 2 * LON + cells.stop)
            return first[rows], second[rows]

        return weights

    @pl.when(pl.program_id(0) == 0)
    def _():
        silu_pair(0, pre, 0, up[3 * LON :], cond[0], weights_of(up, head), w_ref, ex_ref, rd_ref, out, sums)

    @pl.when(pl.program_id(0) == 1)
    def _():
        weights, below = weights_of(tail, down), down[3 * LON :]
        silu_pair(PAIRS, pre, 2, cond[PAIRS - 1], below, weights, w_ref, ex_ref, rd_ref, out, sums)


def silu_pair(q, pre, at, above, below, cot_pair, w_ref, ex_ref, rd_ref, out, sums):
    lhs = jnp.concatenate([above[:PC], above[PC:], below[:PC], below[PC:]], axis=1)
    west, here, east = [dot(lhs, w_ref[k]) for k in range(3)]
    inner = (west + here + east).astype(BF)
    at_first = (shift_patch(west, 1) - west).astype(BF)
    at_last = (shift_patch(east, -1) - east).astype(BF)
    per = EX_CELLS // PW
    part_sum, part_first, part_last = [], [], []
    for lo in range(0, LON, EX_CELLS):
        cells = slice(lo, lo + EX_CELLS)
        cut = slice(lo // PW, lo // PW + per)
        terms = jnp.concatenate([inner[cut], at_first[cut], at_last[cut]], axis=0)
        spread_terms = dot(ex_ref[...], terms)
        weights = cot_pair(cells)
        grads = []
        for r in range(2):
            half = 0.5 * (pre[at + r, cells] + spread_terms[:, r * CH : (r + 1) * CH])
            t = jnp.tanh(half)
            slope = (0.5 + 0.5 * t) * (1.0 + half * (1.0 - t))
            g = (weights[r].astype(F32) * slope).astype(BF)
            out[2 * q + r, cells] = g
            grads.append(g)
        grads = jnp.concatenate(grads, axis=1)
        for first in range(0, EX_CELLS, RD_CELLS):
            reduced = dot(rd_ref[...], grads[first : first + RD_CELLS])
            part_sum.append(reduced[:PW])
            part_first.append(reduced[PW : 2 * PW])
            part_last.append(reduced[2 * PW :])
    whole, firsts, lasts = [jnp.concatenate(p, axis=0) for p in (part_sum, part_first, part_last)]
    from_west = (whole - lasts + shift_patch(lasts, 1)).astype(BF)
    from_east = (whole - firsts + shift_patch(firsts, -1)).astype(BF)
    whole = whole.astype(BF)
    for r in range(2):
        cut = slice(r * CH, (r + 1) * CH)
        sums[2 * q + r] = jnp.concatenate([from_west[:, cut], whole[:, cut], from_east[:, cut]], axis=1)


def silu_grad(pre, cotangent, cond, packed, rims=None, before=None):
    expand = jnp.asarray(patch_marks(EX_CELLS), BF)
    reduce_m = jnp.asarray(patch_marks(RD_CELLS).T, BF)
    inner = rims is None
    args = [pre, cond.reshape(PAIRS, 2 * PC, CH), packed, expand, reduce_m]
    args += [cotangent] if inner else [*rims, *before]
    return pl.pallas_call(
        silu_inner_kernel if inner else silu_rim_kernel,
        grid=(PAIRS - 1 if inner else 2,),
        in_specs=[WHOLE] * len(args),
        out_specs=[WHOLE, WHOLE],
        out_shape=[pltpu.VMEM((EXT, LON, CH), BF), pltpu.VMEM((EXT, PC, 3 * CH), BF)],
        input_output_aliases={} if inner else {9: 0, 10: 1},
        compiler_params=params(8),
        cost_estimate=pl.CostEstimate(flops=10**9, bytes_accessed=8 * ROWS * LON * CH, transcendentals=0),
        name="silu_grad",
    )(*args)


def collect_kernel(here, sums, w_ref, patch, target, weight, count, keep, send, total, slots, shares, picked):
    patches = ROWS * PC
    grad_patch = dot(sums[:patches], w_ref[0])
    grad_patch += dot(sums[PC : PC + patches], w_ref[1])
    grad_patch += dot(sums[2 * PC :], w_ref[2])
    grad_patch = grad_patch.astype(BF)
    owner = lax.broadcasted_iota(jnp.int32, (OWNERS, OWNERS), 0)
    place = ((owner ^ here[1]) & 1) * (OWNERS // 2) + (owner >> 1)
    order = jnp.where(place == lax.broadcasted_iota(jnp.int32, (OWNERS, OWNERS), 1), 1.0, 0.0)
    values = jnp.concatenate(
        [patch[...].astype(F32), target[...].astype(F32), live_weight(weight, count)], axis=0
    )
    values = jnp.dot(values, order, preferred_element_type=F32, precision=lax.Precision.HIGHEST)
    slots[...] = (values[:32] + 0.5).astype(jnp.int32)
    step = lax.broadcasted_iota(jnp.int32, (16, OWNERS), 0)
    for k in range(16):
        hit = step == slots[16 + k : 17 + k, :]
        shares[k] = jnp.where(hit, values[32 + k : 33 + k, :], 0.0)
    for first in range(0, 16, SC_CHUNK // OWNERS):
        got = contract0(grad_patch, onehot(patches, slot_row(slots, first)))
        for k in range(SC_CHUNK // OWNERS):
            picked[first + k] = got[:, k * OWNERS : (k + 1) * OWNERS]
    for t in range(16):
        mine = picked[0] * shares[0, t : t + 1, :]
        for k in range(1, 16):
            mine += picked[k] * shares[k, t : t + 1, :]
        total[pl.ds(t, OWNERS, stride=16), :] = mine.T
    keep[...] = total[: SLOTS // 2]
    send[...] = total[SLOTS // 2 :].astype(BF)


def collect(here, sums, w, patch, target, weight, count):
    return pl.pallas_call(
        collect_kernel,
        in_specs=[SCALARS] + [WHOLE] * 6,
        out_specs=[WHOLE, WHOLE],
        out_shape=[
            jax.ShapeDtypeStruct((SLOTS // 2, CH), F32),
            jax.ShapeDtypeStruct((SLOTS // 2, CH), BF),
        ],
        scratch_shapes=[
            pltpu.VMEM((SLOTS, CH), F32),
            pltpu.VMEM((32, OWNERS), jnp.int32),
            pltpu.VMEM((16, 16, OWNERS), F32),
            pltpu.VMEM((16, CH, OWNERS), F32),
        ],
        compiler_params=params(16),
        cost_estimate=pl.CostEstimate(flops=2 * 2048 * 2048 * 128, bytes_accessed=2 * MB, transcendentals=0),
        name="collect",
    )(here, sums.reshape(EXT * PC, 3 * CH), w, patch, target, weight, count)


def merge_kernel(kept, got, out):
    out[...] = (kept[...] + got[...].astype(F32)).astype(BF)


def merge(kept, got):
    return pl.pallas_call(
        merge_kernel,
        in_specs=[WHOLE] * 2,
        out_specs=WHOLE,
        out_shape=jax.ShapeDtypeStruct(kept.shape, BF),
        compiler_params=params(4),
        name="merge",
    )(kept, got)


def finish_kernel(got, w_ref, out):
    rows = []
    for group in range(4):
        total = got[group * CHIPS].astype(F32)
        for chip in range(1, CHIPS):
            total += got[group * CHIPS + chip].astype(F32)
        rows.append(total.astype(BF))
    out[...] = contract1(jnp.concatenate(rows, axis=0), w_ref[...])


def finish(got, cond_weight):
    return pl.pallas_call(
        finish_kernel,
        in_specs=[WHOLE] * 2,
        out_specs=WHOLE,
        out_shape=jax.ShapeDtypeStruct((64, cond_weight.shape[0]), F32),
        compiler_params=params(4),
        name="finish",
    )(got, cond_weight)


def from_neighbours(head, tail):
    count = lax.axis_size(BOTH)
    up = lax.ppermute(tail, BOTH, [(i, i + 1) for i in range(count - 1)])
    down = lax.ppermute(head, BOTH, [(i + 1, i) for i in range(count - 1)])
    return up, down


def swap(value, axis, bit):
    return lax.ppermute(value, axis, [(i, i ^ bit) for i in range(lax.axis_size(axis))])


def after(value, *earlier):
    return lax.optimization_barrier((value,) + earlier)[0]


def body(
    fine_state,
    cotangent,
    coarse,
    conv_weight,
    cond_weight,
    slot_patch,
    slot_target,
    slot_weight,
    block_count,
    panel_perm,
):
    group = lax.axis_index("group")
    band = lax.axis_index("band")
    here = jnp.stack([group, band]).astype(jnp.int32)
    patch, target, weight = slot_patch[0].T, slot_target[0].T, slot_weight[0].T

    same_core = [[2 * chip + core for chip in range(CHIPS)] for core in range(2)]
    projected, perms, field, cot = lax.optimization_barrier(
        (project(coarse, cond_weight), panel_perm, fine_state, cotangent)
    )
    perm = lax.dynamic_index_in_dim(perms, group, 0, keepdims=False).reshape(-1, 16).T
    near = lax.all_to_all(projected, "band", 0, 0, axis_index_groups=same_core, tiled=True)
    cut = (field[:2], field[-2:], cot[:1], cot[-1:])
    near, here, perm, cut, weights = lax.optimization_barrier((near, here, perm, cut, conv_weight))
    far = swap(near, "band", 1)
    packed, packed_back, w_back = pack(weights)
    far, packed = lax.optimization_barrier((far, packed))
    cond, head, tail = spread(here, near, far, perm, patch, target, weight, block_count, cut)
    up, down = from_neighbours(head, tail)
    pre = conv_state_inner(after(fine_state, far), packed, 1, 5)
    grad_pre, sums = silu_grad(pre, cotangent, cond, packed)
    grad_pre, sums, up, down = lax.optimization_barrier((grad_pre, sums, up, down))
    rims = (up, down, head, tail)
    pre = conv_state_rim(packed, rims)
    grad_pre, sums = silu_grad(pre, cotangent, cond, packed, rims, (grad_pre, sums))

    keep, send = collect(here, sums, w_back, patch, target, weight, block_count)
    got = swap(send, "band", 1)
    grad_fine = conv_grad(after(grad_pre, keep), packed_back, cotangent, 0, 1)
    got, grad_fine = lax.optimization_barrier((got, grad_fine))
    owned = merge(keep, got)
    count = lax.axis_size(BOTH)
    same_core = [list(range(core, count, 2)) for core in range(2)]
    received = lax.all_to_all(
        owned.reshape(count // 2, 16, CH), BOTH, 0, 0, axis_index_groups=same_core, tiled=True
    )
    grad_fine = conv_grad_rest(after(grad_pre, owned), packed_back, cotangent, 1, grad_fine)
    received, grad_fine = lax.optimization_barrier((received, grad_fine))
    grad_owned = finish(received, cond_weight)
    return grad_fine, grad_owned


def solution(mesh):
    rows3 = P(BOTH, None, None)
    rows2 = P(BOTH, None)
    return jax.shard_map(
        body,
        mesh=mesh,
        in_specs=(rows3, rows3, rows2, P(), P(), rows3, rows3, rows3, rows2, P()),
        out_specs=(rows3, rows2),
        check_vma=False,
    )
```

```python
import functools

import jax
import jax.numpy as jnp
import numpy as np
from jax import lax
from jax.experimental import pallas as pl
from jax.experimental.pallas import tpu as pltpu
from jax.sharding import PartitionSpec as P

PW = 16
ROWS = 12
LON = 2048
PC = LON // PW
CH = 128
PAIRS = ROWS // 2
EXT = ROWS + 2
SLOTS = 2048
OWNERS = 128
BF = jnp.bfloat16
F32 = jnp.float32
MB = 1 << 20
BOTH = ("group", "band")


def dot(a, b):
    return jnp.dot(a, b, preferred_element_type=F32)


WHOLE = pl.BlockSpec(memory_space=pltpu.VMEM)


def params(mib):
    return pltpu.CompilerParams(vmem_limit_bytes=mib * MB)


ANYWHERE = pl.BlockSpec(memory_space=pl.ANY)
SCALARS = pl.BlockSpec(memory_space=pltpu.SMEM)


CHIPS = 16


def project_kernel(coarse, w_ref, out):
    rows = coarse.shape[0]
    value = dot(coarse[...], w_ref[...]).astype(BF)
    for chip in range(CHIPS):
        out[chip * rows : (chip + 1) * rows] = value


def project(coarse, cond_weight):
    return pl.pallas_call(
        project_kernel,
        in_specs=[WHOLE] * 2,
        out_specs=WHOLE,
        out_shape=jax.ShapeDtypeStruct((CHIPS * coarse.shape[0], CH), BF),
        compiler_params=params(4),
        name="project",
    )(coarse, cond_weight)


def pack_kernel(w_ref, packed, back, w_back):
    zero = jnp.zeros((CH, CH), BF)
    left, right = slice(0, CH), slice(CH, 2 * CH)
    for kx in range(3):
        flipped = []
        for ky in range(3):
            turned = w_ref[2 - ky, 2 - kx].astype(F32).T.astype(BF)
            w_back[ky, kx * CH : (kx + 1) * CH, :] = turned
            flipped.append(turned)
        for r in range(4):
            rows = slice(r * CH, (r + 1) * CH)
            packed[kx, rows, left] = w_ref[r, kx] if r < 3 else zero
            packed[kx, rows, right] = w_ref[r - 1, kx] if r >= 1 else zero
            back[kx, rows, left] = flipped[r] if r < 3 else zero
            back[kx, rows, right] = flipped[r - 1] if r >= 1 else zero


def pack(conv_weight):
    both = jax.ShapeDtypeStruct((3, 4 * CH, 2 * CH), BF)
    return pl.pallas_call(
        pack_kernel,
        in_specs=[WHOLE],
        out_specs=[WHOLE] * 3,
        out_shape=[both, both, jax.ShapeDtypeStruct((3, 3 * CH, CH), BF)],
        compiler_params=params(4),
        name="pack",
    )(conv_weight)


def conv_pair(rows, w_ref, write):
    lhs = jnp.concatenate(rows, axis=1)
    left = dot(lhs, w_ref[0])
    right = dot(lhs, w_ref[2])
    place = lax.broadcasted_iota(jnp.int32, (LON, 1), 0)
    total = dot(lhs, w_ref[1])
    total += jnp.where(place == 0, 0.0, pltpu.roll(left, 1, 0))
    total += jnp.where(place == LON - 1, 0.0, pltpu.roll(right, LON - 1, 0))
    write(0, total[:, :CH])
    write(1, total[:, CH:])


def conv_state_inner_kernel(start, *refs):
    field, w_ref, out = refs[0], refs[1], refs[-1]
    q = start + pl.program_id(0)

    def write(r, value):
        out[2 * q - 2 + r] = value

    conv_pair([field[2 * q - 2 + r] for r in range(4)], w_ref, write)


def conv_state_rim_kernel(w_ref, up, down, head, tail, out):
    def conv_at(at, above, below):
        def write(r, value):
            out[at + r] = value

        conv_pair([above[:LON], above[LON : 2 * LON], below[:LON], below[LON : 2 * LON]], w_ref, write)

    @pl.when(pl.program_id(0) == 0)
    def _():
        conv_at(0, up, head)

    @pl.when(pl.program_id(0) == 1)
    def _():
        conv_at(2, tail, down)


def conv_cost(pairs):
    return pl.CostEstimate(
        flops=4 * pairs * LON * 12 * CH * CH, bytes_accessed=pairs * LON * CH * 12, transcendentals=0
    )


PRE = pltpu.VMEM((EXT - 4, LON, CH), F32)
PRE_RIM = pltpu.VMEM((4, LON, CH), F32)


def conv_state_inner(field, packed, start, count, before=None):
    args = (field, packed) if before is None else (field, packed, before)
    return pl.pallas_call(
        functools.partial(conv_state_inner_kernel, start),
        grid=(count,),
        in_specs=[WHOLE] * len(args),
        out_specs=WHOLE,
        out_shape=PRE,
        input_output_aliases={} if before is None else {2: 0},
        compiler_params=params(8),
        cost_estimate=conv_cost(count),
        name="conv_state",
    )(*args)


def conv_state_rim(packed, rims):
    return pl.pallas_call(
        conv_state_rim_kernel,
        grid=(2,),
        in_specs=[WHOLE] * 5,
        out_specs=WHOLE,
        out_shape=PRE_RIM,
        compiler_params=params(8),
        cost_estimate=conv_cost(2),
        name="conv_state_rim",
    )(packed, *rims)


def conv_grad_kernel(start, *refs):
    field, w_ref, cot, out = refs[0], refs[1], refs[2], refs[-1]
    p = start + pl.program_id(0)

    def write(r, value):
        out[r] = (cot[2 * p + r].astype(F32) + value).astype(BF)

    conv_pair([field[2 * p + r] for r in range(4)], w_ref, write)


def conv_grad(field, packed, cotangent, start, count, before=None):
    args = [field, packed, cotangent] + ([] if before is None else [before])
    return pl.pallas_call(
        functools.partial(conv_grad_kernel, start),
        grid=(count,),
        in_specs=[WHOLE] * 3 + ([] if before is None else [ANYWHERE]),
        out_specs=pl.BlockSpec((2, LON, CH), lambda i: (start + i, 0, 0)),
        out_shape=jax.ShapeDtypeStruct((ROWS, LON, CH), BF),
        input_output_aliases={} if before is None else {3: 0},
        compiler_params=params(8),
        cost_estimate=conv_cost(count),
        name="conv_grad",
    )(*args)


def conv_grad_rest_kernel(field, w_ref, cot, before, out, held):
    @pl.when(pl.program_id(0) > 0)
    def _():
        def write(r, value):
            out[r] = (cot[r].astype(F32) + value).astype(BF)

        conv_pair([held[0], held[1], field[0], field[1]], w_ref, write)

    held[...] = field[...]


def conv_grad_rest(field, packed, cotangent, start, before):
    done = pl.BlockSpec((2, LON, CH), lambda i: (start + jnp.maximum(i - 1, 0), 0, 0))
    return pl.pallas_call(
        conv_grad_rest_kernel,
        grid=(PAIRS - start + 1,),
        in_specs=[
            pl.BlockSpec((2, LON, CH), lambda i: (start + i, 0, 0)),
            pl.BlockSpec((3, 4 * CH, 2 * CH), lambda i: (0, 0, 0)),
            done,
            ANYWHERE,
        ],
        out_specs=done,
        out_shape=jax.ShapeDtypeStruct((ROWS, LON, CH), BF),
        input_output_aliases={3: 0},
        scratch_shapes=[pltpu.VMEM((2, LON, CH), BF)],
        compiler_params=params(58),
        cost_estimate=conv_cost(PAIRS - start),
        name="conv_grad_rest",
    )(field, packed, cotangent, before)


SC_CHUNK = 512


def onehot(height, index_row):
    place = lax.broadcasted_iota(jnp.int32, (height, index_row.shape[1]), 0)
    return jnp.where(place == index_row, 1.0, 0.0).astype(BF)


def contract0(a, b):
    return lax.dot_general(a, b, (((0,), (0,)), ((), ())), preferred_element_type=F32)


def contract1(a, b):
    return lax.dot_general(a, b, (((1,), (1,)), ((), ())), preferred_element_type=F32)


def slot_row(ref, first):
    return jnp.concatenate([ref[first + k : first + k + 1, :] for k in range(SC_CHUNK // OWNERS)], axis=1)


def live_weight(weight, count):
    slot = lax.broadcasted_iota(jnp.int32, weight.shape, 0)
    return jnp.where(slot < count[...], weight[...], 0.0)


RIM = 3 * LON + 2 * PC


def spread_kernel(
    here,
    near,
    far,
    perm,
    patch,
    target,
    weight,
    count,
    fine_head,
    fine_tail,
    cot_head,
    cot_tail,
    out,
    head,
    tail,
    source,
    live,
    sems,
):
    copies = []
    for to, (buffer, rows) in enumerate(((head, (fine_head, cot_head)), (tail, (fine_tail, cot_tail)))):
        for j, row in enumerate((rows[0].at[0], rows[0].at[1], rows[1].at[0])):
            copies.append(
                pltpu.make_async_copy(row, buffer.at[pl.ds(j * LON, LON)], sems.at[3 * to + j])
            )
    for copy in copies:
        copy.start()
    live[...] = live_weight(weight, count)
    row = jnp.zeros(target.shape, jnp.int32)
    for t in range(16):
        row += jnp.where(target[...] == t, perm[t : t + 1, :], 0)
    source[...] = (row >> 7) * 64 + (row & 63) + jnp.where(((row >> 6) & 1) == (here[1] & 1), 0, SLOTS // 2)
    patches = ROWS * PC
    panel = jnp.concatenate([near[...], far[...]], axis=0)
    total = jnp.zeros((patches, CH), F32)
    for first in range(0, 16, SC_CHUNK // OWNERS):
        picked = contract0(panel, onehot(SLOTS, slot_row(source, first)))
        picked = (picked * slot_row(live, first)).astype(BF)
        total += contract1(onehot(patches, slot_row(patch, first)), picked)
    total = total.astype(BF)
    out[...] = total
    for copy in copies:
        copy.wait()
    head[3 * LON :] = total[: 2 * PC]
    tail[3 * LON :] = total[-2 * PC :]


def spread(here, near, far, perm, patch, target, weight, count, rims):
    rim = pltpu.VMEM((RIM, CH), BF)
    return pl.pallas_call(
        spread_kernel,
        in_specs=[SCALARS] + [WHOLE] * 7 + [ANYWHERE] * 4,
        out_specs=[WHOLE] * 3,
        out_shape=[jax.ShapeDtypeStruct((ROWS * PC, CH), BF), rim, rim],
        scratch_shapes=[
            pltpu.VMEM((16, OWNERS), jnp.int32),
            pltpu.VMEM((16, OWNERS), F32),
            pltpu.SemaphoreType.DMA((6,)),
        ],
        compiler_params=params(12),
        cost_estimate=pl.CostEstimate(flops=4 * 2048 * 2048 * 128, bytes_accessed=MB, transcendentals=0),
        name="spread",
    )(here, near, far, perm, patch, target, weight, count, *rims)


EX_CELLS = 1024
RD_CELLS = 256


def patch_marks(count):
    cells = np.arange(count)[:, None]
    inside = cells // PW == np.arange(count // PW)[None, :]
    marks = [inside, inside & (cells % PW == 0), inside & (cells % PW == PW - 1)]
    return np.concatenate(marks, axis=1).astype(np.float32)


def shift_patch(value, step):
    place = lax.broadcasted_iota(jnp.int32, (PC, 1), 0)
    if step > 0:
        return jnp.where(place == 0, 0.0, pltpu.roll(value, 1, 0))
    return jnp.where(place == PC - 1, 0.0, pltpu.roll(value, PC - 1, 0))


def silu_inner_kernel(pre, cond, w_ref, ex_ref, rd_ref, cot, out, sums):
    q = pl.program_id(0) + 1
    silu_pair(
        q, pre, 2 * q - 2, cond[q - 1], cond[q], lambda cells: (cot[2 * q - 1, cells], cot[2 * q, cells]), w_ref, ex_ref, rd_ref, out, sums
    )


def silu_rim_kernel(pre, cond, w_ref, ex_ref, rd_ref, up, down, head, tail, before, before_sums, out, sums):
    def weights_of(first, second):
        def weights(cells):
            rows = slice(2 * LON + cells.start, 2 * LON + cells.stop)
            return first[rows], second[rows]

        return weights

    @pl.when(pl.program_id(0) == 0)
    def _():
        silu_pair(0, pre, 0, up[3 * LON :], cond[0], weights_of(up, head), w_ref, ex_ref, rd_ref, out, sums)

    @pl.when(pl.program_id(0) == 1)
    def _():
        weights, below = weights_of(tail, down), down[3 * LON :]
        silu_pair(PAIRS, pre, 2, cond[PAIRS - 1], below, weights, w_ref, ex_ref, rd_ref, out, sums)


def silu_pair(q, pre, at, above, below, cot_pair, w_ref, ex_ref, rd_ref, out, sums):
    lhs = jnp.concatenate([above[:PC], above[PC:], below[:PC], below[PC:]], axis=1)
    west, here, east = [dot(lhs, w_ref[k]) for k in range(3)]
    inner = (west + here + east).astype(BF)
    at_first = (shift_patch(west, 1) - west).astype(BF)
    at_last = (shift_patch(east, -1) - east).astype(BF)
    per = EX_CELLS // PW
    part_sum, part_first, part_last = [], [], []
    for lo in range(0, LON, EX_CELLS):
        cells = slice(lo, lo + EX_CELLS)
        cut = slice(lo // PW, lo // PW + per)
        terms = jnp.concatenate([inner[cut], at_first[cut], at_last[cut]], axis=0)
        spread_terms = dot(ex_ref[...], terms)
        weights = cot_pair(cells)
        grads = []
        for r in range(2):
            half = 0.5 * (pre[at + r, cells] + spread_terms[:, r * CH : (r + 1) * CH])
            t = jnp.tanh(half)
            slope = (0.5 + 0.5 * t) * (1.0 + half * (1.0 - t))
            g = (weights[r].astype(F32) * slope).astype(BF)
            out[2 * q + r, cells] = g
            grads.append(g)
        grads = jnp.concatenate(grads, axis=1)
        for first in range(0, EX_CELLS, RD_CELLS):
            reduced = dot(rd_ref[...], grads[first : first + RD_CELLS])
            part_sum.append(reduced[:PW])
            part_first.append(reduced[PW : 2 * PW])
            part_last.append(reduced[2 * PW :])
    whole, firsts, lasts = [jnp.concatenate(p, axis=0) for p in (part_sum, part_first, part_last)]
    from_west = (whole - lasts + shift_patch(lasts, 1)).astype(BF)
    from_east = (whole - firsts + shift_patch(firsts, -1)).astype(BF)
    whole = whole.astype(BF)
    for r in range(2):
        cut = slice(r * CH, (r + 1) * CH)
        sums[2 * q + r] = jnp.concatenate([from_west[:, cut], whole[:, cut], from_east[:, cut]], axis=1)


def silu_grad(pre, cotangent, cond, packed, rims=None, before=None):
    expand = jnp.asarray(patch_marks(EX_CELLS), BF)
    reduce_m = jnp.asarray(patch_marks(RD_CELLS).T, BF)
    inner = rims is None
    args = [pre, cond.reshape(PAIRS, 2 * PC, CH), packed, expand, reduce_m]
    args += [cotangent] if inner else [*rims, *before]
    return pl.pallas_call(
        silu_inner_kernel if inner else silu_rim_kernel,
        grid=(PAIRS - 1 if inner else 2,),
        in_specs=[WHOLE] * len(args),
        out_specs=[WHOLE, WHOLE],
        out_shape=[pltpu.VMEM((EXT, LON, CH), BF), pltpu.VMEM((EXT, PC, 3 * CH), BF)],
        input_output_aliases={} if inner else {9: 0, 10: 1},
        compiler_params=params(8),
        cost_estimate=pl.CostEstimate(flops=10**9, bytes_accessed=8 * ROWS * LON * CH, transcendentals=0),
        name="silu_grad",
    )(*args)


def collect_kernel(here, sums, w_ref, patch, target, weight, count, keep, send, total, slots, shares, picked):
    patches = ROWS * PC
    grad_patch = dot(sums[:patches], w_ref[0])
    grad_patch += dot(sums[PC : PC + patches], w_ref[1])
    grad_patch += dot(sums[2 * PC :], w_ref[2])
    grad_patch = grad_patch.astype(BF)
    owner = lax.broadcasted_iota(jnp.int32, (OWNERS, OWNERS), 0)
    place = ((owner ^ here[1]) & 1) * (OWNERS // 2) + (owner >> 1)
    order = jnp.where(place == lax.broadcasted_iota(jnp.int32, (OWNERS, OWNERS), 1), 1.0, 0.0)
    values = jnp.concatenate(
        [patch[...].astype(F32), target[...].astype(F32), live_weight(weight, count)], axis=0
    )
    values = jnp.dot(values, order, preferred_element_type=F32, precision=lax.Precision.HIGHEST)
    slots[...] = (values[:32] + 0.5).astype(jnp.int32)
    step = lax.broadcasted_iota(jnp.int32, (16, OWNERS), 0)
    for k in range(16):
        hit = step == slots[16 + k : 17 + k, :]
        shares[k] = jnp.where(hit, values[32 + k : 33 + k, :], 0.0)
    for first in range(0, 16, SC_CHUNK // OWNERS):
        got = contract0(grad_patch, onehot(patches, slot_row(slots, first)))
        for k in range(SC_CHUNK // OWNERS):
            picked[first + k] = got[:, k * OWNERS : (k + 1) * OWNERS]
    for t in range(16):
        mine = picked[0] * shares[0, t : t + 1, :]
        for k in range(1, 16):
            mine += picked[k] * shares[k, t : t + 1, :]
        total[pl.ds(t, OWNERS, stride=16), :] = mine.T
    keep[...] = total[: SLOTS // 2]
    send[...] = total[SLOTS // 2 :].astype(BF)


def collect(here, sums, w, patch, target, weight, count):
    return pl.pallas_call(
        collect_kernel,
        in_specs=[SCALARS] + [WHOLE] * 6,
        out_specs=[WHOLE, WHOLE],
        out_shape=[
            jax.ShapeDtypeStruct((SLOTS // 2, CH), F32),
            jax.ShapeDtypeStruct((SLOTS // 2, CH), BF),
        ],
        scratch_shapes=[
            pltpu.VMEM((SLOTS, CH), F32),
            pltpu.VMEM((32, OWNERS), jnp.int32),
            pltpu.VMEM((16, 16, OWNERS), F32),
            pltpu.VMEM((16, CH, OWNERS), F32),
        ],
        compiler_params=params(16),
        cost_estimate=pl.CostEstimate(flops=2 * 2048 * 2048 * 128, bytes_accessed=2 * MB, transcendentals=0),
        name="collect",
    )(here, sums.reshape(EXT * PC, 3 * CH), w, patch, target, weight, count)


def merge_kernel(kept, got, out):
    out[...] = (kept[...] + got[...].astype(F32)).astype(BF)


def merge(kept, got):
    return pl.pallas_call(
        merge_kernel,
        in_specs=[WHOLE] * 2,
        out_specs=WHOLE,
        out_shape=jax.ShapeDtypeStruct(kept.shape, BF),
        compiler_params=params(4),
        name="merge",
    )(kept, got)


def finish_kernel(got, w_ref, out):
    rows = []
    for group in range(4):
        total = got[group * CHIPS].astype(F32)
        for chip in range(1, CHIPS):
            total += got[group * CHIPS + chip].astype(F32)
        rows.append(total.astype(BF))
    out[...] = contract1(jnp.concatenate(rows, axis=0), w_ref[...])


def finish(got, cond_weight):
    return pl.pallas_call(
        finish_kernel,
        in_specs=[WHOLE] * 2,
        out_specs=WHOLE,
        out_shape=jax.ShapeDtypeStruct((64, cond_weight.shape[0]), F32),
        compiler_params=params(4),
        name="finish",
    )(got, cond_weight)


def from_neighbours(head, tail):
    count = lax.axis_size(BOTH)
    up = lax.ppermute(tail, BOTH, [(i, i + 1) for i in range(count - 1)])
    down = lax.ppermute(head, BOTH, [(i + 1, i) for i in range(count - 1)])
    return up, down


def swap(value, axis, bit):
    return lax.ppermute(value, axis, [(i, i ^ bit) for i in range(lax.axis_size(axis))])


def after(value, *earlier):
    return lax.optimization_barrier((value,) + earlier)[0]


def body(
    fine_state,
    cotangent,
    coarse,
    conv_weight,
    cond_weight,
    slot_patch,
    slot_target,
    slot_weight,
    block_count,
    panel_perm,
):
    group = lax.axis_index("group")
    band = lax.axis_index("band")
    here = jnp.stack([group, band]).astype(jnp.int32)
    patch, target, weight = slot_patch[0].T, slot_target[0].T, slot_weight[0].T

    same_core = [[2 * chip + core for chip in range(CHIPS)] for core in range(2)]
    projected, perms, field, cot = lax.optimization_barrier(
        (project(coarse, cond_weight), panel_perm, fine_state, cotangent)
    )
    perm = lax.dynamic_index_in_dim(perms, group, 0, keepdims=False).reshape(-1, 16).T
    near = lax.all_to_all(projected, "band", 0, 0, axis_index_groups=same_core, tiled=True)
    cut = (field[:2], field[-2:], cot[:1], cot[-1:])
    near, here, perm, cut, weights = lax.optimization_barrier((near, here, perm, cut, conv_weight))
    far = swap(near, "band", 1)
    packed, packed_back, w_back = pack(weights)
    far, packed = lax.optimization_barrier((far, packed))
    cond, head, tail = spread(here, near, far, perm, patch, target, weight, block_count, cut)
    up, down = from_neighbours(head, tail)
    pre = conv_state_inner(after(fine_state, near), packed, 1, 5)
    grad_pre, sums = silu_grad(pre, cotangent, cond, packed)
    grad_pre, sums, up, down = lax.optimization_barrier((grad_pre, sums, up, down))
    rims = (up, down, head, tail)
    pre = conv_state_rim(packed, rims)
    grad_pre, sums = silu_grad(pre, cotangent, cond, packed, rims, (grad_pre, sums))

    keep, send = collect(here, sums, w_back, patch, target, weight, block_count)
    got = swap(send, "band", 1)
    grad_fine = conv_grad(after(grad_pre, keep), packed_back, cotangent, 0, 2)
    got, grad_fine = lax.optimization_barrier((got, grad_fine))
    owned = merge(keep, got)
    count = lax.axis_size(BOTH)
    same_core = [list(range(core, count, 2)) for core in range(2)]
    received = lax.all_to_all(
        owned.reshape(count // 2, 16, CH), BOTH, 0, 0, axis_index_groups=same_core, tiled=True
    )
    grad_fine = conv_grad_rest(after(grad_pre, owned), packed_back, cotangent, 2, grad_fine)
    received, grad_fine = lax.optimization_barrier((received, grad_fine))
    grad_owned = finish(received, cond_weight)
    return grad_fine, grad_owned


def solution(mesh):
    rows3 = P(BOTH, None, None)
    rows2 = P(BOTH, None)
    return jax.shard_map(
        body,
        mesh=mesh,
        in_specs=(rows3, rows3, rows2, P(), P(), rows3, rows3, rows3, rows2, P()),
        out_specs=(rows3, rows2),
        check_vma=False,
    )
```
